32 devices in a mesh: dp: 8 (over y, x, core), tensor: 4 (over z).
Axes of the slice: x: 2, y: 2, z: 4, core: 2. Of those that a mesh axis runs over, the one named last changes fastest.
Arguments:
- inputs: bfloat16 [16384, 512], P(('dp', 'tensor')), may hold values from -6 to 6
- memory: bfloat16 [4096, 512], P(('dp', 'tensor')), may hold values from -6 to 6
- prefix: int32 [16], P('dp'), may hold values from 102 to 512
- self_query: bfloat16 [512, 512], P('dp', 'tensor'), may hold values from -0.25 to 0.25
- self_query_bias: bfloat16 [512], P('tensor'), may hold values from -3 to 3
- self_key: bfloat16 [512, 512], P('dp', 'tensor'), may hold values from -0.25 to 0.25
- self_value: bfloat16 [512, 512], P('dp', 'tensor'), may hold values from -0.25 to 0.25
- self_value_bias: bfloat16 [512], P('tensor'), may hold values from -1.1953125 to 1.1953125
- self_out: bfloat16 [512, 512], P('tensor', 'dp'), may hold values from -1.5 to 1.5
- self_out_bias: bfloat16 [512], replicated, may hold values from -1.796875 to 1.796875
- self_norm_gain: bfloat16 [512], replicated, may hold values from 0.5 to 1.5
- self_norm_bias: bfloat16 [512], replicated, may hold values from -1.796875 to 1.796875
- cross_query: bfloat16 [512, 512], P('dp', 'tensor'), may hold values from -0.25 to 0.25
- cross_query_bias: bfloat16 [512], P('tensor'), may hold values from -3 to 3
- cross_key: bfloat16 [512, 512], P('dp', 'tensor'), may hold values from -0.25 to 0.25
- cross_value: bfloat16 [512, 512], P('dp', 'tensor'), may hold values from -0.25 to 0.25
- cross_value_bias: bfloat16 [512], P('tensor'), may hold values from -1.1953125 to 1.1953125
- cross_out: bfloat16 [512, 512], P('tensor', 'dp'), may hold values from -1.5 to 1.5
- cross_out_bias: bfloat16 [512], replicated, may hold values from -1.796875 to 1.796875
- cross_norm_gain: bfloat16 [512], replicated, may hold values from 0.5 to 1.5
- cross_norm_bias: bfloat16 [512], replicated, may hold values from -1.796875 to 1.796875
- feed_in: bfloat16 [512, 2048], P('dp', 'tensor'), may hold values from -0.25 to 0.25
- feed_in_bias: bfloat16 [2048], P('tensor'), may hold values from -3 to 3
- feed_out: bfloat16 [2048, 512], P('tensor', 'dp'), may hold values from -0.125 to 0.125
- feed_out_bias: bfloat16 [512], replicated, may hold values from -1.796875 to 1.796875
- feed_norm_gain: bfloat16 [512], replicated, may hold values from 0.5 to 1.5
- feed_norm_bias: bfloat16 [512], replicated, may hold values from -1.796875 to 1.796875
- cotangent: bfloat16 [16384, 512], P(('dp', 'tensor')), may hold values from -12 to 12
Outputs:
- outputs: bfloat16 [16384, 512], P(('dp', 'tensor'))
- grad_inputs: float32 [16384, 512], P(('dp', 'tensor'))
- grad_memory: float32 [4096, 512], P(('dp', 'tensor'))
- grad_self_query: float32 [512, 512], P('dp', 'tensor')
- grad_self_query_bias: float32 [512], P('tensor')
- grad_self_key: float32 [512, 512], P('dp', 'tensor')
- grad_self_value: float32 [512, 512], P('dp', 'tensor')
- grad_self_value_bias: float32 [512], P('tensor')
- grad_self_out: float32 [512, 512], P('tensor', 'dp')
- grad_self_out_bias: float32 [512], replicated
- grad_self_norm_gain: float32 [512], replicated
- grad_self_norm_bias: float32 [512], replicated
- grad_cross_query: float32 [512, 512], P('dp', 'tensor')
- grad_cross_query_bias: float32 [512], P('tensor')
- grad_cross_key: float32 [512, 512], P('dp', 'tensor')
- grad_cross_value: float32 [512, 512], P('dp', 'tensor')
- grad_cross_value_bias: float32 [512], P('tensor')
- grad_cross_out: float32 [512, 512], P('tensor', 'dp')
- grad_cross_out_bias: float32 [512], replicated
- grad_cross_norm_gain: float32 [512], replicated
- grad_cross_norm_bias: float32 [512], replicated
- grad_feed_in: float32 [512, 2048], P('dp', 'tensor')
- grad_feed_in_bias: float32 [2048], P('tensor')
- grad_feed_out: float32 [2048, 512], P('tensor', 'dp')
- grad_feed_out_bias: float32 [512], replicated
- grad_feed_norm_gain: float32 [512], replicated
- grad_feed_norm_bias: float32 [512], replicated
The draws below stay inside these ranges and needn't reach their ends.
All inputs are finite; a program needn't handle non-finite values.
Results may differ from the reference program's by a relative error of at most 0.025.
Values may be sent and summed in bfloat16 or wider, within the bound.
No kernel may reach another device: no remote copies, remote signals or barrier semaphores. Data moves between devices by JAX's collectives and lax.ppermute only.
A program may use at most 128 MiB of HBM per device.

```python
import jax
import jax.numpy as jnp
from jax import lax

D = 512
FF = 2048
HEADS = 8
HD = 64
LEN = 1024
MEM = 256
SEQS = 16
TOKENS = 16384
MEM_ROWS = 4096


def draw_cotangent(key, part):
    row_pos = jnp.arange(TOKENS, dtype=jnp.float32)[:, None] / max(TOKENS - 1, 1)
    row_scale = 1.0 + 2.0 * row_pos
    base_draw = jax.random.normal(key, (TOKENS, D), jnp.float32)
    return jnp.clip(base_draw * row_scale, -12.0, 12.0).astype(jnp.bfloat16)


def with_ends(array, rng, least, top_value):
    longest = array.shape.index(max(array.shape))
    spots = []
    for shift in (0, 1):
        where = [jax.random.randint(jax.random.fold_in(rng, axis), (), 0, length) for axis, length in enumerate(array.shape)]
        where[longest] = (where[longest] + shift) % array.shape[longest]
        spots.append(tuple(where))
    return array.at[spots[0]].set(least).at[spots[1]].set(top_value)


def levels(key, extent, pieces, least, top_value):
    def one(position, parts):
        heights = jax.random.uniform(jax.random.fold_in(jax.random.fold_in(key, 6), position), (parts,), jnp.float32, least / len(pieces), top_value / len(pieces))
        return jnp.repeat(jnp.exp(heights), extent[position] // parts).reshape((-1,) + (1,) * (len(extent) - position - 1))

    gain = one(*pieces[0])
    for cut in pieces[1:]:
        gain = gain * one(*cut)
    return gain


def gaussian(stream_key, shape, spread, bound, cuts=(), held_as=jnp.bfloat16):
    values = spread * jax.random.normal(stream_key, shape, jnp.float32)
    if cuts:
        values = values * levels(stream_key, shape, cuts, -0.22, 0.18)
    return jnp.clip(values, -bound, bound).astype(held_as)


def setup_inputs(seed: int = 0) -> dict:
    key_of = jax.random.split(jax.random.key(seed), 29)
    inputs = gaussian(key_of[0], (TOKENS, D), 1.0, 6.0, ((0, 32),))
    memory = gaussian(key_of[1], (MEM_ROWS, D), 1.0, 6.0, ((0, 32),))
    prefix = with_ends(jax.random.randint(key_of[2], (SEQS,), LEN // 10, LEN // 2 + 1), jax.random.fold_in(key_of[2], 1), LEN // 10, (LEN // 2 + 1) - 1).astype(jnp.int32)
    self_query = gaussian(key_of[3], (D, D), D ** -0.5, 0.25, ((0, 8), (1, 4)))
    self_query_bias = gaussian(key_of[4], (D,), 0.5, 3.0, ((0, 4),))
    self_key = gaussian(key_of[5], (D, D), D ** -0.5, 0.25, ((0, 8), (1, 4)))
    self_value = gaussian(key_of[6], (D, D), D ** -0.5, 0.25, ((0, 8), (1, 4)))
    self_value_bias = gaussian(key_of[7], (D,), 0.2, 1.1953125, ((0, 4),))
    self_out = gaussian(key_of[8], (D, D), (D // 32) ** -0.5, 1.5, ((0, 4), (1, 8)))
    self_out_bias = gaussian(key_of[9], (D,), 0.3, 1.796875)
    self_norm_gain = jnp.clip(1.0 + 0.1 * jax.random.normal(key_of[10], (D,), jnp.float32), 0.5, 1.5).astype(jnp.bfloat16)
    self_norm_bias = gaussian(key_of[11], (D,), 0.3, 1.796875)
    cross_query = gaussian(key_of[12], (D, D), D ** -0.5, 0.25, ((0, 8), (1, 4)))
    cross_query_bias = gaussian(key_of[13], (D,), 0.5, 3.0, ((0, 4),))
    cross_key = gaussian(key_of[14], (D, D), D ** -0.5, 0.25, ((0, 8), (1, 4)))
    cross_value = gaussian(key_of[15], (D, D), D ** -0.5, 0.25, ((0, 8), (1, 4)))
    cross_value_bias = gaussian(key_of[16], (D,), 0.2, 1.1953125, ((0, 4),))
    cross_out = gaussian(key_of[17], (D, D), (D // 32) ** -0.5, 1.5, ((0, 4), (1, 8)))
    cross_out_bias = gaussian(key_of[18], (D,), 0.3, 1.796875)
    cross_norm_gain = jnp.clip(1.0 + 0.1 * jax.random.normal(key_of[19], (D,), jnp.float32), 0.5, 1.5).astype(jnp.bfloat16)
    cross_norm_bias = gaussian(key_of[20], (D,), 0.3, 1.796875)
    feed_in = gaussian(key_of[21], (D, FF), D ** -0.5, 0.25, ((0, 8), (1, 4)))
    feed_in_bias = gaussian(key_of[22], (FF,), 0.5, 3.0, ((0, 4),))
    feed_out = gaussian(key_of[23], (FF, D), FF ** -0.5, 0.125, ((0, 4), (1, 8)))
    feed_out_bias = gaussian(key_of[24], (D,), 0.3, 1.796875)
    feed_norm_gain = jnp.clip(1.0 + 0.1 * jax.random.normal(key_of[25], (D,), jnp.float32), 0.5, 1.5).astype(jnp.bfloat16)
    feed_norm_bias = gaussian(key_of[26], (D,), 0.3, 1.796875)
    cotangent = draw_cotangent(jax.random.fold_in(key_of[28], 71), 0)
    return {"inputs": inputs, "memory": memory, "prefix": prefix, "self_query": self_query, "self_query_bias": self_query_bias, "self_key": self_key, "self_value": self_value, "self_value_bias": self_value_bias, "self_out": self_out, "self_out_bias": self_out_bias, "self_norm_gain": self_norm_gain, "self_norm_bias": self_norm_bias, "cross_query": cross_query, "cross_query_bias": cross_query_bias, "cross_key": cross_key, "cross_value": cross_value, "cross_value_bias": cross_value_bias, "cross_out": cross_out, "cross_out_bias": cross_out_bias, "cross_norm_gain": cross_norm_gain, "cross_norm_bias": cross_norm_bias, "feed_in": feed_in, "feed_in_bias": feed_in_bias, "feed_out": feed_out, "feed_out_bias": feed_out_bias, "feed_norm_gain": feed_norm_gain, "feed_norm_bias": feed_norm_bias, "cotangent": cotangent}


@jax.custom_vjp
def low(v):
    return lax.optimization_barrier(v.astype(jnp.bfloat16)).astype(jnp.float32)

@jax.custom_vjp
def low_back(v):
    return v

def low_keep(v):
    return (low(v), None)

def low_pass(kept, grad):
    return (grad,)

def back_keep(v):
    return (v, None)

def back_low(kept, grad):
    return (low(grad),)
low.defvjp(low_keep, low_pass)
low_back.defvjp(back_keep, back_low)

def matmul_high(left_side, right_side):
    return jnp.dot(left_side, right_side, precision=lax.Precision.HIGHEST)

def rounded(values):
    return low(low_back(values))

def layer_norm(summed, norm_gain, norm_shift):
    row_mean = lax.optimization_barrier(jnp.mean(summed, axis=-1, keepdims=True))
    centred = summed - row_mean
    variance = lax.optimization_barrier(jnp.mean(centred * centred, axis=-1, keepdims=True))
    return centred * lax.rsqrt(variance + 1e-05) * norm_gain + norm_shift

def attend(query_heads, key_heads, value_heads, allowed):
    scores = jnp.einsum('qhd,khd->hqk', query_heads, key_heads, precision=lax.Precision.HIGHEST) * HD ** (-0.5)
    scores = jnp.where(allowed[None], low_back(scores), -1e+30)
    row_peak = lax.optimization_barrier(jnp.max(scores, axis=-1, keepdims=True))
    exponent = jnp.exp(scores - row_peak)
    weights_soft = exponent / lax.optimization_barrier(jnp.sum(exponent, axis=-1, keepdims=True))
    return jnp.einsum('hqk,khd->qhd', low(weights_soft), value_heads, precision=lax.Precision.HIGHEST)

def self_attention(queries, keys, values, prefix):
    positions = jnp.arange(LEN, dtype=jnp.int32)
    causal = positions[None, :] <= positions[:, None]
    head_shape = (SEQS, LEN, HEADS, HD)

    def one_sequence(seq_items):
        query_seq, key_seq, value_seq, prefix_len = seq_items
        allowed = causal | (positions[None, :] < prefix_len)
        return attend(query_seq, key_seq, value_seq, allowed)
    mapped = lax.map(jax.checkpoint(one_sequence), (queries.reshape(head_shape), keys.reshape(head_shape), values.reshape(head_shape), prefix))
    return mapped.reshape(TOKENS, D)

def cross_attention(queries, keys, values):
    allowed = jnp.ones((LEN, MEM), dtype=jnp.bool_)

    def one_sequence(seq_items):
        query_seq, key_seq, value_seq = seq_items
        return attend(query_seq, key_seq, value_seq, allowed)
    mapped = lax.map(jax.checkpoint(one_sequence), (queries.reshape(SEQS, LEN, HEADS, HD), keys.reshape(SEQS, MEM, HEADS, HD), values.reshape(SEQS, MEM, HEADS, HD)))
    return mapped.reshape(TOKENS, D)

def forward(inputs, memory, weights, prefix):
    self_query, self_query_bias, self_key, self_value, self_value_bias, self_out, self_out_bias, self_norm_gain, self_norm_bias, cross_query, cross_query_bias, cross_key, cross_value, cross_value_bias, cross_out, cross_out_bias, cross_norm_gain, cross_norm_bias, feed_in, feed_in_bias, feed_out, feed_out_bias, feed_norm_gain, feed_norm_bias = weights
    query_one = rounded(matmul_high(inputs, self_query) + self_query_bias)
    key_one = rounded(matmul_high(inputs, self_key))
    value_one = rounded(matmul_high(inputs, self_value) + self_value_bias)
    context_one = rounded(self_attention(query_one, key_one, value_one, prefix))
    branch_one = low_back(matmul_high(context_one, self_out) + self_out_bias)
    first_out = layer_norm(inputs + branch_one, self_norm_gain, self_norm_bias)
    first_low = low(first_out)
    query_two = rounded(matmul_high(first_low, cross_query) + cross_query_bias)
    key_two = rounded(matmul_high(memory, cross_key))
    value_two = rounded(matmul_high(memory, cross_value) + cross_value_bias)
    context_two = rounded(cross_attention(query_two, key_two, value_two))
    branch_two = low_back(matmul_high(context_two, cross_out) + cross_out_bias)
    second_out = layer_norm(first_out + branch_two, cross_norm_gain, cross_norm_bias)
    second_low = low(second_out)
    hidden = low_back(matmul_high(second_low, feed_in) + feed_in_bias)
    active = low(jax.nn.silu(hidden))
    branch_three = low_back(matmul_high(active, feed_out) + feed_out_bias)
    return layer_norm(second_out + branch_three, feed_norm_gain, feed_norm_bias)

def reference(inputs, memory, prefix, self_query, self_query_bias, self_key, self_value, self_value_bias, self_out, self_out_bias, self_norm_gain, self_norm_bias, cross_query, cross_query_bias, cross_key, cross_value, cross_value_bias, cross_out, cross_out_bias, cross_norm_gain, cross_norm_bias, feed_in, feed_in_bias, feed_out, feed_out_bias, feed_norm_gain, feed_norm_bias, cotangent):
    weights = (self_query, self_query_bias, self_key, self_value, self_value_bias, self_out, self_out_bias, self_norm_gain, self_norm_bias, cross_query, cross_query_bias, cross_key, cross_value, cross_value_bias, cross_out, cross_out_bias, cross_norm_gain, cross_norm_bias, feed_in, feed_in_bias, feed_out, feed_out_bias, feed_norm_gain, feed_norm_bias)
    weights_float = tuple((weight.astype(jnp.float32) for weight in weights))

    def run_layer(tokens_float, memory_float, params_float):
        return forward(tokens_float, memory_float, params_float, prefix)
    result, pullback = jax.vjp(run_layer, inputs.astype(jnp.float32), memory.astype(jnp.float32), weights_float)
    grad_inputs, grad_memory, grad_weights = pullback(cotangent.astype(jnp.float32))
    grad_self_query, grad_self_query_bias, grad_self_key, grad_self_value, grad_self_value_bias, grad_self_out, grad_self_out_bias, grad_self_norm_gain, grad_self_norm_bias, grad_cross_query, grad_cross_query_bias, grad_cross_key, grad_cross_value, grad_cross_value_bias, grad_cross_out, grad_cross_out_bias, grad_cross_norm_gain, grad_cross_norm_bias, grad_feed_in, grad_feed_in_bias, grad_feed_out, grad_feed_out_bias, grad_feed_norm_gain, grad_feed_norm_bias = grad_weights
    return (result.astype(jnp.bfloat16), grad_inputs, grad_memory, grad_self_query, grad_self_query_bias, grad_self_key, grad_self_value, grad_self_value_bias, grad_self_out, grad_self_out_bias, grad_self_norm_gain, grad_self_norm_bias, grad_cross_query, grad_cross_query_bias, grad_cross_key, grad_cross_value, grad_cross_value_bias, grad_cross_out, grad_cross_out_bias, grad_cross_norm_gain, grad_cross_norm_bias, grad_feed_in, grad_feed_in_bias, grad_feed_out, grad_feed_out_bias, grad_feed_norm_gain, grad_feed_norm_bias)
```

```python
import functools

import jax
import jax.numpy as jnp
from jax import lax
from jax.experimental import pallas as pl
from jax.experimental.pallas import tpu as pltpu
from jax.sharding import PartitionSpec as P

HD = 64
LEN = 1024
MEM = 256
PAIR = 128
BLOCK = 256

EPSILON = 1e-05
MASKED = -1e30
SCALE = float(HD) ** (-0.5)

F32 = jnp.float32
BF16 = jnp.bfloat16
NN = (((1,), (0,)), ((), ()))
NT = (((1,), (1,)), ((), ()))
TN = (((0,), (0,)), ((), ()))
SMEM = pl.BlockSpec(memory_space=pltpu.SMEM)
ANY = pl.BlockSpec(memory_space=pl.ANY)
VMEM = pl.BlockSpec(memory_space=pltpu.VMEM)


def mm(left_side, right_side, dims):
    return lax.dot_general(left_side, right_side, dims, preferred_element_type=F32)


def shaped(shape, dtype):
    return jax.ShapeDtypeStruct(shape, dtype)


def cost(macs, moved):
    return pl.CostEstimate(flops=2 * macs, bytes_accessed=moved, transcendentals=0)


def limit(mebibytes):
    return pltpu.CompilerParams(vmem_limit_bytes=mebibytes << 20)


def swap(array, dp_mask, tensor_mask):
    nd, nt = lax.axis_size("dp"), lax.axis_size("tensor")
    pairs = [
        (d * nt + t, (d ^ dp_mask) * nt + (t ^ tensor_mask)) for d in range(nd) for t in range(nt)
    ]
    return lax.ppermute(array, ("dp", "tensor"), pairs)


def hand_over(array, parity, step):
    nd, nt = lax.axis_size("dp"), lax.axis_size("tensor")
    pairs = [(d * nt + t, d * nt + t + step) for d in range(nd) for t in range(parity, nt, 2)]
    return lax.ppermute(array, ("dp", "tensor"), pairs)


def tree_sum(terms):
    while len(terms) > 1:
        terms = [terms[i] + terms[i + 1] for i in range(0, len(terms), 2)]
    return terms[0]


def along_line(shard):
    return jnp.stack([shard] + [swap(shard, 0, k) for k in range(1, lax.axis_size("tensor"))])


def over_planes(line):
    planes = lax.axis_size("dp") // 2
    plane = jnp.stack([line] + [swap(line, 2 * j, 0) for j in range(1, planes)])
    return plane, swap(plane, 1, 0)


def gather_group(shard):
    return over_planes(along_line(shard))


def scatter_group(keep, send):
    nd, nt = lax.axis_size("dp"), lax.axis_size("tensor")
    chip = (keep.astype(F32) + swap(send, 1, 0).astype(F32)).astype(BF16)
    line = tree_sum(
        [chip[0].astype(F32)] + [swap(chip[j], 2 * j, 0).astype(F32) for j in range(1, nd // 2)]
    ).astype(BF16)
    return tree_sum([line[0].astype(F32)] + [swap(line[s], 0, s).astype(F32) for s in range(1, nt)])


def sum_everywhere(vector):
    nd, nt = lax.axis_size("dp"), lax.axis_size("tensor")
    vector = vector + swap(vector, 1, 0)
    vector = tree_sum([vector] + [swap(vector, 2 * j, 0) for j in range(1, nd // 2)])
    return tree_sum([vector] + [swap(vector, 0, s) for s in range(1, nt)])


def slot_blocks(info, planes, nt):
    for j in range(planes):
        for c in range(2):
            d = jnp.bitwise_xor(info[2], 2 * j + c)
            for s in range(nt):
                yield j, c, s, d, jnp.bitwise_xor(info[3], s)


def assemble_kernel(info, plane, sibling, whole):
    planes, nt, n, r, w = plane.shape
    for j, c, s, d, t in slot_blocks(info, planes, nt):
        rows = pl.ds(pl.multiple_of(d * r, r), r)
        columns = pl.ds(pl.multiple_of(t * w, w), w)
        for i in range(n):
            whole[i, rows, columns] = (plane, sibling)[c][j, s, i]


def aligned(r, w):
    return w % PAIR == 0 and r % 16 == 0


def assemble(info, plane, sibling):
    planes, nt, n, r, w = plane.shape
    nd = 2 * planes
    if aligned(r, w):
        return pl.pallas_call(
            assemble_kernel,
            out_shape=shaped((n, nd * r, nt * w), BF16),
            in_specs=[SMEM, VMEM, VMEM],
            out_specs=VMEM,
            compiler_params=limit(32),
            cost_estimate=cost(0, 4 * plane.size * 2),
        )(info, plane, sibling)
    full = jnp.stack([plane, sibling], axis=1).reshape(nd, nt, n, r, w)
    full = jnp.take(full, jnp.bitwise_xor(jnp.arange(nd), info[2]), axis=0)
    full = jnp.take(full, jnp.bitwise_xor(jnp.arange(nt), info[3]), axis=1)
    return full.transpose(2, 0, 3, 1, 4).reshape(n, nd * r, nt * w)


def disperse_kernel(info, whole, keep, send):
    planes, nt, n, r, w = keep.shape
    for j, c, s, d, t in slot_blocks(info, planes, nt):
        rows = pl.ds(pl.multiple_of(d * r, r), r)
        columns = pl.ds(pl.multiple_of(t * w, w), w)
        for i in range(n):
            (keep, send)[c][j, s, i] = whole[i, rows, columns]


def disperse(info, whole):
    nd, nt = lax.axis_size("dp"), lax.axis_size("tensor")
    n, r, w = whole.shape[0], whole.shape[1] // nd, whole.shape[2] // nt
    half = (nd // 2, nt, n, r, w)
    if aligned(r, w):
        return pl.pallas_call(
            disperse_kernel,
            out_shape=(shaped(half, BF16), shaped(half, BF16)),
            in_specs=[SMEM, VMEM],
            out_specs=(VMEM, VMEM),
            compiler_params=limit(32),
            cost_estimate=cost(0, 2 * whole.size * 2),
        )(info, whole)
    full = whole.reshape(n, nd, r, nt, w).transpose(1, 3, 0, 2, 4)
    full = jnp.take(full, jnp.bitwise_xor(jnp.arange(nd), info[2]), axis=0)
    full = jnp.take(full, jnp.bitwise_xor(jnp.arange(nt), info[3]), axis=1)
    full = full.reshape(nd // 2, 2, nt, n, r, w)
    return full[:, 0], full[:, 1]


def norm_forward(summed):
    row_mean = jnp.mean(summed, axis=-1, keepdims=True)
    centred = summed - row_mean
    variance = jnp.mean(centred * centred, axis=-1, keepdims=True)
    inverse = lax.rsqrt(variance + EPSILON)
    return centred * inverse, inverse


def norm_backward(grad_out, normed, inverse, norm_gain):
    grad_normed = grad_out * norm_gain
    return inverse * (
        grad_normed
        - jnp.mean(grad_normed, axis=-1, keepdims=True)
        - normed * jnp.mean(grad_normed * normed, axis=-1, keepdims=True)
    )


def column_sum(values):
    return jnp.sum(values.astype(F32), axis=0, keepdims=True)


def head_lanes(e):
    lane = lax.broadcasted_iota(jnp.int32, (1, PAIR), 1)
    chosen = (lane < HD) if e == 0 else (lane >= HD)
    return jnp.where(chosen, 1.0, 0.0)


def join_heads(first, second):
    lane = lax.broadcasted_iota(jnp.int32, first.shape, 1)
    return jnp.where(lane < HD, first, second)


def attend_forward(q, segments, contexts, inverses, lo):
    rows = slice(lo, lo + BLOCK)
    results = []
    for e in range(2):
        query = q[rows, :] * head_lanes(e).astype(BF16)
        scores = [edit(mm(query, k, NT)) for k, _, _, edit in segments]
        peak = functools.reduce(
            jnp.maximum, [jnp.max(piece, axis=-1, keepdims=True) for piece in scores]
        )
        total = None
        for piece, (_, v, store, _) in zip(scores, segments):
            weights = jnp.exp(piece - peak).astype(BF16)
            store(e, weights)
            wide = jnp.concatenate([v, jnp.ones(v.shape, BF16)], axis=1)
            part = mm(weights, wide, NN)
            total = part if total is None else total + part
        inverse = 1.0 / total[:, PAIR:]
        results.append((total[:, :PAIR] * inverse, inverse))
    contexts[rows, :] = join_heads(results[0][0], results[1][0]).astype(BF16)
    inverses[rows, :] = join_heads(results[0][1], results[1][1])


def attend_backward(q, grad, ctx, inv, segments, grad_query, lo):
    rows = slice(lo, lo + BLOCK)
    scaled = grad[rows, :].astype(F32) * inv[rows, :]
    product = scaled * ctx[rows, :].astype(F32)
    low = scaled.astype(BF16)
    total = None
    for e in range(2):
        lanes = head_lanes(e)
        low_lanes = lanes.astype(BF16)
        delta = jnp.sum(product * lanes, axis=-1, keepdims=True)
        grad_low = low * low_lanes
        query = q[rows, :] * low_lanes
        for k, v, load, add in segments:
            weights = load(e)
            slope = mm(grad_low, v, NT) - delta
            grad_scores = (weights.astype(F32) * slope).astype(BF16)
            part = mm(grad_scores, k * low_lanes, NN)
            total = part if total is None else total + part
            add(mm(grad_scores, query, TN), mm(weights, grad_low, TN))
    grad_query[rows, :] = (total * SCALE).astype(BF16)


def same(scores):
    return scores


def self_forward_kernel(info, q, k, v, ko, vo, ctx, inv, we, wo):
    tokens = q.shape[0]

    def masked(lo, col_lo, prefix_len):
        def edit(scores):
            row = lo + lax.broadcasted_iota(jnp.int32, scores.shape, 0)
            col = col_lo + lax.broadcasted_iota(jnp.int32, scores.shape, 1)
            allowed = col <= row
            if prefix_len is not None:
                allowed = allowed | (col < prefix_len)
            return jnp.where(allowed, scores, MASKED)

        return edit

    def keeper(target, lo, col_lo, width):
        def store(e, weights):
            target[e, lo : lo + BLOCK, col_lo : col_lo + width] = weights

        return store

    @pl.when(info[0] == 0)
    def _():
        for lo in range(0, tokens, BLOCK):
            attend_forward(
                q,
                [(k[...], v[...], keeper(we, lo, 0, tokens), masked(lo, 0, info[1]))],
                ctx,
                inv,
                lo,
            )

    @pl.when(info[0] != 0)
    def _():
        for lo in range(0, tokens, BLOCK):
            near = slice(lo, lo + BLOCK)
            segments = [(ko[...], vo[...], keeper(wo, lo, 0, tokens), same)]
            if lo:
                segments.append((k[:lo, :], v[:lo, :], keeper(we, lo, 0, lo), same))
            segments.append(
                (k[near, :], v[near, :], keeper(we, lo, lo, BLOCK), masked(lo, lo, None))
            )
            attend_forward(q, segments, ctx, inv, lo)


def self_backward_kernel(
    info, q, k, v, ko, vo, ctx, inv, we, wo, grad, dq, dk, dv, dko, dvo, ak, av, ako, avo
):
    tokens = q.shape[0]
    ak[...] = jnp.zeros_like(ak)
    av[...] = jnp.zeros_like(av)

    def loader(source, lo, col_lo, width):
        return lambda e: source[e, lo : lo + BLOCK, col_lo : col_lo + width]

    def adder(keys, values, col_lo, width):
        def add(part_keys, part_values):
            keys[col_lo : col_lo + width, :] += part_keys
            values[col_lo : col_lo + width, :] += part_values

        return add

    @pl.when(info[0] == 0)
    def _():
        for lo in range(0, tokens, BLOCK):
            attend_backward(
                q,
                grad,
                ctx,
                inv,
                [(k[...], v[...], loader(we, lo, 0, tokens), adder(ak, av, 0, tokens))],
                dq,
                lo,
            )

    @pl.when(info[0] != 0)
    def _():
        ako[...] = jnp.zeros_like(ako)
        avo[...] = jnp.zeros_like(avo)
        for lo in range(0, tokens, BLOCK):
            width = lo + BLOCK
            segments = [
                (ko[...], vo[...], loader(wo, lo, 0, tokens), adder(ako, avo, 0, tokens)),
            ]
            if lo:
                segments.append(
                    (k[:lo, :], v[:lo, :], loader(we, lo, 0, lo), adder(ak, av, 0, lo))
                )
            segments.append(
                (
                    k[lo:width, :],
                    v[lo:width, :],
                    loader(we, lo, lo, BLOCK),
                    adder(ak, av, lo, BLOCK),
                )
            )
            attend_backward(q, grad, ctx, inv, segments, dq, lo)
        dko[...] = ako[...].astype(BF16)
        dvo[...] = avo[...].astype(BF16)

    dk[...] = ak[...].astype(BF16)
    dv[...] = av[...].astype(BF16)


def cross_forward_kernel(q, k, v, ctx, inv, we):
    for lo in range(0, q.shape[0], BLOCK):

        def store(e, weights, lo=lo):
            we[e, lo : lo + BLOCK, :] = weights

        attend_forward(q, [(k[...], v[...], store, same)], ctx, inv, lo)


def cross_backward_kernel(q, k, v, ctx, inv, we, grad, dq, dk, dv, ak, av):
    ak[...] = jnp.zeros_like(ak)
    av[...] = jnp.zeros_like(av)
    for lo in range(0, q.shape[0], BLOCK):

        def load(e, lo=lo):
            return we[e, lo : lo + BLOCK, :]

        def add(part_keys, part_values):
            ak[...] += part_keys
            av[...] += part_values

        attend_backward(q, grad, ctx, inv, [(k[...], v[...], load, add)], dq, lo)
    dk[...] = ak[...].astype(BF16)
    dv[...] = av[...].astype(BF16)


def lanes_of(rows):
    return pl.BlockSpec((rows, PAIR), lambda h: (0, h))


def weights_of(rows, columns):
    return pl.BlockSpec((2, rows, columns), lambda h: (h, 0, 0))


def self_forward(info, q, k, v, ko, vo):
    tokens, width = q.shape
    heads = width // HD
    row = lanes_of(tokens)
    square = shaped((heads, tokens, tokens), BF16)
    return pl.pallas_call(
        self_forward_kernel,
        grid=(width // PAIR,),
        out_shape=(shaped((tokens, width), BF16), shaped((tokens, width), F32), square, square),
        in_specs=[SMEM] + [row] * 5,
        out_specs=(row, row) + (weights_of(tokens, tokens),) * 2,
        compiler_params=limit(48),
        cost_estimate=cost(heads * tokens * tokens * 2 * 256 * 2, 12 << 20),
    )(info, q, k, v, ko, vo)


def self_backward(info, q, k, v, ko, vo, ctx, inv, we, wo, grad):
    tokens, width = q.shape
    heads = width // HD
    row = lanes_of(tokens)
    low = shaped((tokens, width), BF16)
    return pl.pallas_call(
        self_backward_kernel,
        grid=(width // PAIR,),
        out_shape=(low,) * 5,
        in_specs=[SMEM] + [row] * 7 + [weights_of(tokens, tokens)] * 2 + [row],
        out_specs=(row,) * 5,
        scratch_shapes=[pltpu.VMEM((tokens, PAIR), F32)] * 4,
        compiler_params=limit(48),
        cost_estimate=cost(heads * tokens * tokens * 2 * 256 * 4, 14 << 20),
    )(info, q, k, v, ko, vo, ctx, inv, we, wo, grad)


def cross_forward(q, k, v):
    tokens, width = q.shape
    rows = k.shape[0]
    heads = width // HD
    return pl.pallas_call(
        cross_forward_kernel,
        grid=(width // PAIR,),
        out_shape=(
            shaped((tokens, width), BF16),
            shaped((tokens, width), F32),
            shaped((heads, tokens, rows), BF16),
        ),
        in_specs=[lanes_of(tokens), lanes_of(rows), lanes_of(rows)],
        out_specs=(lanes_of(tokens), lanes_of(tokens), weights_of(tokens, rows)),
        compiler_params=limit(48),
        cost_estimate=cost(heads * tokens * rows * 256 * 2, 5 << 20),
    )(q, k, v)


def cross_backward(q, k, v, ctx, inv, we, grad):
    tokens, width = q.shape
    rows = k.shape[0]
    heads = width // HD
    return pl.pallas_call(
        cross_backward_kernel,
        grid=(width // PAIR,),
        out_shape=(
            shaped((tokens, width), BF16),
            shaped((rows, width), BF16),
            shaped((rows, width), BF16),
        ),
        in_specs=[lanes_of(tokens), lanes_of(rows), lanes_of(rows)]
        + [lanes_of(tokens)] * 2
        + [weights_of(tokens, rows), lanes_of(tokens)],
        out_specs=(lanes_of(tokens), lanes_of(rows), lanes_of(rows)),
        scratch_shapes=[pltpu.VMEM((rows, PAIR), F32)] * 2,
        compiler_params=limit(48),
        cost_estimate=cost(heads * tokens * rows * 256 * 4, 6 << 20),
    )(q, k, v, ctx, inv, we, grad)


def project_self_kernel(info, x, xo, w, bq, bv, q, k, v, ko, vo):
    rows = x[...]
    q[...] = (mm(rows, w[0], NN) + bq[...].astype(F32)).astype(BF16) * jnp.asarray(SCALE, BF16)
    k[...] = mm(rows, w[1], NN).astype(BF16)
    v[...] = (mm(rows, w[2], NN) + bv[...].astype(F32)).astype(BF16)

    @pl.when(info[0] != 0)
    def _():
        other = xo[...]
        ko[...] = mm(other, w[1], NN).astype(BF16)
        vo[...] = (mm(other, w[2], NN) + bv[...].astype(F32)).astype(BF16)


def project_self(info, x, xo, w, bq, bv):
    low = shaped(x.shape, BF16)
    return pl.pallas_call(
        project_self_kernel,
        out_shape=(low,) * 5,
        in_specs=[SMEM] + [VMEM] * 5,
        compiler_params=limit(48),
        cost_estimate=cost(5 * x.size * x.shape[1], 5 << 20),
    )(info, x, xo, w, bq, bv)


def first_norm_kernel(
    ctx, x, mem, memo, w, ob, gain, bias, bq, bv, first, normed, inverse, q, k, v
):
    summed = x[...].astype(F32) + mm(ctx[...], w[0], NT) + ob[...].astype(F32)
    n, r = norm_forward(summed)
    out = n * gain[...].astype(F32) + bias[...].astype(F32)
    normed[...] = n
    inverse[...] = r
    first[...] = out
    q[...] = (mm(out.astype(BF16), w[1], NN) + bq[...].astype(F32)).astype(BF16) * jnp.asarray(
        SCALE, BF16
    )
    rows = mem.shape[0]
    for source, lo in ((mem, 0), (memo, rows)):
        k[lo : lo + rows, :] = mm(source[...], w[2], NN).astype(BF16)
        v[lo : lo + rows, :] = (mm(source[...], w[3], NN) + bv[...].astype(F32)).astype(BF16)


def first_norm(ctx, x, mem, memo, w, ob, gain, bias, bq, bv):
    rows = 2 * mem.shape[0]
    tokens, width = x.shape
    full = shaped(x.shape, F32)
    return pl.pallas_call(
        first_norm_kernel,
        out_shape=(
            full,
            full,
            shaped((tokens, 1), F32),
            shaped(x.shape, BF16),
            shaped((rows, width), BF16),
            shaped((rows, width), BF16),
        ),
        in_specs=[VMEM] * 10,
        compiler_params=limit(48),
        cost_estimate=cost(3 * x.size * width, 8 << 20),
    )(ctx, x, mem, memo, w, ob, gain, bias, bq, bv)


def feed_kernel(
    ctx,
    first,
    cot,
    wo,
    wf,
    ob,
    gain2,
    bias2,
    fib,
    fob,
    gain3,
    bias3,
    out,
    dw,
    du2,
    db2,
    sums,
    hsum,
    act,
    slope,
    acc,
    second,
):
    tokens, width = first.shape
    chunks = wf.shape[2] // width
    summed = first[...] + mm(ctx[...], wo[4], NT) + ob[...].astype(F32)
    n2, r2 = norm_forward(summed)
    out2 = n2 * gain2[...].astype(F32) + bias2[...].astype(F32)
    second[...] = out2.astype(BF16)
    acc[...] = out2 + fob[...].astype(F32)

    @pl.loop(0, chunks)
    def _(c):
        cols = pl.ds(pl.multiple_of(c * width, width), width)
        hidden = mm(second[...], wf[0, :, cols], NN) + fib[:, cols].astype(F32)
        gate = 1.0 / (1.0 + jnp.exp(-hidden))
        active = (hidden * gate).astype(BF16)
        act[:, cols] = active
        slope[:, cols] = (gate * (1.0 + hidden * (1.0 - gate))).astype(BF16)
        acc[...] += mm(active, wf[1, :, cols], NT)

    n3, r3 = norm_forward(acc[...])
    out[...] = (n3 * gain3[...].astype(F32) + bias3[...].astype(F32)).astype(BF16)
    dy = cot[...].astype(F32)
    du3 = norm_backward(dy, n3, r3, gain3[...].astype(F32))
    db3 = du3.astype(BF16)
    sums[6:7, :] = column_sum(db3)
    sums[7:8, :] = column_sum(dy * n3)
    sums[8:9, :] = column_sum(dy)
    acc[...] = du3
    db2[...] = db3

    @pl.loop(0, chunks)
    def _(c):
        cols = pl.ds(pl.multiple_of(c * width, width), width)
        back = db2[...]
        dact = mm(back, wf[1, :, cols], NN)
        dhid = (dact * slope[:, cols].astype(F32)).astype(BF16)
        hsum[:, cols] = column_sum(dhid)
        dw[1, :, cols] = mm(back, act[:, cols], TN).astype(BF16)
        dw[0, :, cols] = mm(second[...], dhid, TN).astype(BF16)
        acc[...] += mm(dhid, wf[0, :, cols], NT)

    dsecond = acc[...]
    grad2 = norm_backward(dsecond, n2, r2, gain2[...].astype(F32))
    low2 = grad2.astype(BF16)
    du2[...] = grad2
    db2[...] = low2
    sums[3:4, :] = column_sum(low2)
    sums[4:5, :] = column_sum(dsecond * n2)
    sums[5:6, :] = column_sum(dsecond)
    sums[0:3, :] = jnp.zeros((3, width), F32)
    sums[9:16, :] = jnp.zeros((7, width), F32)


def feed(ctx, first, cot, wo, wf, ob, gain2, bias2, fib, fob, gain3, bias3):
    tokens, width = first.shape
    wide = wf.shape[2]
    return pl.pallas_call(
        feed_kernel,
        out_shape=(
            shaped(first.shape, BF16),
            shaped(wf.shape, BF16),
            shaped(first.shape, F32),
            shaped(first.shape, BF16),
            shaped((16, width), F32),
            shaped((1, wide), F32),
        ),
        in_specs=[VMEM] * 12,
        scratch_shapes=[
            pltpu.VMEM((tokens, wide), BF16),
            pltpu.VMEM((tokens, wide), BF16),
            pltpu.VMEM((tokens, width), F32),
            pltpu.VMEM((tokens, width), BF16),
        ],
        compiler_params=limit(48),
        cost_estimate=cost(6 * tokens * width * wide, 14 << 20),
    )(ctx, first, cot, wo, wf, ob, gain2, bias2, fib, fob, gain3, bias3)


def context_grad_kernel(db, w, out):
    out[...] = mm(db[...], w[4], NN).astype(BF16)


def context_grad(db, w):
    return pl.pallas_call(
        context_grad_kernel,
        out_shape=shaped(db.shape, BF16),
        in_specs=[VMEM] * 2,
        compiler_params=limit(48),
        cost_estimate=cost(db.size * db.shape[1], 2 << 20),
    )(db, w)


def first_back_kernel(du2, dq2, normed, inverse, w, gain, du1, db1, dctx, sums):
    width = du2.shape[1]
    dfirst = du2[...] + mm(dq2[...], w[1], NT)
    n = normed[...]
    grad = norm_backward(dfirst, n, inverse[...], gain[...].astype(F32))
    low = grad.astype(BF16)
    du1[...] = grad
    db1[...] = low
    dctx[...] = mm(low, w[0], NN).astype(BF16)
    sums[0:1, :] = column_sum(low)
    sums[1:2, :] = column_sum(dfirst * n)
    sums[2:3, :] = column_sum(dfirst)
    sums[3:8, :] = jnp.zeros((5, width), F32)


def first_back(du2, dq2, normed, inverse, w, gain):
    width = du2.shape[1]
    low = shaped(du2.shape, BF16)
    return pl.pallas_call(
        first_back_kernel,
        out_shape=(shaped(du2.shape, F32), low, low, shaped((8, width), F32)),
        in_specs=[VMEM] * 6,
        compiler_params=limit(48),
        cost_estimate=cost(2 * du2.size * width, 8 << 20),
    )(du2, dq2, normed, inverse, w, gain)


def middle_grads_kernel(
    first, dq2, mem, memo, dk2, dv2, db2, ctx2, db1, ctx1, w, dw, own, other, sums
):
    rows, width = mem.shape
    dw[0] = mm(db1[...], ctx1[...], TN).astype(BF16)
    dw[1] = mm(first[...].astype(BF16), dq2[...], TN).astype(BF16)
    for slot, grad in ((2, dk2), (3, dv2)):
        dw[slot] = (
            mm(mem[...], grad[:rows, :], TN) + mm(memo[...], grad[rows:, :], TN)
        ).astype(BF16)
    dw[4] = mm(db2[...], ctx2[...], TN).astype(BF16)
    back = mm(dk2[...], w[2], NT) + mm(dv2[...], w[3], NT)
    own[...] = back[:rows, :]
    other[...] = back[rows:, :].astype(BF16)
    sums[0:1, :] = column_sum(dq2[...])
    sums[1:2, :] = column_sum(dv2[...])
    sums[2:8, :] = jnp.zeros((6, width), F32)


def middle_grads(first, dq2, mem, memo, dk2, dv2, db2, ctx2, db1, ctx1, w):
    tokens, width = first.shape
    rows = mem.shape[0]
    return pl.pallas_call(
        middle_grads_kernel,
        out_shape=(
            shaped(w.shape, BF16),
            shaped((rows, width), F32),
            shaped((rows, width), BF16),
            shaped((8, width), F32),
        ),
        in_specs=[VMEM] * 11,
        compiler_params=limit(48),
        cost_estimate=cost(5 * first.size * width, 10 << 20),
    )(first, dq2, mem, memo, dk2, dv2, db2, ctx2, db1, ctx1, w)


def self_grads_kernel(info, x, xo, dq, dk, dv, dko, dvo, w, dw, other, sums):
    width = x.shape[1]
    dw[0] = mm(x[...], dq[...], TN).astype(BF16)
    sums[0:1, :] = column_sum(dq[...])
    sums[2:8, :] = jnp.zeros((6, width), F32)

    @pl.when(info[0] == 0)
    def _():
        dw[1] = mm(x[...], dk[...], TN).astype(BF16)
        dw[2] = mm(x[...], dv[...], TN).astype(BF16)
        sums[1:2, :] = column_sum(dv[...])
        other[...] = jnp.zeros_like(other)

    @pl.when(info[0] != 0)
    def _():
        dw[1] = (mm(x[...], dk[...], TN) + mm(xo[...], dko[...], TN)).astype(BF16)
        dw[2] = (mm(x[...], dv[...], TN) + mm(xo[...], dvo[...], TN)).astype(BF16)
        sums[1:2, :] = column_sum(dv[...]) + column_sum(dvo[...])
        other[...] = (mm(dko[...], w[1], NT) + mm(dvo[...], w[2], NT)).astype(BF16)


def self_grads(info, x, xo, dq, dk, dv, dko, dvo, w):
    width = x.shape[1]
    return pl.pallas_call(
        self_grads_kernel,
        out_shape=(shaped(w.shape, BF16), shaped(x.shape, BF16), shaped((8, width), F32)),
        in_specs=[SMEM] + [VMEM] * 8,
        compiler_params=limit(48),
        cost_estimate=cost(7 * x.size * width, 8 << 20),
    )(info, x, xo, dq, dk, dv, dko, dvo, w)


def input_grads_kernel(du1, dq, dk, dv, w, back, out):
    out[...] = (
        du1[...]
        + mm(dq[...], w[0], NT)
        + mm(dk[...], w[1], NT)
        + mm(dv[...], w[2], NT)
        + back[...].astype(F32)
    )


def input_grads(du1, dq, dk, dv, w, back):
    return pl.pallas_call(
        input_grads_kernel,
        out_shape=shaped(du1.shape, F32),
        in_specs=[VMEM] * 6,
        compiler_params=limit(48),
        cost_estimate=cost(3 * du1.size * du1.shape[1], 6 << 20),
    )(du1, dq, dk, dv, w, back)


def on_device(
    inputs,
    memory,
    prefix,
    self_query,
    self_query_bias,
    self_key,
    self_value,
    self_value_bias,
    self_out,
    self_out_bias,
    self_norm_gain,
    self_norm_bias,
    cross_query,
    cross_query_bias,
    cross_key,
    cross_value,
    cross_value_bias,
    cross_out,
    cross_out_bias,
    cross_norm_gain,
    cross_norm_bias,
    feed_in,
    feed_in_bias,
    feed_out,
    feed_out_bias,
    feed_norm_gain,
    feed_norm_bias,
    cotangent,
):
    nd, nt = lax.axis_size("dp"), lax.axis_size("tensor")
    me_d, me_t = lax.axis_index("dp"), lax.axis_index("tensor")
    late = me_t % 2
    width = inputs.shape[1]
    assert LEN == 2 * inputs.shape[0] and MEM == 2 * memory.shape[0]
    assert nd & (nd - 1) == 0 and nt & (nt - 1) == 0
    prefix_here = jnp.where(late == 0, lax.dynamic_index_in_dim(prefix, me_t // 2, keepdims=False), 0)
    info = jnp.stack([late, prefix_here, me_d, me_t]).astype(jnp.int32)

    columns = self_query_bias.shape[0]
    riders = jnp.concatenate(
        [self_query_bias, self_value_bias, cross_query_bias, cross_value_bias, feed_in_bias]
    ).reshape(-1, columns)
    count = riders.shape[0]
    riders = jnp.pad(riders, ((0, -count % 16), (0, 0)))
    projections = jnp.stack([self_query, self_key, self_value])
    flat = projections.reshape(-1, columns)
    line_self = along_line(jnp.concatenate([flat, riders]))
    line_biases = line_self[:, flat.shape[0] :]
    line_self = line_self[:, : flat.shape[0]].reshape((nt,) + projections.shape)
    line_biases = jnp.take(line_biases, jnp.bitwise_xor(jnp.arange(nt), me_t), axis=0)
    biases = [line_biases[:, i].reshape(1, width) for i in range(4)]
    hidden_bias = line_biases[:, 4:count].reshape(1, -1)
    row = lambda vector: vector.reshape(1, -1)

    group_self = over_planes(line_self)
    inputs_other = hand_over(inputs, 0, 1)
    memory_other = swap(memory, 0, 1)
    group_middle = gather_group(
        jnp.stack([self_out.T, cross_query, cross_key, cross_value, cross_out.T])
    )
    group_feed = gather_group(jnp.stack([feed_in, feed_out.T]))

    w_self = assemble(info, *group_self)
    q1, k1, v1, k1o, v1o = project_self(info, inputs, inputs_other, w_self, biases[0], biases[1])
    ctx1, inv1, we1, wo1 = self_forward(info, q1, k1, v1, k1o, v1o)
    w_middle = assemble(info, *group_middle)
    first, normed1, inverse1, q2, k2, v2 = first_norm(
        ctx1,
        inputs,
        memory,
        memory_other,
        w_middle,
        row(self_out_bias),
        row(self_norm_gain),
        row(self_norm_bias),
        biases[2],
        biases[3],
    )
    ctx2, inv2, we2 = cross_forward(q2, k2, v2)
    w_feed = assemble(info, *group_feed)
    outputs, dw_feed, du2, db2, sums_feed, sums_hidden = feed(
        ctx2,
        first,
        cotangent,
        w_middle,
        w_feed,
        row(cross_out_bias),
        row(cross_norm_gain),
        row(cross_norm_bias),
        hidden_bias,
        row(feed_out_bias),
        row(feed_norm_gain),
        row(feed_norm_bias),
    )
    grad_feed = scatter_group(*disperse(info, dw_feed))
    dctx2 = context_grad(db2, w_middle)
    dq2, dk2, dv2 = cross_backward(q2, k2, v2, ctx2, inv2, we2, dctx2)
    du1, db1, dctx1, sums_first = first_back(
        du2, dq2, normed1, inverse1, w_middle, row(self_norm_gain)
    )
    dw_middle, memory_own, memory_back, sums_cross = middle_grads(
        first, dq2, memory, memory_other, dk2, dv2, db2, ctx2, db1, ctx1, w_middle
    )
    grad_middle = scatter_group(*disperse(info, dw_middle))
    grad_memory = memory_own + swap(memory_back, 0, 1).astype(F32)
    early = jnp.concatenate(
        [
            sums_feed[:9] + jnp.pad(sums_first[:3], ((0, 6), (0, 0))),
            sums_cross[:2],
            sums_hidden.reshape(-1, width),
        ]
    )
    early = jnp.pad(early, ((0, 16 - early.shape[0]), (0, 0)))
    early = sum_everywhere(early)
    dq1, dk1, dv1, dk1o, dv1o = self_backward(
        info, q1, k1, v1, k1o, v1o, ctx1, inv1, we1, wo1, dctx1
    )
    dw_self, inputs_back, sums_self = self_grads(
        info, inputs, inputs_other, dq1, dk1, dv1, dk1o, dv1o, w_self
    )
    grad_self = scatter_group(*disperse(info, dw_self))
    late_sums = sum_everywhere(sums_self)
    grad_inputs = input_grads(du1, dq1, dk1, dv1, w_self, hand_over(inputs_back, 1, -1))

    def mine(vector):
        count = vector.shape[0] // nt
        return lax.dynamic_slice_in_dim(vector, me_t * count, count)

    return (
        outputs,
        grad_inputs,
        grad_memory,
        grad_self[0],
        mine(late_sums[0]),
        grad_self[1],
        grad_self[2],
        mine(late_sums[1]),
        grad_middle[0].T,
        early[0],
        early[1],
        early[2],
        grad_middle[1],
        mine(early[9]),
        grad_middle[2],
        grad_middle[3],
        mine(early[10]),
        grad_middle[4].T,
        early[3],
        early[4],
        early[5],
        grad_feed[0],
        mine(early[11:15].reshape(-1)),
        grad_feed[1].T,
        early[6],
        early[7],
        early[8],
    )


def solution(mesh):
    placed = (
        P(("dp", "tensor"), None),
        P(("dp", "tensor"), None),
        P("dp"),
        P("dp", "tensor"),
        P("tensor"),
        P("dp", "tensor"),
        P("dp", "tensor"),
        P("tensor"),
        P("tensor", "dp"),
        P(),
        P(),
        P(),
        P("dp", "tensor"),
        P("tensor"),
        P("dp", "tensor"),
        P("dp", "tensor"),
        P("tensor"),
        P("tensor", "dp"),
        P(),
        P(),
        P(),
        P("dp", "tensor"),
        P("tensor"),
        P("tensor", "dp"),
        P(),
        P(),
        P(),
        P(("dp", "tensor"), None),
    )
    return jax.shard_map(
        on_device,
        mesh=mesh,
        in_specs=placed,
        out_specs=(
            P(("dp", "tensor"), None),
            P(("dp", "tensor"), None),
            P(("dp", "tensor"), None),
            P("dp", "tensor"),
            P("tensor"),
            P("dp", "tensor"),
            P("dp", "tensor"),
            P("tensor"),
            P("tensor", "dp"),
            P(),
            P(),
            P(),
            P("dp", "tensor"),
            P("tensor"),
            P("dp", "tensor"),
            P("dp", "tensor"),
            P("tensor"),
            P("tensor", "dp"),
            P(),
            P(),
            P(),
            P("dp", "tensor"),
            P("tensor"),
            P("tensor", "dp"),
            P(),
            P(),
            P(),
        ),
        check_vma=False,
    )
```

```python
import functools

import jax
import jax.numpy as jnp
from jax import lax
from jax.experimental import pallas as pl
from jax.experimental.pallas import tpu as pltpu
from jax.sharding import PartitionSpec as P

HD = 64
LEN = 1024
MEM = 256
PAIR = 128
BLOCK = 256
BACK_BLOCK = 512

EPSILON = 1e-05
MASKED = -1e30
SCALE = float(HD) ** (-0.5)

F32 = jnp.float32
BF16 = jnp.bfloat16
NN = (((1,), (0,)), ((), ()))
NT = (((1,), (1,)), ((), ()))
TN = (((0,), (0,)), ((), ()))
SMEM = pl.BlockSpec(memory_space=pltpu.SMEM)
ANY = pl.BlockSpec(memory_space=pl.ANY)
VMEM = pl.BlockSpec(memory_space=pltpu.VMEM)


def mm(left_side, right_side, dims):
    return lax.dot_general(left_side, right_side, dims, preferred_element_type=F32)


def shaped(shape, dtype):
    return jax.ShapeDtypeStruct(shape, dtype)


def cost(macs, moved):
    return pl.CostEstimate(flops=macs // 64, bytes_accessed=moved // 64, transcendentals=0)


def limit(mebibytes):
    return pltpu.CompilerParams(vmem_limit_bytes=mebibytes << 20)


def far(*arrays):
    return [pltpu.with_memory_space_constraint(array, pltpu.HBM) for array in arrays]


def swap(array, dp_mask, tensor_mask):
    nd, nt = lax.axis_size("dp"), lax.axis_size("tensor")
    pairs = [
        (d * nt + t, (d ^ dp_mask) * nt + (t ^ tensor_mask)) for d in range(nd) for t in range(nt)
    ]
    return lax.ppermute(array, ("dp", "tensor"), pairs)


def hand_over(array, parity, step):
    nd, nt = lax.axis_size("dp"), lax.axis_size("tensor")
    pairs = [(d * nt + t, d * nt + t + step) for d in range(nd) for t in range(parity, nt, 2)]
    return lax.ppermute(array, ("dp", "tensor"), pairs)


def tree_sum(terms):
    while len(terms) > 1:
        terms = [terms[i] + terms[i + 1] for i in range(0, len(terms), 2)]
    return terms[0]


def doubled(line, bits):
    for bit in bits:
        line = jnp.concatenate([line, swap(line, 0, bit)])
    return line


def over_planes(line):
    return [line] + [swap(line, 2 * j, 0) for j in range(1, lax.axis_size("dp") // 2)]


def both_cores(planes, *others):
    plane = jnp.stack([after(planes[0], *others)] + planes[1:])
    return plane, swap(plane, 1, 0)


def rounded(values):
    return lax.optimization_barrier(values.astype(BF16))


def added(mine, other):
    return rounded(mine.astype(F32) + other.astype(F32))


def joined(arrays):
    return arrays[0] if len(arrays) == 1 else jnp.concatenate(arrays)


class Halves:
    def __init__(self, groups, r, rider):
        self.planes, self.nt = lax.axis_size("dp") // 2, lax.axis_size("tensor")
        self.groups, self.r, self.rider = groups, r, rider
        self.sizes = [self.nt * count * r for count in groups]
        self.total = self.planes * sum(self.sizes) + rider

    def parts(self, keep, got):
        pieces, lo = [], 0
        for size in self.sizes:
            cut = [slice(lo + j * size, lo + j * size + size) for j in range(self.planes)]
            pieces.append([added(keep[rows], got[rows]) for rows in cut])
            lo += self.planes * size
        return pieces, added(keep[lo:], got[lo:]) if self.rider else None

    def step(self, pieces, rider, index):
        count = self.planes.bit_length() - 1
        results = []
        for group, held in enumerate(pieces):
            bit = 1 << (index if group % 2 == 0 else count - 1 - index)
            stay = [j for j in held if not j & bit]
            carry = rider is not None and group == len(pieces) - 1
            sent = joined([held[j | bit] for j in stay] + ([rider] if carry else []))
            results.append((held, stay, carry, swap(sent, 2 * bit, 0)))
        return results

    def settle(self, moves, rider):
        pieces = []
        for group, (held, stay, carry, got) in enumerate(moves):
            size = self.sizes[group]
            pieces.append(
                {j: added(held[j], got[i * size : i * size + size]) for i, j in enumerate(stay)}
            )
            if carry:
                rider = added(rider, got[len(stay) * size :])
        return pieces, rider

    def line_parts(self, pieces, rider):
        parts = []
        for k in range(self.nt):
            rows = []
            for group, count in enumerate(self.groups):
                size = count * self.r
                rows.append(pieces[group][0][k * size : k * size + size])
            parts.append(joined(rows + ([rider] if rider is not None else [])))
        return parts


def direct_plane(pieces, rider):
    sent = [joined([piece, rider]) for piece in pieces]
    got = [sent[0]] + [swap(part, 2 * j, 0) for j, part in enumerate(sent) if j]
    total = rounded(tree_sum([part.astype(F32) for part in got]))
    return total[: pieces[0].shape[0]], total[pieces[0].shape[0] :]


def line_swaps(parts):
    return [parts[0]] + [swap(part, 0, k) for k, part in enumerate(parts) if k]


def line_sum(parts):
    return tree_sum([part.astype(F32) for part in parts])


def after(array, *others):
    return lax.optimization_barrier((array,) + others)[0]


def slot_blocks(info, planes, nt, slots=True):
    for j in range(planes):
        for c in range(2):
            d = jnp.bitwise_xor(info[2], 2 * j + c)
            for s in range(nt):
                yield j, c, s, d, jnp.bitwise_xor(info[3], s) if slots else s


def assemble_kernel(info, plane, sibling, whole, *, slots):
    planes, nt, n, r, w = plane.shape
    for j, c, s, d, t in slot_blocks(info, planes, nt, slots):
        rows = pl.ds(pl.multiple_of(d * r, r), r)
        columns = pl.ds(pl.multiple_of(t * w, w), w) if slots else slice(t * w, t * w + w)
        for i in range(n):
            whole[i, rows, columns] = (plane, sibling)[c][j, s, i]


def aligned(r, w):
    return w % PAIR == 0 and r % 16 == 0


def assemble(info, plane, sibling, slots=True):
    planes, nt, n, r, w = plane.shape
    nd = 2 * planes
    if aligned(r, w):
        return pl.pallas_call(
            functools.partial(assemble_kernel, slots=slots),
            out_shape=shaped((n, nd * r, nt * w), BF16),
            in_specs=[SMEM, VMEM, VMEM],
            out_specs=VMEM,
            compiler_params=limit(18),
            cost_estimate=cost(0, 4 * plane.size * 2),
        )(info, plane, sibling)
    full = jnp.stack([plane, sibling], axis=1).reshape(nd, nt, n, r, w)
    full = jnp.take(full, jnp.bitwise_xor(jnp.arange(nd), info[2]), axis=0)
    if slots:
        full = jnp.take(full, jnp.bitwise_xor(jnp.arange(nt), info[3]), axis=1)
    return full.transpose(2, 0, 3, 1, 4).reshape(n, nd * r, nt * w)


def disperse_kernel(info, whole, rider, keep, send, *, halves):
    n, r, w = whole.shape[0], halves.r, whole.shape[2] // halves.nt
    for j, c, s, d, t in slot_blocks(info, halves.planes, halves.nt):
        rows = pl.ds(pl.multiple_of(d * r, r), r)
        columns = pl.ds(pl.multiple_of(t * w, w), w)
        base, first = 0, 0
        for count, size in zip(halves.groups, halves.sizes):
            for i in range(count):
                lo = base + j * size + (s * count + i) * r
                (keep, send)[c][lo : lo + r, :] = whole[first + i, rows, columns]
            base += halves.planes * size
            first += count
    if halves.rider:
        for target in (keep, send):
            target[halves.total - halves.rider :, :] = rider[...]


def disperse(info, whole, groups, rider):
    nd, nt = lax.axis_size("dp"), lax.axis_size("tensor")
    n, r, w = whole.shape[0], whole.shape[1] // nd, whole.shape[2] // nt
    rider = rider.astype(BF16).reshape(-1, w)
    halves = Halves(groups, r, rider.shape[0])
    if aligned(r, w):
        flat = shaped((halves.total, w), BF16)
        if rider.shape[0] == 0:
            rider = jnp.zeros((16, w), BF16)
        keep, send = pl.pallas_call(
            functools.partial(disperse_kernel, halves=halves),
            out_shape=(flat, flat),
            in_specs=[SMEM, VMEM, VMEM],
            out_specs=(VMEM, VMEM),
            compiler_params=limit(18),
            cost_estimate=cost(0, 2 * whole.size * 2),
        )(info, whole, rider)
        return keep, send, halves
    full = whole.reshape(n, nd, r, nt, w).transpose(1, 3, 0, 2, 4)
    full = jnp.take(full, jnp.bitwise_xor(jnp.arange(nd), info[2]), axis=0)
    full = jnp.take(full, jnp.bitwise_xor(jnp.arange(nt), info[3]), axis=1)
    full = full.reshape(nd // 2, 2, nt, n, r, w)
    flats = []
    for c in range(2):
        rows, first = [], 0
        for count in groups:
            rows.append(full[:, c, :, first : first + count].reshape(-1, w))
            first += count
        flats.append(jnp.concatenate(rows + [rider]))
    return flats[0], flats[1], halves


def pack_kernel(wq, wk, wv, *rest):
    vectors, out = rest[:-1], rest[-1]
    r, w = wq.shape
    for i, block in enumerate((wq, wk, wv)):
        out[i * r : (i + 1) * r, :] = block[...]
    row = lax.broadcasted_iota(jnp.int32, (16, w), 0)
    filled = jnp.zeros((16, w), F32)
    count = 0
    for vector in vectors:
        for lo in range(0, vector.shape[1], w):
            filled = jnp.where(row == count, vector[:, lo : lo + w].astype(F32), filled)
            count += 1
    out[3 * r :, :] = filled.astype(BF16)


def pack(blocks, vectors):
    r, w = blocks[0].shape
    if aligned(r, w):
        return pl.pallas_call(
            pack_kernel,
            out_shape=shaped((3 * r + 16, w), BF16),
            in_specs=[VMEM] * (3 + len(vectors)),
            out_specs=VMEM,
            cost_estimate=cost(0, 8 * r * w * 2),
        )(*blocks, *[vector.reshape(1, -1) for vector in vectors])
    rows = jnp.concatenate(vectors).reshape(-1, w)
    return jnp.concatenate(list(blocks) + [jnp.pad(rows, ((0, 16 - rows.shape[0]), (0, 0)))])


def pack_rest_kernel(wo, wq, wk, wv, co, fi, fo, middle, feed):
    for i, block in enumerate((wo, wq, wk, wv, co)):
        middle[i] = block[...]
    feed[0] = fi[...]
    feed[1] = fo[...]


def pack_rest(middle, feed):
    if aligned(*middle[0].shape):
        return pl.pallas_call(
            pack_rest_kernel,
            out_shape=(
                shaped((len(middle),) + middle[0].shape, BF16),
                shaped((len(feed),) + feed[0].shape, BF16),
            ),
            in_specs=[VMEM] * (len(middle) + len(feed)),
            out_specs=(VMEM, VMEM),
            cost_estimate=cost(0, 8 * feed[0].size * 2),
        )(*middle, *feed)
    return jnp.stack(middle), jnp.stack(feed)


def spread_kernel(info, riders, small, hidden):
    nt, _, w = riders.shape
    for s in range(nt):
        t = jnp.bitwise_xor(info[3], s)
        block = riders[s].astype(F32)
        small[:, pl.ds(pl.multiple_of(t * w, w), w)] = block
        for i in range(4):
            hidden[:, pl.ds(pl.multiple_of((4 * t + i) * w, w), w)] = block[4 + i : 5 + i]


def spread(info, riders):
    nt, _, w = riders.shape
    if aligned(16, w):
        return pl.pallas_call(
            spread_kernel,
            out_shape=(shaped((16, nt * w), F32), shaped((1, 4 * nt * w), F32)),
            in_specs=[SMEM, VMEM],
            out_specs=(VMEM, VMEM),
            cost_estimate=cost(0, 64 * nt * w),
        )(info, riders)
    full = jnp.take(riders, jnp.bitwise_xor(jnp.arange(nt), info[3]), axis=0).astype(F32)
    return full.transpose(1, 0, 2).reshape(16, nt * w), full[:, 4:8].reshape(1, -1)


def norm_forward(summed):
    row_mean = jnp.mean(summed, axis=-1, keepdims=True)
    centred = summed - row_mean
    variance = jnp.mean(centred * centred, axis=-1, keepdims=True)
    inverse = lax.rsqrt(variance + EPSILON)
    return centred * inverse, inverse


def norm_backward(grad_out, normed, inverse, norm_gain):
    grad_normed = grad_out * norm_gain
    return inverse * (
        grad_normed
        - jnp.mean(grad_normed, axis=-1, keepdims=True)
        - normed * jnp.mean(grad_normed * normed, axis=-1, keepdims=True)
    )


def column_sum(values):
    return jnp.sum(values.astype(F32), axis=0, keepdims=True)


def head_lanes(e):
    lane = lax.broadcasted_iota(jnp.int32, (1, PAIR), 1)
    chosen = (lane < HD) if e == 0 else (lane >= HD)
    return jnp.where(chosen, 1.0, 0.0)


def join_heads(first, second):
    lane = lax.broadcasted_iota(jnp.int32, first.shape, 1)
    return jnp.where(lane < HD, first, second)


def attend_forward(q, segments, contexts, logs, lo):
    rows = slice(lo, lo + BLOCK)
    results = []
    for e in range(2):
        query = q[rows, :] * head_lanes(e).astype(BF16)
        scores = [edit(mm(query, k, NT)) for k, _, edit in segments]
        peak = functools.reduce(
            jnp.maximum, [jnp.max(piece, axis=-1, keepdims=True) for piece in scores]
        )
        total = None
        for piece, (_, v, _) in zip(scores, segments):
            weights = jnp.exp(piece - peak).astype(BF16)
            wide = jnp.concatenate([v, jnp.ones(v.shape, BF16)], axis=1)
            part = mm(weights, wide, NN)
            total = part if total is None else total + part
        row_total = total[:, PAIR:]
        results.append((total[:, :PAIR] / row_total, peak + jnp.log(row_total)))
    contexts[rows, :] = join_heads(results[0][0], results[1][0]).astype(BF16)
    logs[rows, :] = join_heads(results[0][1], results[1][1])


def attend_backward(q, grad, ctx, logs, segments, grad_query, lo):
    rows = slice(lo, lo + BACK_BLOCK)
    grad_rows = grad[rows, :]
    product = grad_rows.astype(F32) * ctx[rows, :].astype(F32)
    query_rows = q[rows, :]
    query_turned = jnp.transpose(query_rows)
    grad_turned = jnp.transpose(grad_rows)
    total = None
    for e in range(2):
        lanes = head_lanes(e)
        low_lanes = lanes.astype(BF16)
        delta = jnp.sum(product * lanes, axis=-1, keepdims=True)
        row_log = logs[rows, e * HD : e * HD + 1]
        grad_low = grad_rows * low_lanes
        query = query_rows * low_lanes
        for k, v, edit, add in segments:
            weights = jnp.exp(edit(mm(query, k, NT)) - row_log)
            slope = mm(grad_low, v, NT) - delta
            grad_scores = (weights * slope).astype(BF16)
            part = mm(grad_scores, k * low_lanes, NN)
            total = part if total is None else total + part
            head = slice(e * HD, e * HD + HD)
            add(
                head,
                mm(query_turned[head], grad_scores, NN),
                mm(grad_turned[head], weights.astype(BF16), NN),
            )
    grad_query[rows, :] = (total * SCALE).astype(BF16)


def same(scores):
    return scores


def masked(lo, col_lo, prefix_len):
    def edit(scores):
        row = lo + lax.broadcasted_iota(jnp.int32, scores.shape, 0)
        col = col_lo + lax.broadcasted_iota(jnp.int32, scores.shape, 1)
        allowed = col <= row
        if prefix_len is not None:
            allowed = allowed | (col < prefix_len)
        return jnp.where(allowed, scores, MASKED)

    return edit


def adder(keys, values, col_lo, width):
    def add(head, part_keys, part_values):
        keys[head, col_lo : col_lo + width] += part_keys
        values[head, col_lo : col_lo + width] += part_values

    return add


def self_forward_kernel(info, q, k, v, ko, vo, ctx, logs):
    tokens = q.shape[0]

    @pl.when(info[0] == 0)
    def _():
        for lo in range(0, tokens, BLOCK):
            attend_forward(q, [(k[...], v[...], masked(lo, 0, info[1]))], ctx, logs, lo)

    @pl.when(info[0] != 0)
    def _():
        for lo in range(0, tokens, BLOCK):
            near = slice(lo, lo + BLOCK)
            segments = [(ko[...], vo[...], same)]
            if lo:
                segments.append((k[:lo, :], v[:lo, :], same))
            segments.append((k[near, :], v[near, :], masked(lo, lo, None)))
            attend_forward(q, segments, ctx, logs, lo)


def self_backward_kernel(
    info, q, k, v, ko, vo, ctx, logs, low, w, dq, dk, dv, dko, dvo, ak, av, ako, avo, grad
):
    tokens = q.shape[0]
    ak[...] = jnp.zeros_like(ak)
    av[...] = jnp.zeros_like(av)
    grad[...] = mm(low[...], w[0], NN).astype(BF16)

    @pl.when(info[0] == 0)
    def _():
        for lo in range(0, tokens, BACK_BLOCK):
            segments = [(k[...], v[...], masked(lo, 0, info[1]), adder(ak, av, 0, tokens))]
            attend_backward(q, grad, ctx, logs, segments, dq, lo)

    @pl.when(info[0] != 0)
    def _():
        ako[...] = jnp.zeros_like(ako)
        avo[...] = jnp.zeros_like(avo)
        for lo in range(0, tokens, BACK_BLOCK):
            near = slice(lo, lo + BACK_BLOCK)
            segments = [(ko[...], vo[...], same, adder(ako, avo, 0, tokens))]
            if lo:
                segments.append((k[:lo, :], v[:lo, :], same, adder(ak, av, 0, lo)))
            segments.append(
                (k[near, :], v[near, :], masked(lo, lo, None), adder(ak, av, lo, BACK_BLOCK))
            )
            attend_backward(q, grad, ctx, logs, segments, dq, lo)
        dko[...] = jnp.transpose(ako[...]).astype(BF16)
        dvo[...] = jnp.transpose(avo[...]).astype(BF16)

    dk[...] = jnp.transpose(ak[...]).astype(BF16)
    dv[...] = jnp.transpose(av[...]).astype(BF16)


def cross_forward_kernel(q, k, v, ctx, logs):
    for lo in range(0, q.shape[0], BLOCK):
        attend_forward(q, [(k[...], v[...], same)], ctx, logs, lo)


def cross_backward_kernel(q, k, v, ctx, logs, low, w, dq, dk, dv, ak, av, grad):
    ak[...] = jnp.zeros_like(ak)
    av[...] = jnp.zeros_like(av)
    grad[...] = mm(low[...], w[0], NN).astype(BF16)
    for lo in range(0, q.shape[0], BACK_BLOCK):
        segments = [(k[...], v[...], same, adder(ak, av, 0, k.shape[0]))]
        attend_backward(q, grad, ctx, logs, segments, dq, lo)
    dk[...] = jnp.transpose(ak[...]).astype(BF16)
    dv[...] = jnp.transpose(av[...]).astype(BF16)


def lanes_of(rows, first=0):
    return pl.BlockSpec((rows, PAIR), lambda h: (0, first + h))


def output_columns(slot, width, first=0):
    return pl.BlockSpec((1, width, PAIR), lambda h: (slot, 0, first + h))


def self_forward(info, q, k, v, ko, vo):
    tokens, width = q.shape
    row = lanes_of(tokens)
    return pl.pallas_call(
        self_forward_kernel,
        grid=(width // PAIR,),
        out_shape=(shaped((tokens, width), BF16), shaped((tokens, width), F32)),
        in_specs=[SMEM] + [row] * 5,
        out_specs=(row, row),
        compiler_params=limit(16),
        cost_estimate=cost(width // HD * tokens * tokens * 2 * 256 * 2, 5 << 20),
    )(info, q, k, v, ko, vo)


def self_backward(info, q, k, v, ko, vo, ctx, logs, low, w, first, pairs):
    tokens, width = q.shape
    row = lanes_of(tokens, first)
    out = shaped((tokens, pairs * PAIR), BF16)
    return pl.pallas_call(
        self_backward_kernel,
        grid=(pairs,),
        out_shape=(out,) * 5,
        in_specs=[SMEM] + [row] * 7 + [VMEM, output_columns(0, width, first)],
        out_specs=(lanes_of(tokens),) * 5,
        scratch_shapes=[pltpu.VMEM((PAIR, tokens), F32)] * 4 + [pltpu.VMEM((tokens, PAIR), BF16)],
        compiler_params=limit(16),
        cost_estimate=cost(width // HD * tokens * tokens * 256 * 5, 8 << 20),
    )(info, *far(q, k, v, ko, vo, ctx, logs), low, *far(w))


def cross_forward(q, k, v):
    tokens, width = q.shape
    rows = k.shape[0]
    return pl.pallas_call(
        cross_forward_kernel,
        grid=(width // PAIR,),
        out_shape=(shaped((tokens, width), BF16), shaped((tokens, width), F32)),
        in_specs=[lanes_of(tokens), lanes_of(rows), lanes_of(rows)],
        out_specs=(lanes_of(tokens), lanes_of(tokens)),
        compiler_params=limit(16),
        cost_estimate=cost(width // HD * tokens * rows * 256 * 2, 3 << 20),
    )(q, k, v)


def cross_backward(q, k, v, ctx, logs, low, w):
    tokens, width = q.shape
    rows = k.shape[0]
    small = shaped((rows, width), BF16)
    return pl.pallas_call(
        cross_backward_kernel,
        grid=(width // PAIR,),
        out_shape=(shaped((tokens, width), BF16), small, small),
        in_specs=[lanes_of(tokens), lanes_of(rows), lanes_of(rows)]
        + [lanes_of(tokens)] * 2
        + [VMEM, output_columns(4, width)],
        out_specs=(lanes_of(tokens), lanes_of(rows), lanes_of(rows)),
        scratch_shapes=[pltpu.VMEM((PAIR, rows), F32)] * 2 + [pltpu.VMEM((tokens, PAIR), BF16)],
        compiler_params=limit(16),
        cost_estimate=cost(width // HD * tokens * rows * 256 * 5, 4 << 20),
    )(*far(q, k, v, ctx, logs), low, *far(w))


def project_self_kernel(info, x, xo, w, b, q, k, v, ko, vo):
    rows = x[...]
    q[...] = (mm(rows, w[0], NN) + b[0:1, :]).astype(BF16) * jnp.asarray(SCALE, BF16)
    k[...] = mm(rows, w[1], NN).astype(BF16)
    v[...] = (mm(rows, w[2], NN) + b[1:2, :]).astype(BF16)

    @pl.when(info[0] != 0)
    def _():
        other = xo[...]
        ko[...] = mm(other, w[1], NN).astype(BF16)
        vo[...] = (mm(other, w[2], NN) + b[1:2, :]).astype(BF16)


def project_self(info, x, xo, w, b):
    low = shaped(x.shape, BF16)
    return pl.pallas_call(
        project_self_kernel,
        out_shape=(low,) * 5,
        in_specs=[SMEM] + [VMEM] * 4,
        compiler_params=limit(16),
        cost_estimate=cost(5 * x.size * x.shape[1], 5 << 20),
    )(info, x, xo, w, b)


def first_norm_kernel(
    ctx, x, mem, memo, w, ob, gain, bias, b, first, normed, inverse, q, k, v
):
    summed = x[...].astype(F32) + mm(ctx[...], w[0], NT) + ob[...].astype(F32)
    n, r = norm_forward(summed)
    out = n * gain[...].astype(F32) + bias[...].astype(F32)
    normed[...] = n
    inverse[...] = r
    first[...] = out
    q[...] = (mm(out.astype(BF16), w[1], NN) + b[2:3, :]).astype(BF16) * jnp.asarray(SCALE, BF16)
    rows = mem.shape[0]
    for source, lo in ((mem, 0), (memo, rows)):
        k[lo : lo + rows, :] = mm(source[...], w[2], NN).astype(BF16)
        v[lo : lo + rows, :] = (mm(source[...], w[3], NN) + b[3:4, :]).astype(BF16)


def first_norm(ctx, x, mem, memo, w, ob, gain, bias, b):
    rows = 2 * mem.shape[0]
    tokens, width = x.shape
    full = shaped(x.shape, F32)
    return pl.pallas_call(
        first_norm_kernel,
        out_shape=(
            full,
            full,
            shaped((tokens, 1), F32),
            shaped(x.shape, BF16),
            shaped((rows, width), BF16),
            shaped((rows, width), BF16),
        ),
        in_specs=[VMEM] * 9,
        compiler_params=limit(16),
        cost_estimate=cost(3 * x.size * width, 8 << 20),
    )(ctx, x, mem, memo, w, ob, gain, bias, b)


def feed_kernel(
    ctx,
    first,
    cot,
    wo,
    wf,
    ob,
    gain2,
    bias2,
    fib,
    fob,
    gain3,
    bias3,
    out,
    dw,
    du2,
    db2,
    sums,
    hsum,
    act,
    slope,
    acc,
    second,
):
    tokens, width = first.shape
    chunks = wf.shape[2] // width
    summed = first[...] + mm(ctx[...], wo[4], NT) + ob[...].astype(F32)
    n2, r2 = norm_forward(summed)
    out2 = n2 * gain2[...].astype(F32) + bias2[...].astype(F32)
    second[...] = out2.astype(BF16)
    acc[...] = out2 + fob[...].astype(F32)

    @pl.loop(0, chunks)
    def _(c):
        cols = pl.ds(pl.multiple_of(c * width, width), width)
        hidden = mm(second[...], wf[0, :, cols], NN) + fib[:, cols]
        gate = 1.0 / (1.0 + jnp.exp(-hidden))
        active = (hidden * gate).astype(BF16)
        act[:, cols] = active
        slope[:, cols] = (gate * (1.0 + hidden * (1.0 - gate))).astype(BF16)
        acc[...] += mm(active, wf[1, :, cols], NT)

    n3, r3 = norm_forward(acc[...])
    out[...] = (n3 * gain3[...].astype(F32) + bias3[...].astype(F32)).astype(BF16)
    dy = cot[...].astype(F32)
    du3 = norm_backward(dy, n3, r3, gain3[...].astype(F32))
    db3 = du3.astype(BF16)
    sums[6:7, :] = column_sum(db3)
    sums[7:8, :] = column_sum(dy * n3)
    sums[8:9, :] = column_sum(dy)
    acc[...] = du3
    db2[...] = db3

    @pl.loop(0, chunks)
    def _(c):
        cols = pl.ds(pl.multiple_of(c * width, width), width)
        back = db2[...]
        dact = mm(back, wf[1, :, cols], NN)
        dhid = (dact * slope[:, cols].astype(F32)).astype(BF16)
        hsum[:, cols] = column_sum(dhid)
        dw[1, :, cols] = mm(back, act[:, cols], TN).astype(BF16)
        dw[0, :, cols] = mm(second[...], dhid, TN).astype(BF16)
        acc[...] += mm(dhid, wf[0, :, cols], NT)

    dsecond = acc[...]
    grad2 = norm_backward(dsecond, n2, r2, gain2[...].astype(F32))
    low2 = grad2.astype(BF16)
    du2[...] = grad2
    db2[...] = low2
    sums[3:4, :] = column_sum(low2)
    sums[4:5, :] = column_sum(dsecond * n2)
    sums[5:6, :] = column_sum(dsecond)
    sums[0:3, :] = jnp.zeros((3, width), F32)
    sums[9:16, :] = jnp.zeros((7, width), F32)


def feed(ctx, first, cot, wo, wf, ob, gain2, bias2, fib, fob, gain3, bias3):
    tokens, width = first.shape
    wide = wf.shape[2]
    return pl.pallas_call(
        feed_kernel,
        out_shape=(
            shaped(first.shape, BF16),
            shaped(wf.shape, BF16),
            shaped(first.shape, F32),
            shaped(first.shape, BF16),
            shaped((16, width), F32),
            shaped((1, wide), F32),
        ),
        in_specs=[VMEM] * 12,
        scratch_shapes=[
            pltpu.VMEM((tokens, wide), BF16),
            pltpu.VMEM((tokens, wide), BF16),
            pltpu.VMEM((tokens, width), F32),
            pltpu.VMEM((tokens, width), BF16),
        ],
        compiler_params=limit(28),
        cost_estimate=cost(6 * tokens * width * wide, 14 << 20),
    )(ctx, first, cot, wo, wf, ob, gain2, bias2, fib, fob, gain3, bias3)


def first_back_kernel(du2, dq2, normed, inverse, w, gain, du1, db1, sums):
    width = du2.shape[1]
    dfirst = du2[...] + mm(dq2[...], w[1], NT)
    n = normed[...]
    grad = norm_backward(dfirst, n, inverse[...], gain[...].astype(F32))
    low = grad.astype(BF16)
    du1[...] = grad
    db1[...] = low
    sums[0:1, :] = column_sum(low)
    sums[1:2, :] = column_sum(dfirst * n)
    sums[2:3, :] = column_sum(dfirst)
    sums[3:8, :] = jnp.zeros((5, width), F32)


def first_back(du2, dq2, normed, inverse, w, gain):
    width = du2.shape[1]
    low = shaped(du2.shape, BF16)
    return pl.pallas_call(
        first_back_kernel,
        out_shape=(shaped(du2.shape, F32), low, shaped((8, width), F32)),
        in_specs=[VMEM] * 6,
        compiler_params=limit(16),
        cost_estimate=cost(2 * du2.size * width, 8 << 20),
    )(du2, dq2, *far(normed, inverse, w), gain)


def middle_grads_kernel(
    first, dq2, mem, memo, dk2, dv2, db2, ctx2, db1, ctx1, w, dw, own, other, sums
):
    rows, width = mem.shape
    dw[0] = mm(db1[...], ctx1[...], TN).astype(BF16)
    dw[1] = mm(first[...].astype(BF16), dq2[...], TN).astype(BF16)
    for slot, grad in ((2, dk2), (3, dv2)):
        dw[slot] = (
            mm(mem[...], grad[:rows, :], TN) + mm(memo[...], grad[rows:, :], TN)
        ).astype(BF16)
    dw[4] = mm(db2[...], ctx2[...], TN).astype(BF16)
    back = mm(dk2[...], w[2], NT) + mm(dv2[...], w[3], NT)
    own[...] = back[:rows, :]
    other[...] = back[rows:, :].astype(BF16)
    sums[0:1, :] = column_sum(dq2[...])
    sums[1:2, :] = column_sum(dv2[...])
    sums[2:8, :] = jnp.zeros((6, width), F32)


def middle_grads(first, dq2, mem, memo, dk2, dv2, db2, ctx2, db1, ctx1, w):
    tokens, width = first.shape
    rows = mem.shape[0]
    return pl.pallas_call(
        middle_grads_kernel,
        out_shape=(
            shaped(w.shape, BF16),
            shaped((rows, width), F32),
            shaped((rows, width), BF16),
            shaped((8, width), F32),
        ),
        in_specs=[VMEM] * 11,
        compiler_params=limit(16),
        cost_estimate=cost(5 * first.size * width, 10 << 20),
    )(*far(first), dq2, *far(mem, memo), dk2, dv2, db2, *far(ctx2), db1, *far(ctx1, w))


def self_grads_kernel(
    info, x, xo, dqa, dka, dva, dkoa, dvoa, dqb, dkb, dvb, dkob, dvob, w, dw, other, sums
):
    width = x.shape[1]
    both = lambda left, right: jnp.concatenate([left[...], right[...]], axis=1)
    dq, dk, dv = both(dqa, dqb), both(dka, dkb), both(dva, dvb)
    dw[0] = mm(x[...], dq, TN).astype(BF16)
    sums[0:1, :] = column_sum(dq)
    sums[2:8, :] = jnp.zeros((6, width), F32)

    @pl.when(info[0] == 0)
    def _():
        dw[1] = mm(x[...], dk, TN).astype(BF16)
        dw[2] = mm(x[...], dv, TN).astype(BF16)
        sums[1:2, :] = column_sum(dv)
        other[...] = jnp.zeros_like(other)

    @pl.when(info[0] != 0)
    def _():
        dko, dvo = both(dkoa, dkob), both(dvoa, dvob)
        dw[1] = (mm(x[...], dk, TN) + mm(xo[...], dko, TN)).astype(BF16)
        dw[2] = (mm(x[...], dv, TN) + mm(xo[...], dvo, TN)).astype(BF16)
        sums[1:2, :] = column_sum(dv) + column_sum(dvo)
        other[...] = (mm(dko, w[1], NT) + mm(dvo, w[2], NT)).astype(BF16)


def self_grads(info, x, xo, early, late, w):
    width = x.shape[1]
    return pl.pallas_call(
        self_grads_kernel,
        out_shape=(shaped(w.shape, BF16), shaped(x.shape, BF16), shaped((8, width), F32)),
        in_specs=[SMEM] + [VMEM] * 13,
        compiler_params=limit(16),
        cost_estimate=cost(7 * x.size * width, 8 << 20),
    )(info, *far(x, xo), *early, *late, *far(w))


def input_grads_kernel(du1, dqa, dka, dva, dqb, dkb, dvb, w, back, out):
    both = lambda left, right: jnp.concatenate([left[...], right[...]], axis=1)
    out[...] = (
        du1[...]
        + mm(both(dqa, dqb), w[0], NT)
        + mm(both(dka, dkb), w[1], NT)
        + mm(both(dva, dvb), w[2], NT)
        + back[...].astype(F32)
    )


def input_grads(du1, early, late, w, back):
    return pl.pallas_call(
        input_grads_kernel,
        out_shape=shaped(du1.shape, F32),
        in_specs=[VMEM] * 9,
        compiler_params=limit(16),
        cost_estimate=cost(3 * du1.size * du1.shape[1], 6 << 20),
    )(*far(du1), *early, *late, *far(w), back)


def on_device(
    inputs,
    memory,
    prefix,
    self_query,
    self_query_bias,
    self_key,
    self_value,
    self_value_bias,
    self_out,
    self_out_bias,
    self_norm_gain,
    self_norm_bias,
    cross_query,
    cross_query_bias,
    cross_key,
    cross_value,
    cross_value_bias,
    cross_out,
    cross_out_bias,
    cross_norm_gain,
    cross_norm_bias,
    feed_in,
    feed_in_bias,
    feed_out,
    feed_out_bias,
    feed_norm_gain,
    feed_norm_bias,
    cotangent,
):
    nd, nt = lax.axis_size("dp"), lax.axis_size("tensor")
    me_d, me_t = lax.axis_index("dp"), lax.axis_index("tensor")
    late = me_t % 2
    width = inputs.shape[1]
    assert LEN == 2 * inputs.shape[0] and MEM == 2 * memory.shape[0]
    assert nd & (nd - 1) == 0 and nt & (nt - 1) == 0
    prefix_here = jnp.where(late == 0, lax.dynamic_index_in_dim(prefix, me_t // 2, keepdims=False), 0)
    info = jnp.stack([late, prefix_here, me_d, me_t]).astype(jnp.int32)

    columns = self_query_bias.shape[0]
    row = lambda vector: vector.reshape(1, -1)
    packed = pack(
        (self_query, self_key, self_value),
        (self_query_bias, self_value_bias, cross_query_bias, cross_value_bias, feed_in_bias),
    )
    middle_shard, feed_shard = pack_rest(
        (self_out.T, after(cross_query, packed), cross_key, cross_value, cross_out.T),
        (feed_in, feed_out.T),
    )

    bits = [1 << i for i in range(nt.bit_length() - 1)]
    swapped = [swap(packed, 0, k) for k in range(1, nt)]
    line_middle = doubled(middle_shard[None], bits[:1])
    inputs_other = hand_over(after(inputs, middle_shard), 0, 1)
    line_self = jnp.stack([after(packed, line_middle)] + swapped)
    count = 3 * self_query.shape[0]
    riders = line_self[:, count:]
    line_self = line_self[:, :count].reshape((nt, 3) + self_query.shape)
    line_middle = doubled(after(line_middle, line_self), bits[1:])
    line_feed = doubled(after(feed_shard, line_self)[None], bits[:1])
    group_self = both_cores(over_planes(line_self), line_middle, line_feed)
    planes_middle = over_planes(after(line_middle, group_self[0]))
    line_feed = doubled(after(line_feed, group_self[0]), bits[1:])
    head_biases, hidden_bias = spread(info, riders)

    w_self = assemble(info, *group_self)
    q1, k1, v1, k1o, v1o = project_self(info, inputs, inputs_other, w_self, head_biases)
    group_middle = both_cores(planes_middle, q1, line_feed)
    line_feed = after(line_feed, group_middle[0])
    planes_feed = over_planes(line_feed)
    memory_other = swap(after(memory, line_feed), 0, 1)
    q1 = after(q1, group_middle[0])
    ctx1, log1 = self_forward(info, q1, k1, v1, k1o, v1o)
    w_middle = assemble(info, *group_middle)
    first, normed1, inverse1, q2, k2, v2 = first_norm(
        ctx1,
        inputs,
        memory,
        memory_other,
        w_middle,
        row(self_out_bias),
        row(self_norm_gain),
        row(self_norm_bias),
        head_biases,
    )
    ctx2, log2 = cross_forward(q2, k2, v2)
    w_feed = assemble(info, *both_cores(planes_feed, ctx2))
    outputs, dw_feed, du2, db2, sums_feed, sums_hidden = feed(
        ctx2,
        first,
        cotangent,
        w_middle,
        w_feed,
        row(cross_out_bias),
        row(cross_norm_gain),
        row(cross_norm_bias),
        hidden_bias,
        row(feed_out_bias),
        row(feed_norm_gain),
        row(feed_norm_bias),
    )
    rounds = (nd // 2).bit_length() - 1
    keep, send, feed_halves = disperse(info, dw_feed, (1, 1), jnp.zeros((0, PAIR), BF16))
    got = swap(send, 1, 0)
    dq2, dk2, dv2 = cross_backward(q2, k2, v2, ctx2, log2, db2, w_middle)
    held, _ = feed_halves.parts(after(keep, dq2), got)
    held = [dict(enumerate(pieces)) for pieces in held]
    moves = feed_halves.step(held, None, 0)
    du2, _ = lax.optimization_barrier((du2, held))
    du1, db1, sums_first = first_back(
        du2, dq2, normed1, inverse1, w_middle, row(self_norm_gain)
    )
    dw_middle, memory_own, memory_back, sums_cross = middle_grads(
        first, dq2, memory, memory_other, dk2, dv2, db2, ctx2, db1, ctx1, w_middle
    )
    early = jnp.concatenate(
        [
            sums_first[:3],
            sums_feed[3:9],
            sums_cross[:2],
            sums_hidden.reshape(-1, width),
            jnp.zeros((1, width), F32),
        ]
    )
    early_rows = early.size // columns
    keep, send, middle_halves = disperse(info, dw_middle, (3, 2), early)
    held[0][0] = after(held[0][0], send)
    held, _ = feed_halves.settle(moves, None)
    got = swap(send, 1, 0)
    memory_got = swap(memory_back, 0, 1)
    for index in range(1, rounds):
        moves = feed_halves.step(held, None, index)
        if index < rounds - 1:
            held, _ = feed_halves.settle(moves, None)
    db1, _ = lax.optimization_barrier((db1, held))
    pairs = width // PAIR // 2
    operands = (info, q1, k1, v1, k1o, v1o, ctx1, log1)
    grads_early = self_backward(*operands, db1, w_middle, 0, pairs)
    moves[0][0][0] = after(moves[0][0][0], grads_early[0])
    held, _ = feed_halves.settle(moves, None)
    lines_feed = line_swaps(feed_halves.line_parts(held, None))
    held, rider = middle_halves.parts(after(keep, grads_early[0]), got)
    held = [dict(enumerate(pieces)) for pieces in held]
    moves = middle_halves.step(held, rider, 0)
    db1, _, _ = lax.optimization_barrier((db1, held, lines_feed[0]))
    grads_late = self_backward(*operands, db1, w_middle, pairs, pairs)
    moves[0][0][0] = after(moves[0][0][0], grads_late[0])
    held, rider = middle_halves.settle(moves, rider)
    for index in range(1, rounds):
        moves = middle_halves.step(held, rider, index)
        if index < rounds - 1:
            held, rider = middle_halves.settle(moves, rider)
    grad_feed = line_sum([after(lines_feed[0], grads_late[0])] + lines_feed[1:])
    grad_feed = grad_feed.reshape(2, -1, feed_in.shape[1])
    grads_late = list(grads_late)
    grads_late[0], _ = lax.optimization_barrier((grads_late[0], held))
    dw_self, inputs_back, sums_self = self_grads(
        info, inputs, inputs_other, grads_early, grads_late, w_self
    )
    sums_self = sums_self[:4]
    late_rows = sums_self.size // columns
    keep, send, self_halves = disperse(info, dw_self, (3,), sums_self)
    got = swap(send, 1, 0)
    inputs_got = hand_over(inputs_back, 1, -1)
    moves[0][0][0] = after(moves[0][0][0], send)
    held, rider = middle_halves.settle(moves, rider)
    lines_middle = line_swaps(middle_halves.line_parts(held, rider))
    grad_memory = memory_own + memory_got.astype(F32)
    held, rider = self_halves.parts(keep, got)
    grad_self, rider = direct_plane(held[0], rider)
    grad_middle = line_sum([after(lines_middle[0], grad_self)] + lines_middle[1:])
    lines_self = line_swaps(self_halves.line_parts([{0: grad_self}], rider))
    grad_inputs = input_grads(du1, grads_early[:3], grads_late[:3], w_self, inputs_got)
    grad_self = line_sum(lines_self)
    early = grad_middle[-early_rows:].reshape(-1, width)
    late_sums = grad_self[-late_rows:].reshape(-1, width)
    grad_middle = grad_middle[:-early_rows].reshape(5, -1, columns)
    grad_self = grad_self[:-late_rows].reshape(3, -1, columns)

    def mine(vector):
        count = vector.shape[0] // nt
        return lax.dynamic_slice_in_dim(vector, me_t * count, count)

    return (
        outputs,
        grad_inputs,
        grad_memory,
        grad_self[0],
        mine(late_sums[0]),
        grad_self[1],
        grad_self[2],
        mine(late_sums[1]),
        grad_middle[0].T,
        early[0],
        early[1],
        early[2],
        grad_middle[1],
        mine(early[9]),
        grad_middle[2],
        grad_middle[3],
        mine(early[10]),
        grad_middle[4].T,
        early[3],
        early[4],
        early[5],
        grad_feed[0],
        mine(early[11:15].reshape(-1)),
        grad_feed[1].T,
        early[6],
        early[7],
        early[8],
    )


def solution(mesh):
    placed = (
        P(("dp", "tensor"), None),
        P(("dp", "tensor"), None),
        P("dp"),
        P("dp", "tensor"),
        P("tensor"),
        P("dp", "tensor"),
        P("dp", "tensor"),
        P("tensor"),
        P("tensor", "dp"),
        P(),
        P(),
        P(),
        P("dp", "tensor"),
        P("tensor"),
        P("dp", "tensor"),
        P("dp", "tensor"),
        P("tensor"),
        P("tensor", "dp"),
        P(),
        P(),
        P(),
        P("dp", "tensor"),
        P("tensor"),
        P("tensor", "dp"),
        P(),
        P(),
        P(),
        P(("dp", "tensor"), None),
    )
    return jax.shard_map(
        on_device,
        mesh=mesh,
        in_specs=placed,
        out_specs=(
            P(("dp", "tensor"), None),
            P(("dp", "tensor"), None),
            P(("dp", "tensor"), None),
            P("dp", "tensor"),
            P("tensor"),
            P("dp", "tensor"),
            P("dp", "tensor"),
            P("tensor"),
            P("tensor", "dp"),
            P(),
            P(),
            P(),
            P("dp", "tensor"),
            P("tensor"),
            P("dp", "tensor"),
            P("dp", "tensor"),
            P("tensor"),
            P("tensor", "dp"),
            P(),
            P(),
            P(),
            P("dp", "tensor"),
            P("tensor"),
            P("tensor", "dp"),
            P(),
            P(),
            P(),
        ),
        check_vma=False,
    )
```

```python
import functools

import jax
import jax.numpy as jnp
from jax import lax
from jax.experimental import pallas as pl
from jax.experimental.pallas import tpu as pltpu
from jax.sharding import PartitionSpec as P

HD = 64
LEN = 1024
MEM = 256
PAIR = 128
BLOCK = 256
BACK_BLOCK = 512

EPSILON = 1e-05
MASKED = -1e30
SCALE = float(HD) ** (-0.5)

F32 = jnp.float32
BF16 = jnp.bfloat16
NN = (((1,), (0,)), ((), ()))
NT = (((1,), (1,)), ((), ()))
TN = (((0,), (0,)), ((), ()))
SMEM = pl.BlockSpec(memory_space=pltpu.SMEM)
ANY = pl.BlockSpec(memory_space=pl.ANY)
VMEM = pl.BlockSpec(memory_space=pltpu.VMEM)


def mm(left_side, right_side, dims):
    return lax.dot_general(left_side, right_side, dims, preferred_element_type=F32)


def shaped(shape, dtype):
    return jax.ShapeDtypeStruct(shape, dtype)


def cost(macs, moved):
    return pl.CostEstimate(flops=macs // 64, bytes_accessed=moved // 64, transcendentals=0)


def limit(mebibytes):
    return pltpu.CompilerParams(vmem_limit_bytes=mebibytes << 20)


def far(*arrays):
    return [pltpu.with_memory_space_constraint(array, pltpu.HBM) for array in arrays]


def swap(array, dp_mask, tensor_mask):
    nd, nt = lax.axis_size("dp"), lax.axis_size("tensor")
    pairs = [
        (d * nt + t, (d ^ dp_mask) * nt + (t ^ tensor_mask)) for d in range(nd) for t in range(nt)
    ]
    return lax.ppermute(array, ("dp", "tensor"), pairs)


def hand_over(array, parity, step):
    nd, nt = lax.axis_size("dp"), lax.axis_size("tensor")
    pairs = [(d * nt + t, d * nt + t + step) for d in range(nd) for t in range(parity, nt, 2)]
    return lax.ppermute(array, ("dp", "tensor"), pairs)


def tree_sum(terms):
    while len(terms) > 1:
        terms = [terms[i] + terms[i + 1] for i in range(0, len(terms), 2)]
    return terms[0]


def doubled(line, bits):
    for bit in bits:
        line = jnp.concatenate([line, swap(line, 0, bit)])
    return line


def over_planes(line):
    return [line] + [swap(line, 2 * j, 0) for j in range(1, lax.axis_size("dp") // 2)]


def both_cores(planes, *others):
    plane = jnp.stack([after(planes[0], *others)] + planes[1:])
    return plane, swap(plane, 1, 0)


class Halves:
    def __init__(self, groups, r, rider):
        self.planes, self.nt = lax.axis_size("dp") // 2, lax.axis_size("tensor")
        self.groups, self.r, self.rider = groups, r, rider
        self.rounds = self.planes.bit_length() - 1
        self.sizes = [self.nt * count * r for count in groups]
        self.bases = [self.planes * sum(self.sizes[:g]) for g in range(len(groups))]
        self.main = self.planes * sum(self.sizes)
        self.total = self.main + rider

    def bit(self, group, index):
        return 1 << (index if group % 2 == 0 else self.rounds - 1 - index)

    def place(self, i, j):
        group = 0
        while i >= self.groups[group]:
            i -= self.groups[group]
            group += 1
        bits = [self.bit(group, index) for index in range(self.rounds)]
        position = sum((j & b > 0) << (self.rounds - 1 - n) for n, b in enumerate(bits))
        count = self.groups[group]
        return self.bases[group] + position * self.sizes[group] + i * self.r, count * self.r

    def split(self, arrays, held, rider, index):
        stay, sent = [], []
        for group, terms in enumerate(held):
            rows = (self.planes >> (index + 1)) * self.sizes[group]
            stay.append([(rows, terms)])
            sent.append([(rows, [(array, lo + rows) for array, lo in terms])])
        if self.rider:
            sent[-1].append((self.rider, rider))
        return stay + sent

    def line(self, held, rider):
        plans = []
        for k in range(self.nt):
            plan = []
            for group, terms in enumerate(held):
                rows = self.groups[group] * self.r
                plan.append((rows, [(array, lo + k * rows) for array, lo in terms]))
            if self.rider:
                plan.append((self.rider, rider))
            plans.append(plan)
        return plans


def add_rows_kernel(*refs, plans, count):
    for out, plan in zip(refs[count:], plans):
        at = 0
        for rows, terms in plan:
            total = tree_sum([refs[i][lo : lo + rows, :].astype(F32) for i, lo in terms])
            out[at : at + rows, :] = total.astype(out.dtype)
            at += rows


def add_rows(arrays, plans, dtype=BF16):
    width = arrays[0].shape[1]
    moved = sum(array.size * array.dtype.itemsize for array in arrays)
    return pl.pallas_call(
        functools.partial(add_rows_kernel, plans=plans, count=len(arrays)),
        out_shape=tuple(shaped((sum(n for n, _ in plan), width), dtype) for plan in plans),
        in_specs=[VMEM] * len(arrays),
        out_specs=(VMEM,) * len(plans),
        compiler_params=limit(20),
        cost_estimate=cost(0, 2 * moved),
    )(*arrays)


def halve(halves, arrays, held, rider, index):
    groups = len(halves.groups)
    outs = list(add_rows(arrays, halves.split(arrays, held, rider, index)))
    stay, sent = outs[:groups], outs[groups:]
    got = [swap(part, 2 * halves.bit(group, index), 0) for group, part in enumerate(sent)]
    held = [[(group, 0), (groups + group, 0)] for group in range(groups)]
    end = sent[-1].shape[0] - halves.rider
    rider = [(2 * groups, end), (2 * groups - 1, end)]
    return stay + got + sent[-1:], held, rider


def line_swaps(parts):
    return [parts[0]] + [swap(part, 0, k) for k, part in enumerate(parts) if k]


def after(array, *others):
    return lax.optimization_barrier((array,) + others)[0]


def slot_blocks(info, planes, nt):
    for j in range(planes):
        for c in range(2):
            d = jnp.bitwise_xor(info[2], 2 * j + c)
            for s in range(nt):
                yield j, c, s, d, jnp.bitwise_xor(info[3], s)


def aligned(r, w):
    return w % PAIR == 0 and r % 16 == 0


def assemble_kernel(info, *refs, planes):
    whole = refs[-1]
    nt, n, r, w = refs[0].shape[-4:]
    for j, c, s, d, t in slot_blocks(info, planes, nt):
        rows = pl.ds(pl.multiple_of(d * r, r), r)
        columns = pl.ds(pl.multiple_of(t * w, w), w)
        piece = refs[c].at[j] if len(refs) == 3 else refs[c * planes + j]
        for i in range(n):
            whole[i, rows, columns] = piece[s, i]


def assemble(info, halves):
    nt, n, r, w = halves[0].shape[-4:]
    planes = lax.axis_size("dp") // 2
    nd = 2 * planes
    if aligned(r, w):
        return pl.pallas_call(
            functools.partial(assemble_kernel, planes=planes),
            out_shape=shaped((n, nd * r, nt * w), BF16),
            in_specs=[SMEM] + [VMEM] * len(halves),
            out_specs=VMEM,
            compiler_params=limit(18),
            cost_estimate=cost(0, 8 * nd * nt * n * r * w),
        )(info, *halves)
    full = jnp.stack(halves).reshape(2, planes, nt, n, r, w).swapaxes(0, 1)
    full = full.reshape(nd, nt, n, r, w)
    full = jnp.take(full, jnp.bitwise_xor(jnp.arange(nd), info[2]), axis=0)
    full = jnp.take(full, jnp.bitwise_xor(jnp.arange(nt), info[3]), axis=1)
    return full.transpose(2, 0, 3, 1, 4).reshape(n, nd * r, nt * w)


def disperse(info, halves, scratch, i, t, s, keep, send):
    for j in range(halves.planes):
        base, stride = halves.place(i, j)
        lo = base + s * stride
        if not isinstance(s, int):
            lo = pl.multiple_of(lo, 16)
        for c in range(2):
            d = jnp.bitwise_xor(info[2], 2 * j + c)
            rows = pl.ds(pl.multiple_of(d * halves.r, halves.r), halves.r)
            (keep, send)[c][pl.ds(lo, halves.r), :] = scratch[rows, t]


def disperse_whole(info, halves, scratch, i, keep, send):
    w = keep.shape[1]
    for s in range(halves.nt):
        t = jnp.bitwise_xor(info[3], s)
        disperse(info, halves, scratch, i, pl.ds(pl.multiple_of(t * w, w), w), s, keep, send)


def disperse_plain(info, halves, whole, rider):
    nd, nt = 2 * halves.planes, halves.nt
    n, r, w = whole.shape[0], halves.r, whole.shape[2] // nt
    full = whole.reshape(n, nd, r, nt, w).transpose(1, 3, 0, 2, 4)
    full = jnp.take(full, jnp.bitwise_xor(jnp.arange(nd), info[2]), axis=0)
    full = jnp.take(full, jnp.bitwise_xor(jnp.arange(nt), info[3]), axis=1)
    full = full.reshape(nd // 2, 2, nt, n, r, w)
    flats = []
    for c in range(2):
        rows, first = [], 0
        for count in halves.groups:
            order = sorted(range(halves.planes), key=lambda j: halves.place(first, j)[0])
            group = jnp.stack([full[j, c, :, first : first + count] for j in order])
            rows.append(group.reshape(-1, w))
            first += count
        flats.append(jnp.concatenate(rows + [rider]))
    return flats


def pack_kernel(*refs, blocks):
    out = refs[-1]
    r, w = refs[0].shape
    for i, block in enumerate(refs[:blocks]):
        out[i * r : (i + 1) * r, :] = block[...]
    row = lax.broadcasted_iota(jnp.int32, (16, w), 0)
    filled = jnp.zeros((16, w), F32)
    count = 0
    for vector in refs[blocks:-1]:
        for i in range(vector.shape[0]):
            filled = jnp.where(row == count, vector[i : i + 1, :].astype(F32), filled)
            count += 1
    out[blocks * r :, :] = filled.astype(BF16)


def pack(blocks, vectors):
    r, w = blocks[0].shape
    if aligned(r, w):
        return pl.pallas_call(
            functools.partial(pack_kernel, blocks=len(blocks)),
            out_shape=shaped((len(blocks) * r + 16, w), BF16),
            in_specs=[VMEM] * (len(blocks) + len(vectors)),
            out_specs=VMEM,
            cost_estimate=cost(0, 32 * r * w),
        )(*blocks, *[vector.reshape(-1, w) for vector in vectors])
    rows = jnp.concatenate(vectors).reshape(-1, w)
    return jnp.concatenate(list(blocks) + [jnp.pad(rows, ((0, 16 - rows.shape[0]), (0, 0)))])


def spread_kernel(info, riders, small, hidden):
    nt, _, w = riders.shape
    for s in range(nt):
        t = jnp.bitwise_xor(info[3], s)
        block = riders[s].astype(F32)
        small[:, pl.ds(pl.multiple_of(t * w, w), w)] = block
        for i in range(4):
            hidden[:, pl.ds(pl.multiple_of((4 * t + i) * w, w), w)] = block[4 + i : 5 + i]


def spread(info, riders):
    nt, _, w = riders.shape
    if aligned(16, w):
        return pl.pallas_call(
            spread_kernel,
            out_shape=(shaped((16, nt * w), F32), shaped((1, 4 * nt * w), F32)),
            in_specs=[SMEM, VMEM],
            out_specs=(VMEM, VMEM),
            cost_estimate=cost(0, 64 * nt * w),
        )(info, riders)
    full = jnp.take(riders, jnp.bitwise_xor(jnp.arange(nt), info[3]), axis=0).astype(F32)
    return full.transpose(1, 0, 2).reshape(16, nt * w), full[:, 4:8].reshape(1, -1)


def norm_forward(summed):
    row_mean = jnp.mean(summed, axis=-1, keepdims=True)
    centred = summed - row_mean
    variance = jnp.mean(centred * centred, axis=-1, keepdims=True)
    inverse = lax.rsqrt(variance + EPSILON)
    return centred * inverse, inverse


def norm_backward(grad_out, normed, inverse, norm_gain):
    grad_normed = grad_out * norm_gain
    return inverse * (
        grad_normed
        - jnp.mean(grad_normed, axis=-1, keepdims=True)
        - normed * jnp.mean(grad_normed * normed, axis=-1, keepdims=True)
    )


def column_sum(values):
    return jnp.sum(values.astype(F32), axis=0, keepdims=True)


def head_lanes(e):
    lane = lax.broadcasted_iota(jnp.int32, (1, PAIR), 1)
    chosen = (lane < HD) if e == 0 else (lane >= HD)
    return jnp.where(chosen, 1.0, 0.0)


def join_heads(first, second):
    lane = lax.broadcasted_iota(jnp.int32, first.shape, 1)
    return jnp.where(lane < HD, first, second)


def attend_forward(q, segments, contexts, logs, lo):
    rows = slice(lo, lo + BLOCK)
    results = []
    for e in range(2):
        query = q[rows, :] * head_lanes(e).astype(BF16)
        scores = [edit(mm(query, k, NT)) for k, _, edit in segments]
        peak = functools.reduce(
            jnp.maximum, [jnp.max(piece, axis=-1, keepdims=True) for piece in scores]
        )
        total = None
        for piece, (_, v, _) in zip(scores, segments):
            weights = jnp.exp(piece - peak).astype(BF16)
            wide = jnp.concatenate([v, jnp.ones(v.shape, BF16)], axis=1)
            part = mm(weights, wide, NN)
            total = part if total is None else total + part
        row_total = total[:, PAIR:]
        results.append((total[:, :PAIR] / row_total, peak + jnp.log(row_total)))
    contexts[rows, :] = join_heads(results[0][0], results[1][0]).astype(BF16)
    logs[rows, :] = join_heads(results[0][1], results[1][1])


def attend_backward(q, grad, ctx, logs, segments, grad_query, lo):
    rows = slice(lo, lo + BACK_BLOCK)
    grad_rows = grad[rows, :]
    product = grad_rows.astype(F32) * ctx[rows, :].astype(F32)
    query_rows = q[rows, :]
    query_turned = jnp.transpose(query_rows)
    grad_turned = jnp.transpose(grad_rows)
    total = None
    for e in range(2):
        lanes = head_lanes(e)
        low_lanes = lanes.astype(BF16)
        delta = jnp.sum(product * lanes, axis=-1, keepdims=True)
        row_log = logs[rows, e * HD : e * HD + 1]
        grad_low = grad_rows * low_lanes
        query = query_rows * low_lanes
        for k, v, edit, add in segments:
            weights = jnp.exp(edit(mm(query, k, NT)) - row_log)
            slope = mm(grad_low, v, NT) - delta
            grad_scores = (weights * slope).astype(BF16)
            part = mm(grad_scores, k * low_lanes, NN)
            total = part if total is None else total + part
            head = slice(e * HD, e * HD + HD)
            add(
                head,
                mm(query_turned[head], grad_scores, NN),
                mm(grad_turned[head], weights.astype(BF16), NN),
            )
    grad_query[rows, :] = (total * SCALE).astype(BF16)


def same(scores):
    return scores


def masked(lo, col_lo, prefix_len):
    def edit(scores):
        row = lo + lax.broadcasted_iota(jnp.int32, scores.shape, 0)
        col = col_lo + lax.broadcasted_iota(jnp.int32, scores.shape, 1)
        allowed = col <= row
        if prefix_len is not None:
            allowed = allowed | (col < prefix_len)
        return jnp.where(allowed, scores, MASKED)

    return edit


def adder(keys, values, col_lo, width):
    def add(head, part_keys, part_values):
        keys[head, col_lo : col_lo + width] += part_keys
        values[head, col_lo : col_lo + width] += part_values

    return add


def self_forward_kernel(info, q, k, v, ko, vo, ctx, logs):
    tokens = q.shape[0]

    @pl.when(info[0] == 0)
    def _():
        for lo in range(0, tokens, BLOCK):
            attend_forward(q, [(k[...], v[...], masked(lo, 0, info[1]))], ctx, logs, lo)

    @pl.when(info[0] != 0)
    def _():
        for lo in range(0, tokens, BLOCK):
            near = slice(lo, lo + BLOCK)
            segments = [(ko[...], vo[...], same)]
            if lo:
                segments.append((k[:lo, :], v[:lo, :], same))
            segments.append((k[near, :], v[near, :], masked(lo, lo, None)))
            attend_forward(q, segments, ctx, logs, lo)


def self_backward_kernel(
    info, q, k, v, ko, vo, ctx, logs, low, w, dq, dk, dv, dko, dvo, ak, av, ako, avo, grad
):
    tokens = q.shape[0]
    ak[...] = jnp.zeros_like(ak)
    av[...] = jnp.zeros_like(av)
    grad[...] = mm(low[...], w[0], NN).astype(BF16)

    @pl.when(info[0] == 0)
    def _():
        for lo in range(0, tokens, BACK_BLOCK):
            segments = [(k[...], v[...], masked(lo, 0, info[1]), adder(ak, av, 0, tokens))]
            attend_backward(q, grad, ctx, logs, segments, dq, lo)

    @pl.when(info[0] != 0)
    def _():
        ako[...] = jnp.zeros_like(ako)
        avo[...] = jnp.zeros_like(avo)
        for lo in range(0, tokens, BACK_BLOCK):
            near = slice(lo, lo + BACK_BLOCK)
            segments = [(ko[...], vo[...], same, adder(ako, avo, 0, tokens))]
            if lo:
                segments.append((k[:lo, :], v[:lo, :], same, adder(ak, av, 0, lo)))
            segments.append(
                (k[near, :], v[near, :], masked(lo, lo, None), adder(ak, av, lo, BACK_BLOCK))
            )
            attend_backward(q, grad, ctx, logs, segments, dq, lo)
        dko[...] = jnp.transpose(ako[...]).astype(BF16)
        dvo[...] = jnp.transpose(avo[...]).astype(BF16)

    dk[...] = jnp.transpose(ak[...]).astype(BF16)
    dv[...] = jnp.transpose(av[...]).astype(BF16)


def cross_forward_kernel(q, k, v, ctx, logs):
    for lo in range(0, q.shape[0], BLOCK):
        attend_forward(q, [(k[...], v[...], same)], ctx, logs, lo)


def cross_backward_kernel(q, k, v, ctx, logs, low, w, dq, dk, dv, ak, av, grad):
    ak[...] = jnp.zeros_like(ak)
    av[...] = jnp.zeros_like(av)
    grad[...] = mm(low[...], w[0], NN).astype(BF16)
    for lo in range(0, q.shape[0], BACK_BLOCK):
        segments = [(k[...], v[...], same, adder(ak, av, 0, k.shape[0]))]
        attend_backward(q, grad, ctx, logs, segments, dq, lo)
    dk[...] = jnp.transpose(ak[...]).astype(BF16)
    dv[...] = jnp.transpose(av[...]).astype(BF16)


def lanes_of(rows, first=0):
    return pl.BlockSpec((rows, PAIR), lambda h: (0, first + h))


def output_columns(slot, width, first=0):
    return pl.BlockSpec((1, width, PAIR), lambda h: (slot, 0, first + h))


def self_forward(info, q, k, v, ko, vo):
    tokens, width = q.shape
    row = lanes_of(tokens)
    return pl.pallas_call(
        self_forward_kernel,
        grid=(width // PAIR,),
        out_shape=(shaped((tokens, width), BF16), shaped((tokens, width), F32)),
        in_specs=[SMEM] + [row] * 5,
        out_specs=(row, row),
        compiler_params=limit(16),
        cost_estimate=cost(width // HD * tokens * tokens * 2 * 256 * 2, 5 << 20),
    )(info, q, k, v, ko, vo)


def self_backward(info, q, k, v, ko, vo, ctx, logs, low, w, first, pairs):
    tokens, width = q.shape
    row = lanes_of(tokens, first)
    out = shaped((tokens, pairs * PAIR), BF16)
    return pl.pallas_call(
        self_backward_kernel,
        grid=(pairs,),
        out_shape=(out,) * 5,
        in_specs=[SMEM] + [row] * 7 + [VMEM, output_columns(3, width, first)],
        out_specs=(lanes_of(tokens),) * 5,
        scratch_shapes=[pltpu.VMEM((PAIR, tokens), F32)] * 4 + [pltpu.VMEM((tokens, PAIR), BF16)],
        compiler_params=limit(16),
        cost_estimate=cost(width // HD * tokens * tokens * 256 * 5, 8 << 20),
    )(info, *far(q, k, v, ko, vo, ctx, logs), low, *far(w))


def cross_forward(q, k, v):
    tokens, width = q.shape
    rows = k.shape[0]
    return pl.pallas_call(
        cross_forward_kernel,
        grid=(width // PAIR,),
        out_shape=(shaped((tokens, width), BF16), shaped((tokens, width), F32)),
        in_specs=[lanes_of(tokens), lanes_of(rows), lanes_of(rows)],
        out_specs=(lanes_of(tokens), lanes_of(tokens)),
        compiler_params=limit(16),
        cost_estimate=cost(width // HD * tokens * rows * 256 * 2, 3 << 20),
    )(q, k, v)


def cross_backward(q, k, v, ctx, logs, low, w):
    tokens, width = q.shape
    rows = k.shape[0]
    small = shaped((rows, width), BF16)
    return pl.pallas_call(
        cross_backward_kernel,
        grid=(width // PAIR,),
        out_shape=(shaped((tokens, width), BF16), small, small),
        in_specs=[lanes_of(tokens), lanes_of(rows), lanes_of(rows)]
        + [lanes_of(tokens)] * 2
        + [VMEM, output_columns(7, width)],
        out_specs=(lanes_of(tokens), lanes_of(rows), lanes_of(rows)),
        scratch_shapes=[pltpu.VMEM((PAIR, rows), F32)] * 2 + [pltpu.VMEM((tokens, PAIR), BF16)],
        compiler_params=limit(16),
        cost_estimate=cost(width // HD * tokens * rows * 256 * 5, 4 << 20),
    )(*far(q, k, v, ctx, logs), low, *far(w))


def project_self_kernel(info, x, xo, wq, wk, wv, b, q, k, v, ko, vo):
    rows = x[...]
    q[...] = (mm(rows, wq[0], NN) + b[0:1, :]).astype(BF16) * jnp.asarray(SCALE, BF16)
    k[...] = mm(rows, wk[0], NN).astype(BF16)
    v[...] = (mm(rows, wv[0], NN) + b[1:2, :]).astype(BF16)

    @pl.when(info[0] != 0)
    def _():
        other = xo[...]
        ko[...] = mm(other, wk[0], NN).astype(BF16)
        vo[...] = (mm(other, wv[0], NN) + b[1:2, :]).astype(BF16)


def project_self(info, x, xo, w, b):
    low = shaped(x.shape, BF16)
    return pl.pallas_call(
        project_self_kernel,
        grid=(1,),
        out_shape=(low,) * 5,
        in_specs=[SMEM] + [VMEM] * 2 + [matrix(i, x.shape[1]) for i in range(3)] + [VMEM],
        compiler_params=limit(16),
        cost_estimate=cost(5 * x.size * x.shape[1], 5 << 20),
    )(info, x, xo, w, w, w, b)


def first_norm_kernel(
    ctx, x, mem, memo, wo, wq, wk, wv, ob, gain, bias, b, first, normed, inverse, q, k, v
):
    summed = x[...].astype(F32) + mm(ctx[...], wo[0], NT) + ob[...].astype(F32)
    n, r = norm_forward(summed)
    out = n * gain[...].astype(F32) + bias[...].astype(F32)
    normed[...] = n
    inverse[...] = r
    first[...] = out
    q[...] = (mm(out.astype(BF16), wq[0], NN) + b[2:3, :]).astype(BF16) * jnp.asarray(SCALE, BF16)
    rows = mem.shape[0]
    for source, lo in ((mem, 0), (memo, rows)):
        k[lo : lo + rows, :] = mm(source[...], wk[0], NN).astype(BF16)
        v[lo : lo + rows, :] = (mm(source[...], wv[0], NN) + b[3:4, :]).astype(BF16)


def first_norm(ctx, x, mem, memo, w, ob, gain, bias, b):
    rows = 2 * mem.shape[0]
    tokens, width = x.shape
    full = shaped(x.shape, F32)
    return pl.pallas_call(
        first_norm_kernel,
        grid=(1,),
        out_shape=(
            full,
            full,
            shaped((tokens, 1), F32),
            shaped(x.shape, BF16),
            shaped((rows, width), BF16),
            shaped((rows, width), BF16),
        ),
        in_specs=[VMEM] * 4 + [matrix(i, width) for i in range(3, 7)] + [VMEM] * 4,
        compiler_params=limit(16),
        cost_estimate=cost(3 * x.size * width, 8 << 20),
    )(ctx, x, mem, memo, w, w, w, w, ob, gain, bias, b)


def feed_kernel(
    info,
    ctx,
    first,
    cot,
    wo,
    wf,
    ob,
    gain2,
    bias2,
    fib,
    fob,
    gain3,
    bias3,
    out,
    keep,
    send,
    du2,
    db2,
    sums,
    hsum,
    act,
    slope,
    acc,
    second,
    turn,
    *,
    halves,
):
    tokens, width = first.shape
    w = keep.shape[1]
    summed = first[...] + mm(ctx[...], wo[0], NT) + ob[...].astype(F32)
    n2, r2 = norm_forward(summed)
    out2 = n2 * gain2[...].astype(F32) + bias2[...].astype(F32)
    second[...] = out2.astype(BF16)
    acc[...] = out2 + fob[...].astype(F32)

    @pl.loop(0, halves.nt, unroll=2)
    def _(t):
        cols = pl.ds(pl.multiple_of(t * w, w), w)
        hidden = mm(second[...], wf[0, :, cols], NN) + fib[:, cols]
        gate = 1.0 / (1.0 + jnp.exp(-hidden))
        active = (hidden * gate).astype(BF16)
        act[:, cols] = active
        slope[:, cols] = (gate * (1.0 + hidden * (1.0 - gate))).astype(BF16)
        acc[...] += mm(active, wf[1, :, cols], NT)

    n3, r3 = norm_forward(acc[...])
    out[...] = (n3 * gain3[...].astype(F32) + bias3[...].astype(F32)).astype(BF16)
    dy = cot[...].astype(F32)
    du3 = norm_backward(dy, n3, r3, gain3[...].astype(F32))
    db3 = du3.astype(BF16)
    sums[3:4, :] = column_sum(db3)
    sums[4:5, :] = column_sum(dy * n3)
    sums[5:6, :] = column_sum(dy)
    acc[...] = du3
    db2[...] = db3

    @pl.loop(0, halves.nt, unroll=2)
    def _(t):
        cols = pl.ds(pl.multiple_of(t * w, w), w)
        s = jnp.bitwise_xor(info[3], t)
        everything = slice(None)
        back = db2[...]
        dact = mm(back, wf[1, :, cols], NN)
        dhid = (dact * slope[:, cols].astype(F32)).astype(BF16)
        hsum[:, cols] = column_sum(dhid)
        turn[0] = mm(second[...], dhid, TN).astype(BF16)
        disperse(info, halves, turn.at[0], 0, everything, s, keep, send)
        turn[1] = mm(back, act[:, cols], TN).astype(BF16)
        disperse(info, halves, turn.at[1], 1, everything, s, keep, send)
        acc[...] += mm(dhid, wf[0, :, cols], NT)

    dsecond = acc[...]
    grad2 = norm_backward(dsecond, n2, r2, gain2[...].astype(F32))
    low2 = grad2.astype(BF16)
    du2[...] = grad2
    db2[...] = low2
    sums[0:1, :] = column_sum(low2)
    sums[1:2, :] = column_sum(dsecond * n2)
    sums[2:3, :] = column_sum(dsecond)
    sums[6:8, :] = jnp.zeros((2, width), F32)


def matrix(slot, width):
    return pl.BlockSpec((1, width, width), lambda h: (slot, 0, 0))


def feed(info, halves, ctx, first, cot, wo, wf, ob, gain2, bias2, fib, fob, gain3, bias3):
    tokens, width = first.shape
    wide = wf.shape[2]
    w = wide // halves.nt
    flat = shaped((halves.total, w), BF16)
    return pl.pallas_call(
        functools.partial(feed_kernel, halves=halves),
        grid=(1,),
        out_shape=(
            shaped(first.shape, BF16),
            flat,
            flat,
            shaped(first.shape, F32),
            shaped(first.shape, BF16),
            shaped((8, width), F32),
            shaped((1, wide), F32),
        ),
        in_specs=[SMEM] + [VMEM] * 3 + [matrix(7, width)] + [VMEM] * 8,
        scratch_shapes=[
            pltpu.VMEM((tokens, wide), BF16),
            pltpu.VMEM((tokens, wide), BF16),
            pltpu.VMEM((tokens, width), F32),
            pltpu.VMEM((tokens, width), BF16),
            pltpu.VMEM((2, width, w), BF16),
        ],
        compiler_params=limit(28),
        cost_estimate=cost(6 * tokens * width * wide, 14 << 20),
    )(info, ctx, first, cot, wo, wf, ob, gain2, bias2, fib, fob, gain3, bias3)


def middle_kernel(
    info,
    du2,
    dq2,
    dk2,
    dv2,
    db2,
    sums2,
    hsum,
    normed,
    inverse,
    first,
    mem,
    memo,
    ctx2,
    ctx1,
    wq,
    wk,
    wv,
    gain,
    *outs,
    halves,
):
    du1, db1, own, other = outs[:4]
    turn, riders = outs[-2:]
    rows, width = mem.shape
    dfirst = du2[...] + mm(dq2[...], wq[0], NT)
    n = normed[...]
    grad = norm_backward(dfirst, n, inverse[...], gain[...].astype(F32))
    low = grad.astype(BF16)
    du1[...] = grad
    db1[...] = low
    riders[0:1, :] = column_sum(low)
    riders[1:2, :] = column_sum(dfirst * n)
    riders[2:3, :] = column_sum(dfirst)
    riders[3:9, :] = sums2[0:6, :]
    riders[9:10, :] = column_sum(dq2[...])
    riders[10:11, :] = column_sum(dv2[...])
    for i in range(4):
        riders[11 + i : 12 + i, :] = hsum[:, i * width : (i + 1) * width]
    riders[15:16, :] = jnp.zeros((1, width), F32)
    turn[0] = mm(low, ctx1[...], TN).astype(BF16)
    turn[1] = mm(first[...].astype(BF16), dq2[...], TN).astype(BF16)
    for slot, part in ((2, dk2), (3, dv2)):
        turn[slot] = (
            mm(mem[...], part[:rows, :], TN) + mm(memo[...], part[rows:, :], TN)
        ).astype(BF16)
    turn[4] = mm(db2[...], ctx2[...], TN).astype(BF16)
    back = mm(dk2[...], wk[0], NT) + mm(dv2[...], wv[0], NT)
    own[...] = back[:rows, :]
    other[...] = back[rows:, :].astype(BF16)
    if halves is None:
        outs[4][...] = turn[...]
        outs[5][...] = riders[...]
        return
    for i in range(5):
        disperse_whole(info, halves, turn.at[i], i, outs[4], outs[5])
    w = outs[4].shape[1]
    for target in outs[4:6]:
        for q in range(width // w):
            lo = halves.main + 16 * q
            target[lo : lo + 16, :] = riders[:, q * w : q * w + w].astype(BF16)


def middle(info, du2, dq2, dk2, dv2, db2, sums2, hsum, normed, inverse, first, mem, memo, ctx2, ctx1, w, gain):
    tokens, width = first.shape
    rows = mem.shape[0]
    nd, nt = lax.axis_size("dp"), lax.axis_size("tensor")
    r, columns = width // nd, width // nt
    halves = Halves((3, 2), r, 16 * nt)
    direct = aligned(r, columns)
    if direct:
        last = (shaped((halves.total, columns), BF16),) * 2
    else:
        last = (shaped((5, width, width), BF16), shaped((16, width), F32))
    outs = pl.pallas_call(
        functools.partial(middle_kernel, halves=halves if direct else None),
        grid=(1,),
        out_shape=(
            shaped(first.shape, F32),
            shaped(first.shape, BF16),
            shaped((rows, width), F32),
            shaped((rows, width), BF16),
        )
        + last,
        in_specs=[SMEM] + [VMEM] * 14 + [matrix(i, width) for i in (4, 5, 6)] + [VMEM],
        scratch_shapes=[pltpu.VMEM((5, width, width), BF16), pltpu.VMEM((16, width), F32)],
        compiler_params=limit(20),
        cost_estimate=cost(6 * first.size * width, 12 << 20),
    )(
        info,
        *(du2, dq2, dk2, dv2, db2, sums2, hsum),
        *far(normed, inverse, first, mem, memo, ctx2, ctx1, w, w, w),
        gain,
    )
    if not direct:
        rider = outs[5].astype(BF16).reshape(16, nt, columns).transpose(1, 0, 2)
        outs = outs[:4] + tuple(disperse_plain(info, halves, outs[4], rider.reshape(-1, columns)))
    return halves, outs


def self_grads_kernel(
    info, x, xo, dqa, dka, dva, dkoa, dvoa, dqb, dkb, dvb, dkob, dvob, wk, wv, *outs, halves
):
    other = outs[0]
    turn, sums = outs[-2:]
    width = x.shape[1]
    both = lambda left, right: jnp.concatenate([left[...], right[...]], axis=1)
    dq, dk, dv = both(dqa, dqb), both(dka, dkb), both(dva, dvb)
    turn[0] = mm(x[...], dq, TN).astype(BF16)
    sums[0:1, :] = column_sum(dq)

    @pl.when(info[0] == 0)
    def _():
        turn[1] = mm(x[...], dk, TN).astype(BF16)
        turn[2] = mm(x[...], dv, TN).astype(BF16)
        sums[1:2, :] = column_sum(dv)
        other[...] = jnp.zeros_like(other)

    @pl.when(info[0] != 0)
    def _():
        dko, dvo = both(dkoa, dkob), both(dvoa, dvob)
        turn[1] = (mm(x[...], dk, TN) + mm(xo[...], dko, TN)).astype(BF16)
        turn[2] = (mm(x[...], dv, TN) + mm(xo[...], dvo, TN)).astype(BF16)
        sums[1:2, :] = column_sum(dv) + column_sum(dvo)
        other[...] = (mm(dko, wk[0], NT) + mm(dvo, wv[0], NT)).astype(BF16)

    if halves is None:
        outs[1][...] = turn[...]
        outs[2][...] = sums[...]
        return
    for i in range(3):
        disperse_whole(info, halves, turn.at[i], i, outs[1], outs[2])
    w = outs[1].shape[1]
    row = lax.broadcasted_iota(jnp.int32, (16, w), 0)
    filled = jnp.zeros((16, w), F32)
    for i in range(2):
        for t in range(width // w):
            piece = sums[i : i + 1, t * w : t * w + w]
            filled = jnp.where(row == i * (width // w) + t, piece, filled)
    for target in outs[1:3]:
        target[halves.main :, :] = filled.astype(BF16)


def self_grads(info, x, xo, early, late, w):
    width = x.shape[1]
    nd, nt = lax.axis_size("dp"), lax.axis_size("tensor")
    r, columns = width // nd, width // nt
    halves = Halves((3,), r, 16)
    direct = aligned(r, columns)
    if direct:
        last = (shaped((halves.total, columns), BF16),) * 2
    else:
        last = (shaped((3, width, width), BF16), shaped((8, width), F32))
    outs = pl.pallas_call(
        functools.partial(self_grads_kernel, halves=halves if direct else None),
        grid=(1,),
        out_shape=(shaped(x.shape, BF16),) + last,
        in_specs=[SMEM] + [VMEM] * 12 + [matrix(i, width) for i in (1, 2)],
        scratch_shapes=[pltpu.VMEM((3, width, width), BF16), pltpu.VMEM((8, width), F32)],
        compiler_params=limit(16),
        cost_estimate=cost(7 * x.size * width, 8 << 20),
    )(info, *far(x, xo), *early, *late, *far(w, w))
    if not direct:
        rider = outs[2][:2].astype(BF16).reshape(-1, columns)
        rider = jnp.pad(rider, ((0, 16 - rider.shape[0]), (0, 0)))
        outs = outs[:1] + tuple(disperse_plain(info, halves, outs[1], rider))
    return halves, outs


def input_grads_kernel(du1, dqa, dka, dva, dqb, dkb, dvb, wq, wk, wv, back, out):
    both = lambda left, right: jnp.concatenate([left[...], right[...]], axis=1)
    out[...] = (
        du1[...]
        + mm(both(dqa, dqb), wq[0], NT)
        + mm(both(dka, dkb), wk[0], NT)
        + mm(both(dva, dvb), wv[0], NT)
        + back[...].astype(F32)
    )


def input_grads(du1, early, late, w, back):
    return pl.pallas_call(
        input_grads_kernel,
        grid=(1,),
        out_shape=shaped(du1.shape, F32),
        in_specs=[VMEM] * 7 + [matrix(i, du1.shape[1]) for i in range(3)] + [VMEM],
        compiler_params=limit(16),
        cost_estimate=cost(3 * du1.size * du1.shape[1], 6 << 20),
    )(*far(du1), *early, *late, *far(w, w, w), back)


def on_device(
    inputs,
    memory,
    prefix,
    self_query,
    self_query_bias,
    self_key,
    self_value,
    self_value_bias,
    self_out,
    self_out_bias,
    self_norm_gain,
    self_norm_bias,
    cross_query,
    cross_query_bias,
    cross_key,
    cross_value,
    cross_value_bias,
    cross_out,
    cross_out_bias,
    cross_norm_gain,
    cross_norm_bias,
    feed_in,
    feed_in_bias,
    feed_out,
    feed_out_bias,
    feed_norm_gain,
    feed_norm_bias,
    cotangent,
):
    nd, nt = lax.axis_size("dp"), lax.axis_size("tensor")
    me_d, me_t = lax.axis_index("dp"), lax.axis_index("tensor")
    late = me_t % 2
    width = inputs.shape[1]
    assert LEN == 2 * inputs.shape[0] and MEM == 2 * memory.shape[0]
    assert nd & (nd - 1) == 0 and nt & (nt - 1) == 0
    prefix_here = jnp.where(late == 0, lax.dynamic_index_in_dim(prefix, me_t // 2, keepdims=False), 0)
    info = jnp.stack([late, prefix_here, me_d, me_t]).astype(jnp.int32)

    columns = self_query_bias.shape[0]
    row = lambda vector: vector.reshape(1, -1)
    packed = pack(
        (
            self_query,
            self_key,
            self_value,
            self_out.T,
            cross_query,
            cross_key,
            cross_value,
            cross_out.T,
        ),
        (self_query_bias, self_value_bias, cross_query_bias, cross_value_bias, feed_in_bias),
    )
    feed_shard = jnp.stack([feed_in, feed_out.T])

    bits = [1 << i for i in range(nt.bit_length() - 1)]
    swapped = [swap(packed, 0, k) for k in range(1, nt)]
    line_feed = doubled(after(feed_shard, packed)[None], bits[:1])
    line = jnp.stack([after(packed, line_feed)] + swapped)
    count = 8 * self_query.shape[0]
    riders = line[:, count:]
    line = line[:, :count].reshape((nt, 8) + self_query.shape)
    line_feed = doubled(after(line_feed, line), bits[1:])
    inputs_other = hand_over(after(inputs, line), 0, 1)
    memory_other = swap(after(memory, line_feed), 0, 1)
    head_biases, hidden_bias = spread(info, riders)
    group = both_cores(over_planes(line), inputs_other, memory_other, head_biases)
    line_feed = after(line_feed, group[0])
    planes_feed = over_planes(line_feed)

    weights = assemble(info, group)
    q1, k1, v1, k1o, v1o = project_self(info, inputs, inputs_other, weights, head_biases)
    ctx1, log1 = self_forward(info, q1, k1, v1, k1o, v1o)
    first, normed1, inverse1, q2, k2, v2 = first_norm(
        ctx1,
        inputs,
        memory,
        memory_other,
        weights,
        row(self_out_bias),
        row(self_norm_gain),
        row(self_norm_bias),
        head_biases,
    )
    ctx2, log2 = cross_forward(q2, k2, v2)
    own = [planes_feed[0]] + [after(piece, ctx2) for piece in planes_feed[1:]]
    w_feed = assemble(info, planes_feed + [swap(piece, 1, 0) for piece in own])
    feed_halves = Halves((1, 1), width // nd, 0)
    outputs, keep, send, du2, db2, sums_feed, sums_hidden = feed(
        info,
        feed_halves,
        ctx2,
        first,
        cotangent,
        weights,
        w_feed,
        row(cross_out_bias),
        row(cross_norm_gain),
        row(cross_norm_bias),
        hidden_bias,
        row(feed_out_bias),
        row(feed_norm_gain),
        row(feed_norm_bias),
    )
    rounds = feed_halves.rounds
    got = swap(send, 1, 0)
    dq2, dk2, dv2 = cross_backward(q2, k2, v2, ctx2, log2, db2, weights)
    whole = [[(0, base), (1, base)] for base in feed_halves.bases]
    arrays, held, _ = halve(feed_halves, [after(keep, dq2), got], whole, None, 0)
    du2 = after(du2, arrays[0])
    middle_halves, (du1, db1, memory_own, memory_back, keep, send) = middle(
        info,
        du2,
        dq2,
        dk2,
        dv2,
        db2,
        sums_feed,
        sums_hidden,
        normed1,
        inverse1,
        first,
        memory,
        memory_other,
        ctx2,
        ctx1,
        weights,
        row(self_norm_gain),
    )
    arrays[0] = after(arrays[0], db1)
    for index in range(1, rounds):
        arrays, held, _ = halve(feed_halves, arrays, held, None, index)
    got = swap(after(send, arrays[0]), 1, 0)
    db1 = after(db1, arrays[0])
    pairs = width // PAIR // 2
    operands = (info, q1, k1, v1, k1o, v1o, ctx1, log1)
    grads_early = self_backward(*operands, db1, weights, 0, pairs)
    arrays[0] = after(arrays[0], grads_early[0])
    plans = feed_halves.line(held, None)
    riding = memory_back.shape[1] == arrays[0].shape[1]
    if riding:
        plans[1].append((memory_back.shape[0], [(len(arrays), 0)]))
        arrays.append(memory_back)
    lines_feed = line_swaps(add_rows(arrays, plans))
    whole = [[(0, base), (1, base)] for base in middle_halves.bases]
    rider = [(0, middle_halves.main), (1, middle_halves.main)]
    keep = after(keep, lines_feed[0])
    arrays, held, rider = halve(middle_halves, [keep, got], whole, rider, 0)
    db1, _, _ = lax.optimization_barrier((db1, arrays[0], lines_feed[0]))
    grads_late = list(self_backward(*operands, db1, weights, pairs, pairs))
    lines_feed[0] = after(lines_feed[0], grads_late[0])
    block = feed_in.shape[0]
    each = range(nt)
    grad_feed_in, grad_feed_out = add_rows(
        lines_feed,
        [[(block, [(k, i * block) for k in each])] for i in range(2)],
        F32,
    )
    arrays[0] = after(arrays[0], grad_feed_in)
    for index in range(1, rounds):
        arrays, held, rider = halve(middle_halves, arrays, held, rider, index)
    grads_late[0] = after(grads_late[0], arrays[0])
    self_halves, (inputs_back, keep, send) = self_grads(
        info, inputs, inputs_other, grads_early, grads_late, weights
    )
    got = swap(after(send, *arrays), 1, 0)
    if riding:
        memory_got = lines_feed[1][2 * block :]
    else:
        memory_got = swap(after(memory_back, lines_feed[0]), 0, 1)
    grad_memory = memory_own + memory_got.astype(F32)

    rider_self = self_halves.rider
    size = self_halves.sizes[0]
    parts = add_rows(
        [keep, got],
        [
            [(size, [(0, j * size), (1, j * size)]), (rider_self, [(0, self_halves.main), (1, self_halves.main)])]
            for j in map(lambda j: self_halves.place(0, j)[0] // size, range(nd // 2))
        ],
    )
    planes = [parts[0]] + [swap(part, 2 * j, 0) for j, part in enumerate(parts) if j]
    inputs_got = hand_over(after(inputs_back, parts[0]), 1, -1)
    count = len(arrays)
    planes_at = range(count, count + len(planes))
    plans = middle_halves.line(held, rider)
    for k, plan in enumerate(plans):
        rows = 3 * block
        plan.append((rows, [(p, k * rows) for p in planes_at]))
        plan.append((rider_self, [(p, size) for p in planes_at]))
    lines = line_swaps(add_rows(arrays + planes, plans))
    grad_inputs = input_grads(du1, grads_early[:3], grads_late[:3], weights, inputs_got)
    lines[0] = after(lines[0], grad_inputs)
    middle_rider = 5 * block
    self_at = middle_rider + middle_halves.rider
    cuts = [(i * block, block) for i in range(5)] + [(middle_rider, middle_halves.rider)]
    cuts += [(self_at + i * block, block) for i in range(3)] + [(self_at + 3 * block, rider_self)]
    sums = add_rows(lines, [[(n, [(k, lo) for k in each])] for lo, n in cuts], F32)
    grad_middle, early = sums[:5], sums[5]
    grad_self, late_sums = sums[6:9], sums[9]
    early = early.reshape(nt, 16, columns).transpose(1, 0, 2).reshape(16, width)
    late_sums = late_sums[: 2 * nt].reshape(2, width)

    def mine(vector):
        count = vector.shape[0] // nt
        return lax.dynamic_slice_in_dim(vector, me_t * count, count)

    return (
        outputs,
        grad_inputs,
        grad_memory,
        grad_self[0],
        mine(late_sums[0]),
        grad_self[1],
        grad_self[2],
        mine(late_sums[1]),
        grad_middle[0].T,
        early[0],
        early[1],
        early[2],
        grad_middle[1],
        mine(early[9]),
        grad_middle[2],
        grad_middle[3],
        mine(early[10]),
        grad_middle[4].T,
        early[3],
        early[4],
        early[5],
        grad_feed_in,
        mine(early[11:15].reshape(-1)),
        grad_feed_out.T,
        early[6],
        early[7],
        early[8],
    )


def solution(mesh):
    placed = (
        P(("dp", "tensor"), None),
        P(("dp", "tensor"), None),
        P("dp"),
        P("dp", "tensor"),
        P("tensor"),
        P("dp", "tensor"),
        P("dp", "tensor"),
        P("tensor"),
        P("tensor", "dp"),
        P(),
        P(),
        P(),
        P("dp", "tensor"),
        P("tensor"),
        P("dp", "tensor"),
        P("dp", "tensor"),
        P("tensor"),
        P("tensor", "dp"),
        P(),
        P(),
        P(),
        P("dp", "tensor"),
        P("tensor"),
        P("tensor", "dp"),
        P(),
        P(),
        P(),
        P(("dp", "tensor"), None),
    )
    return jax.shard_map(
        on_device,
        mesh=mesh,
        in_specs=placed,
        out_specs=(
            P(("dp", "tensor"), None),
            P(("dp", "tensor"), None),
            P(("dp", "tensor"), None),
            P("dp", "tensor"),
            P("tensor"),
            P("dp", "tensor"),
            P("dp", "tensor"),
            P("tensor"),
            P("tensor", "dp"),
            P(),
            P(),
            P(),
            P("dp", "tensor"),
            P("tensor"),
            P("dp", "tensor"),
            P("dp", "tensor"),
            P("tensor"),
            P("tensor", "dp"),
            P(),
            P(),
            P(),
            P("dp", "tensor"),
            P("tensor"),
            P("tensor", "dp"),
            P(),
            P(),
            P(),
        ),
        check_vma=False,
    )
```

```python
import functools

import jax
import jax.numpy as jnp
from jax import lax
from jax.experimental import pallas as pl
from jax.experimental.pallas import tpu as pltpu
from jax.sharding import PartitionSpec as P

HD = 64
LEN = 1024
MEM = 256
PAIR = 128
BLOCK = 256
BACK_BLOCK = 512

EPSILON = 1e-05
MASKED = -1e30
SCALE = float(HD) ** (-0.5)

F32 = jnp.float32
BF16 = jnp.bfloat16
NN = (((1,), (0,)), ((), ()))
NT = (((1,), (1,)), ((), ()))
TN = (((0,), (0,)), ((), ()))
SMEM = pl.BlockSpec(memory_space=pltpu.SMEM)
ANY = pl.BlockSpec(memory_space=pl.ANY)
VMEM = pl.BlockSpec(memory_space=pltpu.VMEM)


def mm(left_side, right_side, dims):
    return lax.dot_general(left_side, right_side, dims, preferred_element_type=F32)


def shaped(shape, dtype):
    return jax.ShapeDtypeStruct(shape, dtype)


def cost(macs, moved):
    return pl.CostEstimate(flops=macs // 64, bytes_accessed=moved // 64, transcendentals=0)


def limit(mebibytes):
    return pltpu.CompilerParams(vmem_limit_bytes=mebibytes << 20)


def far(*arrays):
    return [pltpu.with_memory_space_constraint(array, pltpu.HBM) for array in arrays]


def swap(array, dp_mask, tensor_mask):
    nd, nt = lax.axis_size("dp"), lax.axis_size("tensor")
    pairs = [
        (d * nt + t, (d ^ dp_mask) * nt + (t ^ tensor_mask)) for d in range(nd) for t in range(nt)
    ]
    return lax.ppermute(array, ("dp", "tensor"), pairs)


def hand_over(array, parity, step):
    nd, nt = lax.axis_size("dp"), lax.axis_size("tensor")
    pairs = [(d * nt + t, d * nt + t + step) for d in range(nd) for t in range(parity, nt, 2)]
    return lax.ppermute(array, ("dp", "tensor"), pairs)


def tree_sum(terms):
    while len(terms) > 1:
        terms = [terms[i] + terms[i + 1] for i in range(0, len(terms), 2)]
    return terms[0]


def doubled(line, bits):
    for bit in bits:
        line = jnp.concatenate([line, swap(line, 0, bit)])
    return line


def over_planes(line):
    return [line] + [swap(line, 2 * j, 0) for j in range(1, lax.axis_size("dp") // 2)]


def both_cores(planes, *others):
    plane = jnp.stack([after(planes[0], *others)] + planes[1:])
    return plane, swap(plane, 1, 0)


class Halves:
    def __init__(self, groups, r, rider):
        self.planes, self.nt = lax.axis_size("dp") // 2, lax.axis_size("tensor")
        self.groups, self.r, self.rider = groups, r, rider
        self.rounds = self.planes.bit_length() - 1
        self.sizes = [self.nt * count * r for count in groups]
        self.bases = [self.planes * sum(self.sizes[:g]) for g in range(len(groups))]
        self.main = self.planes * sum(self.sizes)
        self.total = self.main + rider

    def bit(self, group, index):
        return 1 << (index if group % 2 == 0 else self.rounds - 1 - index)

    def place(self, i, j):
        group = 0
        while i >= self.groups[group]:
            i -= self.groups[group]
            group += 1
        bits = [self.bit(group, index) for index in range(self.rounds)]
        position = sum((j & b > 0) << (self.rounds - 1 - n) for n, b in enumerate(bits))
        count = self.groups[group]
        return self.bases[group] + position * self.sizes[group] + i * self.r, count * self.r

    def split(self, arrays, held, rider, index):
        stay, sent = [], []
        for group, terms in enumerate(held):
            rows = (self.planes >> (index + 1)) * self.sizes[group]
            stay.append([(rows, terms)])
            sent.append([(rows, [(array, lo + rows) for array, lo in terms])])
        if self.rider:
            sent[-1].append((self.rider, rider))
        return stay + sent


def add_rows_kernel(*refs, plans, count):
    for out, plan in zip(refs[count:], plans):
        at = 0
        for rows, terms in plan:
            total = tree_sum([refs[i][lo : lo + rows, :].astype(F32) for i, lo in terms])
            out[at : at + rows, :] = total.astype(out.dtype)
            at += rows


def add_rows(arrays, plans, dtype=BF16):
    width = arrays[0].shape[1]
    moved = sum(array.size * array.dtype.itemsize for array in arrays)
    return pl.pallas_call(
        functools.partial(add_rows_kernel, plans=plans, count=len(arrays)),
        out_shape=tuple(shaped((sum(n for n, _ in plan), width), dtype) for plan in plans),
        in_specs=[VMEM] * len(arrays),
        out_specs=(VMEM,) * len(plans),
        compiler_params=limit(20),
        cost_estimate=cost(0, 2 * moved),
    )(*arrays)


def halve(halves, arrays, held, rider, index):
    groups = len(halves.groups)
    outs = list(add_rows(arrays, halves.split(arrays, held, rider, index)))
    stay, sent = outs[:groups], outs[groups:]
    got = [swap(part, 2 * halves.bit(group, index), 0) for group, part in enumerate(sent)]
    held = [[(group, 0), (groups + group, 0)] for group in range(groups)]
    end = sent[-1].shape[0] - halves.rider
    rider = [(2 * groups, end), (2 * groups - 1, end)]
    return stay + got + sent[-1:], held, rider


def line_round(arrays, segments, rider, bit, extra=None):
    stay, sent, after_round, lo = [], [], [], 0
    for rows, terms in segments:
        half = rows // 2
        stay.append((half, terms))
        sent.append((half, [(array, first + half) for array, first in terms]))
        after_round.append((half, [(0, lo), (1, lo)]))
        lo += half
    if rider:
        sent.append(rider)
        rider = (rider[0], [(1, lo), (2, lo)])
    if extra is not None:
        sent.append((extra.shape[0], [(len(arrays), 0)]))
        arrays = arrays + [extra]
    stay, sent = add_rows(arrays, [stay, sent])
    return [stay, swap(sent, 0, bit), sent], after_round, rider


def line_swaps(parts):
    return [parts[0]] + [swap(part, 0, k) for k, part in enumerate(parts) if k]


def after(array, *others):
    return lax.optimization_barrier((array,) + others)[0]


def slot_blocks(info, planes, nt):
    for j in range(planes):
        for c in range(2):
            d = jnp.bitwise_xor(info[2], 2 * j + c)
            for s in range(nt):
                yield j, c, s, d, jnp.bitwise_xor(info[3], s)


def aligned(r, w):
    return w % PAIR == 0 and r % 16 == 0


def assemble_kernel(info, *refs, planes):
    whole = refs[-1]
    nt, n, r, w = refs[0].shape[-4:]
    for j, c, s, d, t in slot_blocks(info, planes, nt):
        rows = pl.ds(pl.multiple_of(d * r, r), r)
        columns = pl.ds(pl.multiple_of(t * w, w), w)
        piece = refs[c].at[j] if len(refs) == 3 else refs[c * planes + j]
        for i in range(n):
            whole[i, rows, columns] = piece[s, i]


def assemble(info, halves):
    nt, n, r, w = halves[0].shape[-4:]
    planes = lax.axis_size("dp") // 2
    nd = 2 * planes
    if aligned(r, w):
        return pl.pallas_call(
            functools.partial(assemble_kernel, planes=planes),
            out_shape=shaped((n, nd * r, nt * w), BF16),
            in_specs=[SMEM] + [VMEM] * len(halves),
            out_specs=VMEM,
            compiler_params=limit(18),
            cost_estimate=cost(0, 8 * nd * nt * n * r * w),
        )(info, *halves)
    full = jnp.stack(halves).reshape(2, planes, nt, n, r, w).swapaxes(0, 1)
    full = full.reshape(nd, nt, n, r, w)
    full = jnp.take(full, jnp.bitwise_xor(jnp.arange(nd), info[2]), axis=0)
    full = jnp.take(full, jnp.bitwise_xor(jnp.arange(nt), info[3]), axis=1)
    return full.transpose(2, 0, 3, 1, 4).reshape(n, nd * r, nt * w)


def disperse(info, halves, scratch, i, t, s, keep, send):
    for j in range(halves.planes):
        base, stride = halves.place(i, j)
        lo = base + s * stride
        if not isinstance(s, int):
            lo = pl.multiple_of(lo, 16)
        for c in range(2):
            d = jnp.bitwise_xor(info[2], 2 * j + c)
            rows = pl.ds(pl.multiple_of(d * halves.r, halves.r), halves.r)
            (keep, send)[c][pl.ds(lo, halves.r), :] = scratch[rows, t]


def disperse_whole(info, halves, scratch, i, keep, send):
    w = keep.shape[1]
    for s in range(halves.nt):
        t = jnp.bitwise_xor(info[3], s)
        disperse(info, halves, scratch, i, pl.ds(pl.multiple_of(t * w, w), w), s, keep, send)


def disperse_plain(info, halves, whole, rider):
    nd, nt = 2 * halves.planes, halves.nt
    n, r, w = whole.shape[0], halves.r, whole.shape[2] // nt
    full = whole.reshape(n, nd, r, nt, w).transpose(1, 3, 0, 2, 4)
    full = jnp.take(full, jnp.bitwise_xor(jnp.arange(nd), info[2]), axis=0)
    full = jnp.take(full, jnp.bitwise_xor(jnp.arange(nt), info[3]), axis=1)
    full = full.reshape(nd // 2, 2, nt, n, r, w)
    flats = []
    for c in range(2):
        rows, first = [], 0
        for count in halves.groups:
            order = sorted(range(halves.planes), key=lambda j: halves.place(first, j)[0])
            group = jnp.stack([full[j, c, :, first : first + count] for j in order])
            rows.append(group.reshape(-1, w))
            first += count
        flats.append(jnp.concatenate(rows + [rider]))
    return flats


def pack_kernel(*refs, blocks):
    out = refs[-1]
    r, w = refs[0].shape
    for i, block in enumerate(refs[:blocks]):
        out[i * r : (i + 1) * r, :] = block[...]
    row = lax.broadcasted_iota(jnp.int32, (16, w), 0)
    filled = jnp.zeros((16, w), F32)
    count = 0
    for vector in refs[blocks:-1]:
        for i in range(vector.shape[0]):
            filled = jnp.where(row == count, vector[i : i + 1, :].astype(F32), filled)
            count += 1
    out[blocks * r :, :] = filled.astype(BF16)


def pack(blocks, vectors):
    r, w = blocks[0].shape
    if aligned(r, w):
        return pl.pallas_call(
            functools.partial(pack_kernel, blocks=len(blocks)),
            out_shape=shaped((len(blocks) * r + 16, w), BF16),
            in_specs=[VMEM] * (len(blocks) + len(vectors)),
            out_specs=VMEM,
            cost_estimate=cost(0, 32 * r * w),
        )(*blocks, *[vector.reshape(-1, w) for vector in vectors])
    rows = jnp.concatenate(vectors).reshape(-1, w)
    return jnp.concatenate(list(blocks) + [jnp.pad(rows, ((0, 16 - rows.shape[0]), (0, 0)))])


def spread_kernel(info, riders, small, hidden):
    nt, _, w = riders.shape
    for s in range(nt):
        t = jnp.bitwise_xor(info[3], s)
        block = riders[s].astype(F32)
        small[:, pl.ds(pl.multiple_of(t * w, w), w)] = block
        for i in range(4):
            hidden[:, pl.ds(pl.multiple_of((4 * t + i) * w, w), w)] = block[4 + i : 5 + i]


def spread(info, riders):
    nt, _, w = riders.shape
    if aligned(16, w):
        return pl.pallas_call(
            spread_kernel,
            out_shape=(shaped((16, nt * w), F32), shaped((1, 4 * nt * w), F32)),
            in_specs=[SMEM, VMEM],
            out_specs=(VMEM, VMEM),
            cost_estimate=cost(0, 64 * nt * w),
        )(info, riders)
    full = jnp.take(riders, jnp.bitwise_xor(jnp.arange(nt), info[3]), axis=0).astype(F32)
    return full.transpose(1, 0, 2).reshape(16, nt * w), full[:, 4:8].reshape(1, -1)


def norm_forward(summed):
    row_mean = jnp.mean(summed, axis=-1, keepdims=True)
    centred = summed - row_mean
    variance = jnp.mean(centred * centred, axis=-1, keepdims=True)
    inverse = lax.rsqrt(variance + EPSILON)
    return centred * inverse, inverse


def norm_backward(grad_out, normed, inverse, norm_gain):
    grad_normed = grad_out * norm_gain
    return inverse * (
        grad_normed
        - jnp.mean(grad_normed, axis=-1, keepdims=True)
        - normed * jnp.mean(grad_normed * normed, axis=-1, keepdims=True)
    )


def column_sum(values):
    return jnp.sum(values.astype(F32), axis=0, keepdims=True)


def head_lanes(e):
    lane = lax.broadcasted_iota(jnp.int32, (1, PAIR), 1)
    chosen = (lane < HD) if e == 0 else (lane >= HD)
    return jnp.where(chosen, 1.0, 0.0)


def join_heads(first, second):
    lane = lax.broadcasted_iota(jnp.int32, first.shape, 1)
    return jnp.where(lane < HD, first, second)


def attend_forward(q, segments, contexts, logs, lo):
    rows = slice(lo, lo + BLOCK)
    results = []
    for e in range(2):
        query = q[rows, :] * head_lanes(e).astype(BF16)
        scores = [edit(mm(query, k, NT)) for k, _, edit in segments]
        peak = functools.reduce(
            jnp.maximum, [jnp.max(piece, axis=-1, keepdims=True) for piece in scores]
        )
        total = None
        for piece, (_, v, _) in zip(scores, segments):
            weights = jnp.exp(piece - peak).astype(BF16)
            wide = jnp.concatenate([v, jnp.ones(v.shape, BF16)], axis=1)
            part = mm(weights, wide, NN)
            total = part if total is None else total + part
        row_total = total[:, PAIR:]
        results.append((total[:, :PAIR] / row_total, peak + jnp.log(row_total)))
    contexts[rows, :] = join_heads(results[0][0], results[1][0]).astype(BF16)
    logs[rows, :] = join_heads(results[0][1], results[1][1])


def attend_backward(q, grad, ctx, logs, segments, grad_query, lo):
    rows = slice(lo, lo + BACK_BLOCK)
    grad_rows = grad[rows, :]
    product = grad_rows.astype(F32) * ctx[rows, :].astype(F32)
    query_rows = q[rows, :]
    query_turned = jnp.transpose(query_rows)
    grad_turned = jnp.transpose(grad_rows)
    total = None
    for e in range(2):
        lanes = head_lanes(e)
        low_lanes = lanes.astype(BF16)
        delta = jnp.sum(product * lanes, axis=-1, keepdims=True)
        row_log = logs[rows, e * HD : e * HD + 1]
        grad_low = grad_rows * low_lanes
        query = query_rows * low_lanes
        for k, v, edit, add in segments:
            weights = jnp.exp(edit(mm(query, k, NT)) - row_log)
            slope = mm(grad_low, v, NT) - delta
            grad_scores = (weights * slope).astype(BF16)
            part = mm(grad_scores, k * low_lanes, NN)
            total = part if total is None else total + part
            head = slice(e * HD, e * HD + HD)
            add(
                head,
                mm(query_turned[head], grad_scores, NN),
                mm(grad_turned[head], weights.astype(BF16), NN),
            )
    grad_query[rows, :] = (total * SCALE).astype(BF16)


def same(scores):
    return scores


def masked(lo, col_lo, prefix_len):
    def edit(scores):
        row = lo + lax.broadcasted_iota(jnp.int32, scores.shape, 0)
        col = col_lo + lax.broadcasted_iota(jnp.int32, scores.shape, 1)
        allowed = col <= row
        if prefix_len is not None:
            allowed = allowed | (col < prefix_len)
        return jnp.where(allowed, scores, MASKED)

    return edit


def adder(keys, values, col_lo, width):
    def add(head, part_keys, part_values):
        keys[head, col_lo : col_lo + width] += part_keys
        values[head, col_lo : col_lo + width] += part_values

    return add


def self_forward_kernel(info, q, k, v, ko, vo, ctx, logs):
    tokens = q.shape[0]

    @pl.when(info[0] == 0)
    def _():
        for lo in range(0, tokens, BLOCK):
            attend_forward(q, [(k[...], v[...], masked(lo, 0, info[1]))], ctx, logs, lo)

    @pl.when(info[0] != 0)
    def _():
        for lo in range(0, tokens, BLOCK):
            near = slice(lo, lo + BLOCK)
            segments = [(ko[...], vo[...], same)]
            if lo:
                segments.append((k[:lo, :], v[:lo, :], same))
            segments.append((k[near, :], v[near, :], masked(lo, lo, None)))
            attend_forward(q, segments, ctx, logs, lo)


def self_backward_kernel(
    info, q, k, v, ko, vo, ctx, logs, low, w, dq, dk, dv, dko, dvo, ak, av, ako, avo, grad
):
    tokens = q.shape[0]
    ak[...] = jnp.zeros_like(ak)
    av[...] = jnp.zeros_like(av)
    grad[...] = mm(low[...], w[0], NN).astype(BF16)

    @pl.when(info[0] == 0)
    def _():
        for lo in range(0, tokens, BACK_BLOCK):
            segments = [(k[...], v[...], masked(lo, 0, info[1]), adder(ak, av, 0, tokens))]
            attend_backward(q, grad, ctx, logs, segments, dq, lo)

    @pl.when(info[0] != 0)
    def _():
        ako[...] = jnp.zeros_like(ako)
        avo[...] = jnp.zeros_like(avo)
        for lo in range(0, tokens, BACK_BLOCK):
            near = slice(lo, lo + BACK_BLOCK)
            segments = [(ko[...], vo[...], same, adder(ako, avo, 0, tokens))]
            if lo:
                segments.append((k[:lo, :], v[:lo, :], same, adder(ak, av, 0, lo)))
            segments.append(
                (k[near, :], v[near, :], masked(lo, lo, None), adder(ak, av, lo, BACK_BLOCK))
            )
            attend_backward(q, grad, ctx, logs, segments, dq, lo)
        dko[...] = jnp.transpose(ako[...]).astype(BF16)
        dvo[...] = jnp.transpose(avo[...]).astype(BF16)

    dk[...] = jnp.transpose(ak[...]).astype(BF16)
    dv[...] = jnp.transpose(av[...]).astype(BF16)


def cross_forward_kernel(q, k, v, ctx, logs):
    for lo in range(0, q.shape[0], BLOCK):
        attend_forward(q, [(k[...], v[...], same)], ctx, logs, lo)


def cross_backward_kernel(q, k, v, ctx, logs, low, w, dq, dk, dv, ak, av, grad):
    ak[...] = jnp.zeros_like(ak)
    av[...] = jnp.zeros_like(av)
    grad[...] = mm(low[...], w[0], NN).astype(BF16)
    for lo in range(0, q.shape[0], BACK_BLOCK):
        segments = [(k[...], v[...], same, adder(ak, av, 0, k.shape[0]))]
        attend_backward(q, grad, ctx, logs, segments, dq, lo)
    dk[...] = jnp.transpose(ak[...]).astype(BF16)
    dv[...] = jnp.transpose(av[...]).astype(BF16)


def lanes_of(rows, first=0):
    return pl.BlockSpec((rows, PAIR), lambda h: (0, first + h))


def output_columns(slot, width, first=0):
    return pl.BlockSpec((1, width, PAIR), lambda h: (slot, 0, first + h))


def self_forward(info, q, k, v, ko, vo):
    tokens, width = q.shape
    row = lanes_of(tokens)
    return pl.pallas_call(
        self_forward_kernel,
        grid=(width // PAIR,),
        out_shape=(shaped((tokens, width), BF16), shaped((tokens, width), F32)),
        in_specs=[SMEM] + [row] * 5,
        out_specs=(row, row),
        compiler_params=limit(16),
        cost_estimate=cost(width // HD * tokens * tokens * 2 * 256 * 2, 5 << 20),
    )(info, q, k, v, ko, vo)


def self_backward(info, q, k, v, ko, vo, ctx, logs, low, w, first, pairs):
    tokens, width = q.shape
    row = lanes_of(tokens, first)
    out = shaped((tokens, pairs * PAIR), BF16)
    return pl.pallas_call(
        self_backward_kernel,
        grid=(pairs,),
        out_shape=(out,) * 5,
        in_specs=[SMEM] + [row] * 7 + [VMEM, output_columns(3, width, first)],
        out_specs=(lanes_of(tokens),) * 5,
        scratch_shapes=[pltpu.VMEM((PAIR, tokens), F32)] * 4 + [pltpu.VMEM((tokens, PAIR), BF16)],
        compiler_params=limit(16),
        cost_estimate=cost(width // HD * tokens * tokens * 256 * 5, 8 << 20),
    )(info, *far(q, k, v, ko, vo, ctx, logs), low, *far(w))


def cross_forward(q, k, v):
    tokens, width = q.shape
    rows = k.shape[0]
    return pl.pallas_call(
        cross_forward_kernel,
        grid=(width // PAIR,),
        out_shape=(shaped((tokens, width), BF16), shaped((tokens, width), F32)),
        in_specs=[lanes_of(tokens), lanes_of(rows), lanes_of(rows)],
        out_specs=(lanes_of(tokens), lanes_of(tokens)),
        compiler_params=limit(16),
        cost_estimate=cost(width // HD * tokens * rows * 256 * 2, 3 << 20),
    )(q, k, v)


def cross_backward(q, k, v, ctx, logs, low, w):
    tokens, width = q.shape
    rows = k.shape[0]
    small = shaped((rows, width), BF16)
    return pl.pallas_call(
        cross_backward_kernel,
        grid=(width // PAIR,),
        out_shape=(shaped((tokens, width), BF16), small, small),
        in_specs=[lanes_of(tokens), lanes_of(rows), lanes_of(rows)]
        + [lanes_of(tokens)] * 2
        + [VMEM, output_columns(7, width)],
        out_specs=(lanes_of(tokens), lanes_of(rows), lanes_of(rows)),
        scratch_shapes=[pltpu.VMEM((PAIR, rows), F32)] * 2 + [pltpu.VMEM((tokens, PAIR), BF16)],
        compiler_params=limit(16),
        cost_estimate=cost(width // HD * tokens * rows * 256 * 5, 4 << 20),
    )(*far(q, k, v, ctx, logs), low, *far(w))


def project_self_kernel(info, x, xo, wq, wk, wv, b, q, k, v, ko, vo):
    rows = x[...]
    q[...] = (mm(rows, wq[0], NN) + b[0:1, :]).astype(BF16) * jnp.asarray(SCALE, BF16)
    k[...] = mm(rows, wk[0], NN).astype(BF16)
    v[...] = (mm(rows, wv[0], NN) + b[1:2, :]).astype(BF16)

    @pl.when(info[0] != 0)
    def _():
        other = xo[...]
        ko[...] = mm(other, wk[0], NN).astype(BF16)
        vo[...] = (mm(other, wv[0], NN) + b[1:2, :]).astype(BF16)


def project_self(info, x, xo, w, b):
    low = shaped(x.shape, BF16)
    return pl.pallas_call(
        project_self_kernel,
        grid=(1,),
        out_shape=(low,) * 5,
        in_specs=[SMEM] + [VMEM] * 2 + [matrix(i, x.shape[1]) for i in range(3)] + [VMEM],
        compiler_params=limit(16),
        cost_estimate=cost(5 * x.size * x.shape[1], 5 << 20),
    )(info, x, xo, w, w, w, b)


def first_norm_kernel(
    ctx, x, mem, memo, wo, wq, wk, wv, ob, gain, bias, b, first, normed, inverse, q, k, v
):
    summed = x[...].astype(F32) + mm(ctx[...], wo[0], NT) + ob[...].astype(F32)
    n, r = norm_forward(summed)
    out = n * gain[...].astype(F32) + bias[...].astype(F32)
    normed[...] = n
    inverse[...] = r
    first[...] = out
    q[...] = (mm(out.astype(BF16), wq[0], NN) + b[2:3, :]).astype(BF16) * jnp.asarray(SCALE, BF16)
    rows = mem.shape[0]
    for source, lo in ((mem, 0), (memo, rows)):
        k[lo : lo + rows, :] = mm(source[...], wk[0], NN).astype(BF16)
        v[lo : lo + rows, :] = (mm(source[...], wv[0], NN) + b[3:4, :]).astype(BF16)


def first_norm(ctx, x, mem, memo, w, ob, gain, bias, b):
    rows = 2 * mem.shape[0]
    tokens, width = x.shape
    full = shaped(x.shape, F32)
    return pl.pallas_call(
        first_norm_kernel,
        grid=(1,),
        out_shape=(
            full,
            full,
            shaped((tokens, 1), F32),
            shaped(x.shape, BF16),
            shaped((rows, width), BF16),
            shaped((rows, width), BF16),
        ),
        in_specs=[VMEM] * 4 + [matrix(i, width) for i in range(3, 7)] + [VMEM] * 4,
        compiler_params=limit(16),
        cost_estimate=cost(3 * x.size * width, 8 << 20),
    )(ctx, x, mem, memo, w, w, w, w, ob, gain, bias, b)


def feed_kernel(
    info,
    ctx,
    first,
    cot,
    wo,
    wf,
    ob,
    gain2,
    bias2,
    fib,
    fob,
    gain3,
    bias3,
    out,
    keep,
    send,
    du3,
    dhid,
    normed,
    inverse,
    sums,
    hsum,
    act,
    slope,
    acc,
    second,
    db3,
    turn,
    *,
    halves,
):
    tokens, width = first.shape
    w = keep.shape[1]
    summed = first[...] + mm(ctx[...], wo[0], NT) + ob[...].astype(F32)
    n2, r2 = norm_forward(summed)
    normed[...] = n2
    inverse[...] = r2
    out2 = n2 * gain2[...].astype(F32) + bias2[...].astype(F32)
    second[...] = out2.astype(BF16)
    acc[...] = out2 + fob[...].astype(F32)

    @pl.loop(0, halves.nt, unroll=2)
    def _(t):
        cols = pl.ds(pl.multiple_of(t * w, w), w)
        hidden = mm(second[...], wf[0, :, cols], NN) + fib[:, cols]
        gate = 1.0 / (1.0 + jnp.exp(-hidden))
        active = (hidden * gate).astype(BF16)
        act[:, cols] = active
        slope[:, cols] = (gate * (1.0 + hidden * (1.0 - gate))).astype(BF16)
        acc[...] += mm(active, wf[1, :, cols], NT)

    n3, r3 = norm_forward(acc[...])
    out[...] = (n3 * gain3[...].astype(F32) + bias3[...].astype(F32)).astype(BF16)
    dy = cot[...].astype(F32)
    grad3 = norm_backward(dy, n3, r3, gain3[...].astype(F32))
    low3 = grad3.astype(BF16)
    sums[0:1, :] = column_sum(low3)
    sums[1:2, :] = column_sum(dy * n3)
    sums[2:3, :] = column_sum(dy)
    sums[3:8, :] = jnp.zeros((5, width), F32)
    du3[...] = grad3
    db3[...] = low3

    @pl.loop(0, halves.nt, unroll=2)
    def _(t):
        cols = pl.ds(pl.multiple_of(t * w, w), w)
        s = jnp.bitwise_xor(info[3], t)
        everything = slice(None)
        back = db3[...]
        dact = mm(back, wf[1, :, cols], NN)
        part = (dact * slope[:, cols].astype(F32)).astype(BF16)
        dhid[:, cols] = part
        hsum[:, cols] = column_sum(part)
        turn[0] = mm(second[...], part, TN).astype(BF16)
        disperse(info, halves, turn.at[0], 0, everything, s, keep, send)
        turn[1] = mm(back, act[:, cols], TN).astype(BF16)
        disperse(info, halves, turn.at[1], 1, everything, s, keep, send)


def feed_back_kernel(du3, dhid, normed, inverse, wf, gain, du2, db2, sums):
    dsecond = du3[...] + mm(dhid[...], wf[0], NT)
    n = normed[...]
    grad = norm_backward(dsecond, n, inverse[...], gain[...].astype(F32))
    low = grad.astype(BF16)
    du2[...] = grad
    db2[...] = low
    sums[0:1, :] = column_sum(low)
    sums[1:2, :] = column_sum(dsecond * n)
    sums[2:3, :] = column_sum(dsecond)
    sums[3:8, :] = jnp.zeros((5, du2.shape[1]), F32)


def feed_back(du3, dhid, normed, inverse, wf, gain):
    tokens, width = du3.shape
    wide = wf.shape[2]
    return pl.pallas_call(
        feed_back_kernel,
        grid=(1,),
        out_shape=(shaped(du3.shape, F32), shaped(du3.shape, BF16), shaped((8, width), F32)),
        in_specs=[VMEM] * 4 + [pl.BlockSpec((1, width, wide), lambda h: (0, 0, 0)), VMEM],
        compiler_params=limit(16),
        cost_estimate=cost(tokens * width * wide, 8 << 20),
    )(du3, dhid, normed, inverse, wf, gain)


def matrix(slot, width):
    return pl.BlockSpec((1, width, width), lambda h: (slot, 0, 0))


def feed(info, halves, ctx, first, cot, wo, wf, ob, gain2, bias2, fib, fob, gain3, bias3):
    tokens, width = first.shape
    wide = wf.shape[2]
    w = wide // halves.nt
    flat = shaped((halves.total, w), BF16)
    return pl.pallas_call(
        functools.partial(feed_kernel, halves=halves),
        grid=(1,),
        out_shape=(
            shaped(first.shape, BF16),
            flat,
            flat,
            shaped(first.shape, F32),
            shaped((tokens, wide), BF16),
            shaped(first.shape, F32),
            shaped((tokens, 1), F32),
            shaped((8, width), F32),
            shaped((1, wide), F32),
        ),
        in_specs=[SMEM] + [VMEM] * 3 + [matrix(7, width)] + [VMEM] * 8,
        scratch_shapes=[
            pltpu.VMEM((tokens, wide), BF16),
            pltpu.VMEM((tokens, wide), BF16),
            pltpu.VMEM((tokens, width), F32),
            pltpu.VMEM((tokens, width), BF16),
            pltpu.VMEM((tokens, width), BF16),
            pltpu.VMEM((2, width, w), BF16),
        ],
        compiler_params=limit(28),
        cost_estimate=cost(6 * tokens * width * wide, 14 << 20),
    )(info, ctx, first, cot, wo, wf, ob, gain2, bias2, fib, fob, gain3, bias3)


def middle_kernel(
    info,
    du2,
    dq2,
    dk2,
    dv2,
    db2,
    sums2,
    sums3,
    hsum,
    normed,
    inverse,
    first,
    mem,
    memo,
    ctx2,
    ctx1,
    wq,
    wk,
    wv,
    gain,
    *outs,
    halves,
):
    du1, db1, own, other = outs[:4]
    turn, riders = outs[-2:]
    rows, width = mem.shape
    dfirst = du2[...] + mm(dq2[...], wq[0], NT)
    n = normed[...]
    grad = norm_backward(dfirst, n, inverse[...], gain[...].astype(F32))
    low = grad.astype(BF16)
    du1[...] = grad
    db1[...] = low
    riders[0:1, :] = column_sum(low)
    riders[1:2, :] = column_sum(dfirst * n)
    riders[2:3, :] = column_sum(dfirst)
    riders[3:6, :] = sums2[0:3, :]
    riders[6:9, :] = sums3[0:3, :]
    riders[9:10, :] = column_sum(dq2[...])
    riders[10:11, :] = column_sum(dv2[...])
    for i in range(4):
        riders[11 + i : 12 + i, :] = hsum[:, i * width : (i + 1) * width]
    riders[15:16, :] = jnp.zeros((1, width), F32)
    turn[0] = mm(low, ctx1[...], TN).astype(BF16)
    turn[1] = mm(first[...].astype(BF16), dq2[...], TN).astype(BF16)
    for slot, part in ((2, dk2), (3, dv2)):
        turn[slot] = (
            mm(mem[...], part[:rows, :], TN) + mm(memo[...], part[rows:, :], TN)
        ).astype(BF16)
    turn[4] = mm(db2[...], ctx2[...], TN).astype(BF16)
    back = mm(dk2[...], wk[0], NT) + mm(dv2[...], wv[0], NT)
    own[...] = back[:rows, :]
    other[...] = back[rows:, :].astype(BF16)
    if halves is None:
        outs[4][...] = turn[...]
        outs[5][...] = riders[...]
        return
    for i in range(5):
        disperse_whole(info, halves, turn.at[i], i, outs[4], outs[5])
    w = outs[4].shape[1]
    for target in outs[4:6]:
        for q in range(width // w):
            lo = halves.main + 16 * q
            target[lo : lo + 16, :] = riders[:, q * w : q * w + w].astype(BF16)


def middle(info, near, normed, inverse, first, mem, memo, ctx2, ctx1, w, gain):
    tokens, width = first.shape
    rows = mem.shape[0]
    nd, nt = lax.axis_size("dp"), lax.axis_size("tensor")
    r, columns = width // nd, width // nt
    halves = Halves((3, 2), r, 16 * nt)
    direct = aligned(r, columns)
    if direct:
        last = (shaped((halves.total, columns), BF16),) * 2
    else:
        last = (shaped((5, width, width), BF16), shaped((16, width), F32))
    outs = pl.pallas_call(
        functools.partial(middle_kernel, halves=halves if direct else None),
        grid=(1,),
        out_shape=(
            shaped(first.shape, F32),
            shaped(first.shape, BF16),
            shaped((rows, width), F32),
            shaped((rows, width), BF16),
        )
        + last,
        in_specs=[SMEM] + [VMEM] * 15 + [matrix(i, width) for i in (4, 5, 6)] + [VMEM],
        scratch_shapes=[pltpu.VMEM((5, width, width), BF16), pltpu.VMEM((16, width), F32)],
        compiler_params=limit(20),
        cost_estimate=cost(6 * first.size * width, 12 << 20),
    )(
        info,
        *near,
        *far(normed, inverse, first, mem, memo, ctx2, ctx1, w, w, w),
        gain,
    )
    if not direct:
        rider = outs[5].astype(BF16).reshape(16, nt, columns).transpose(1, 0, 2)
        outs = outs[:4] + tuple(disperse_plain(info, halves, outs[4], rider.reshape(-1, columns)))
    return halves, outs


def self_grads_kernel(
    info, x, xo, dqa, dka, dva, dkoa, dvoa, dqb, dkb, dvb, dkob, dvob, wk, wv, *outs, halves
):
    other = outs[0]
    turn, sums = outs[-2:]
    width = x.shape[1]
    both = lambda left, right: jnp.concatenate([left[...], right[...]], axis=1)
    dq, dk, dv = both(dqa, dqb), both(dka, dkb), both(dva, dvb)
    turn[0] = mm(x[...], dq, TN).astype(BF16)
    sums[0:1, :] = column_sum(dq)

    @pl.when(info[0] == 0)
    def _():
        turn[1] = mm(x[...], dk, TN).astype(BF16)
        turn[2] = mm(x[...], dv, TN).astype(BF16)
        sums[1:2, :] = column_sum(dv)
        other[...] = jnp.zeros_like(other)

    @pl.when(info[0] != 0)
    def _():
        dko, dvo = both(dkoa, dkob), both(dvoa, dvob)
        turn[1] = (mm(x[...], dk, TN) + mm(xo[...], dko, TN)).astype(BF16)
        turn[2] = (mm(x[...], dv, TN) + mm(xo[...], dvo, TN)).astype(BF16)
        sums[1:2, :] = column_sum(dv) + column_sum(dvo)
        other[...] = (mm(dko, wk[0], NT) + mm(dvo, wv[0], NT)).astype(BF16)

    if halves is None:
        outs[1][...] = turn[...]
        outs[2][...] = sums[...]
        return
    for i in range(3):
        disperse_whole(info, halves, turn.at[i], i, outs[1], outs[2])
    w = outs[1].shape[1]
    row = lax.broadcasted_iota(jnp.int32, (16, w), 0)
    filled = jnp.zeros((16, w), F32)
    for i in range(2):
        for t in range(width // w):
            piece = sums[i : i + 1, t * w : t * w + w]
            filled = jnp.where(row == i * (width // w) + t, piece, filled)
    for target in outs[1:3]:
        target[halves.main :, :] = filled.astype(BF16)


def self_grads(info, x, xo, early, late, w):
    width = x.shape[1]
    nd, nt = lax.axis_size("dp"), lax.axis_size("tensor")
    r, columns = width // nd, width // nt
    halves = Halves((3,), r, 16)
    direct = aligned(r, columns)
    if direct:
        last = (shaped((halves.total, columns), BF16),) * 2
    else:
        last = (shaped((3, width, width), BF16), shaped((8, width), F32))
    outs = pl.pallas_call(
        functools.partial(self_grads_kernel, halves=halves if direct else None),
        grid=(1,),
        out_shape=(shaped(x.shape, BF16),) + last,
        in_specs=[SMEM] + [VMEM] * 12 + [matrix(i, width) for i in (1, 2)],
        scratch_shapes=[pltpu.VMEM((3, width, width), BF16), pltpu.VMEM((8, width), F32)],
        compiler_params=limit(16),
        cost_estimate=cost(7 * x.size * width, 8 << 20),
    )(info, *far(x, xo), *early, *late, *far(w, w))
    if not direct:
        rider = outs[2][:2].astype(BF16).reshape(-1, columns)
        rider = jnp.pad(rider, ((0, 16 - rider.shape[0]), (0, 0)))
        outs = outs[:1] + tuple(disperse_plain(info, halves, outs[1], rider))
    return halves, outs


def input_grads_kernel(du1, dqa, dka, dva, dqb, dkb, dvb, wq, wk, wv, back, out):
    both = lambda left, right: jnp.concatenate([left[...], right[...]], axis=1)
    out[...] = (
        du1[...]
        + mm(both(dqa, dqb), wq[0], NT)
        + mm(both(dka, dkb), wk[0], NT)
        + mm(both(dva, dvb), wv[0], NT)
        + back[...].astype(F32)
    )


def input_grads(du1, early, late, w, back):
    return pl.pallas_call(
        input_grads_kernel,
        grid=(1,),
        out_shape=shaped(du1.shape, F32),
        in_specs=[VMEM] * 7 + [matrix(i, du1.shape[1]) for i in range(3)] + [VMEM],
        compiler_params=limit(16),
        cost_estimate=cost(3 * du1.size * du1.shape[1], 6 << 20),
    )(*far(du1), *early, *late, *far(w, w, w), back)


def on_device(
    inputs,
    memory,
    prefix,
    self_query,
    self_query_bias,
    self_key,
    self_value,
    self_value_bias,
    self_out,
    self_out_bias,
    self_norm_gain,
    self_norm_bias,
    cross_query,
    cross_query_bias,
    cross_key,
    cross_value,
    cross_value_bias,
    cross_out,
    cross_out_bias,
    cross_norm_gain,
    cross_norm_bias,
    feed_in,
    feed_in_bias,
    feed_out,
    feed_out_bias,
    feed_norm_gain,
    feed_norm_bias,
    cotangent,
):
    nd, nt = lax.axis_size("dp"), lax.axis_size("tensor")
    me_d, me_t = lax.axis_index("dp"), lax.axis_index("tensor")
    late = me_t % 2
    width = inputs.shape[1]
    assert LEN == 2 * inputs.shape[0] and MEM == 2 * memory.shape[0]
    assert nd & (nd - 1) == 0 and nt & (nt - 1) == 0
    prefix_here = jnp.where(late == 0, lax.dynamic_index_in_dim(prefix, me_t // 2, keepdims=False), 0)
    info = jnp.stack([late, prefix_here, me_d, me_t]).astype(jnp.int32)

    columns = self_query_bias.shape[0]
    row = lambda vector: vector.reshape(1, -1)
    packed = pack(
        (
            self_query,
            self_key,
            self_value,
            self_out.T,
            cross_query,
            cross_key,
            cross_value,
            cross_out.T,
        ),
        (self_query_bias, self_value_bias, cross_query_bias, cross_value_bias, feed_in_bias),
    )
    feed_shard = jnp.stack([feed_in, feed_out.T])

    bits = [1 << i for i in range(nt.bit_length() - 1)]
    swapped = [swap(packed, 0, k) for k in range(1, nt)]
    line = jnp.stack([packed] + swapped)
    count = 8 * self_query.shape[0]
    riders = line[:, count:]
    line = line[:, :count].reshape((nt, 8) + self_query.shape)
    line_feed = doubled(after(feed_shard, line)[None], bits)
    inputs_other = hand_over(after(inputs, line), 0, 1)
    head_biases, hidden_bias = spread(info, riders)
    group = both_cores(over_planes(line), inputs_other, line_feed, head_biases)
    line_feed = after(line_feed, group[0])
    memory_other = swap(after(memory, group[0]), 0, 1)
    planes_feed = over_planes(line_feed)

    weights = assemble(info, group)
    q1, k1, v1, k1o, v1o = project_self(info, inputs, inputs_other, weights, head_biases)
    ctx1, log1 = self_forward(info, q1, k1, v1, k1o, v1o)
    first, normed1, inverse1, q2, k2, v2 = first_norm(
        ctx1,
        inputs,
        memory,
        memory_other,
        weights,
        row(self_out_bias),
        row(self_norm_gain),
        row(self_norm_bias),
        head_biases,
    )
    ctx2, log2 = cross_forward(q2, k2, v2)
    own = [planes_feed[0]] + [after(piece, ctx2) for piece in planes_feed[1:]]
    w_feed = assemble(info, planes_feed + [swap(piece, 1, 0) for piece in own])
    feed_halves = Halves((1, 1), width // nd, 0)
    outputs, keep, send, du3, dhidden, normed2, inverse2, sums_feed, sums_hidden = feed(
        info,
        feed_halves,
        ctx2,
        first,
        cotangent,
        weights,
        w_feed,
        row(cross_out_bias),
        row(cross_norm_gain),
        row(cross_norm_bias),
        hidden_bias,
        row(feed_out_bias),
        row(feed_norm_gain),
        row(feed_norm_bias),
    )
    rounds = feed_halves.rounds
    got = swap(send, 1, 0)
    du2, db2, sums_second = feed_back(
        du3, dhidden, normed2, inverse2, w_feed, row(cross_norm_gain)
    )
    whole = [[(0, base), (1, base)] for base in feed_halves.bases]
    arrays, held, _ = halve(feed_halves, [after(keep, db2), got], whole, None, 0)
    db2 = after(db2, arrays[0])
    dq2, dk2, dv2 = cross_backward(q2, k2, v2, ctx2, log2, db2, weights)
    middle_halves, (du1, db1, memory_own, memory_back, keep, send) = middle(
        info,
        (du2, dq2, dk2, dv2, db2, sums_second, sums_feed, sums_hidden),
        normed1,
        inverse1,
        first,
        memory,
        memory_other,
        ctx2,
        ctx1,
        weights,
        row(self_norm_gain),
    )
    arrays[0] = after(arrays[0], db1)
    for index in range(1, rounds):
        arrays, held, _ = halve(feed_halves, arrays, held, None, index)
    got = swap(after(send, arrays[0]), 1, 0)
    db1 = after(db1, arrays[0])
    pairs = width // PAIR // 2
    operands = (info, q1, k1, v1, k1o, v1o, ctx1, log1)
    grads_early = self_backward(*operands, db1, weights, 0, pairs)
    arrays[0] = after(arrays[0], grads_early[0])
    block = feed_in.shape[0]
    feed_segments = list(zip(feed_halves.sizes, held))
    feed_arrays = arrays
    for bit in reversed(bits[1:]):
        feed_arrays, feed_segments, _ = line_round(feed_arrays, feed_segments, None, bit)
    whole = [[(0, base), (1, base)] for base in middle_halves.bases]
    rider = [(0, middle_halves.main), (1, middle_halves.main)]
    keep = after(keep, feed_arrays[0])
    arrays, held, rider = halve(middle_halves, [keep, got], whole, rider, 0)
    db1 = after(db1, arrays[0])
    grads_late = list(self_backward(*operands, db1, weights, pairs, pairs))
    arrays[0] = after(arrays[0], grads_late[0])
    for index in range(1, rounds):
        arrays, held, rider = halve(middle_halves, arrays, held, rider, index)
    grads_late[0] = after(grads_late[0], arrays[0])
    self_halves, (inputs_back, keep, send) = self_grads(
        info, inputs, inputs_other, grads_early, grads_late, weights
    )
    send = after(send, *arrays, *feed_arrays)
    got = swap(send, 1, 0)
    inputs_got = hand_over(after(inputs_back, send), 1, -1)
    arrays[0] = after(arrays[0], send)
    segments = list(zip(middle_halves.sizes, held))
    rider = (middle_halves.rider, rider)
    for bit in reversed(bits[1:]):
        arrays, segments, rider = line_round(arrays, segments, rider, bit)
    keep = after(keep, arrays[0])

    size = self_halves.sizes[0]
    end = (self_halves.rider, [(0, self_halves.main), (1, self_halves.main)])
    places = [self_halves.place(0, j)[0] for j in range(nd // 2)]
    parts = add_rows([keep, got], [[(size, [(0, lo), (1, lo)]), end] for lo in places])
    planes = [parts[0]] + [swap(part, 2 * j, 0) for j, part in enumerate(parts) if j]
    planes[0] = after(planes[0], *arrays, inputs_got)
    at = range(len(planes))
    rows = 3 * block
    end = (self_halves.rider, [(p, size) for p in at])
    lines = add_rows(planes, [[(rows, [(p, k * rows) for p in at]), end] for k in range(nt)])
    lines = line_swaps(lines)
    arrays[0] = after(arrays[0], lines[0])
    arrays, segments, rider = line_round(arrays, segments, rider, 1)
    riding = memory_back.shape[1] == feed_arrays[0].shape[1]
    feed_arrays[0] = after(feed_arrays[0], lines[0])
    feed_arrays, feed_segments, _ = line_round(
        feed_arrays, feed_segments, None, 1, memory_back if riding else None
    )

    grad_feed_in, grad_feed_out = add_rows(
        feed_arrays[:2], [[(block, terms)] for _, terms in feed_segments], F32
    )
    if riding:
        memory_got = feed_arrays[1][2 * block :]
    else:
        memory_got = swap(after(memory_back, lines[0]), 0, 1)
    grad_memory = memory_own + memory_got.astype(F32)
    grad_inputs = input_grads(du1, grads_early[:3], grads_late[:3], weights, inputs_got)
    lines[0] = after(lines[0], grad_inputs, grad_feed_in)
    plans = [
        [(block, [(array, lo + i * block) for array, lo in terms])]
        for count, (_, terms) in zip(middle_halves.groups, segments)
        for i in range(count)
    ]
    plans.append([rider])
    cuts = [(i * block, block) for i in range(3)] + [(rows, self_halves.rider)]
    plans += [[(n, [(3 + k, lo) for k in range(nt)])] for lo, n in cuts]
    sums = add_rows(arrays + lines, plans, F32)
    grad_middle, early = sums[:5], sums[5]
    grad_self, late_sums = sums[6:9], sums[9]
    early = early.reshape(nt, 16, columns).transpose(1, 0, 2).reshape(16, width)
    late_sums = late_sums[: 2 * nt].reshape(2, width)

    def mine(vector):
        count = vector.shape[0] // nt
        return lax.dynamic_slice_in_dim(vector, me_t * count, count)

    return (
        outputs,
        grad_inputs,
        grad_memory,
        grad_self[0],
        mine(late_sums[0]),
        grad_self[1],
        grad_self[2],
        mine(late_sums[1]),
        grad_middle[0].T,
        early[0],
        early[1],
        early[2],
        grad_middle[1],
        mine(early[9]),
        grad_middle[2],
        grad_middle[3],
        mine(early[10]),
        grad_middle[4].T,
        early[3],
        early[4],
        early[5],
        grad_feed_in,
        mine(early[11:15].reshape(-1)),
        grad_feed_out.T,
        early[6],
        early[7],
        early[8],
    )


def solution(mesh):
    placed = (
        P(("dp", "tensor"), None),
        P(("dp", "tensor"), None),
        P("dp"),
        P("dp", "tensor"),
        P("tensor"),
        P("dp", "tensor"),
        P("dp", "tensor"),
        P("tensor"),
        P("tensor", "dp"),
        P(),
        P(),
        P(),
        P("dp", "tensor"),
        P("tensor"),
        P("dp", "tensor"),
        P("dp", "tensor"),
        P("tensor"),
        P("tensor", "dp"),
        P(),
        P(),
        P(),
        P("dp", "tensor"),
        P("tensor"),
        P("tensor", "dp"),
        P(),
        P(),
        P(),
        P(("dp", "tensor"), None),
    )
    return jax.shard_map(
        on_device,
        mesh=mesh,
        in_specs=placed,
        out_specs=(
            P(("dp", "tensor"), None),
            P(("dp", "tensor"), None),
            P(("dp", "tensor"), None),
            P("dp", "tensor"),
            P("tensor"),
            P("dp", "tensor"),
            P("dp", "tensor"),
            P("tensor"),
            P("tensor", "dp"),
            P(),
            P(),
            P(),
            P("dp", "tensor"),
            P("tensor"),
            P("dp", "tensor"),
            P("dp", "tensor"),
            P("tensor"),
            P("tensor", "dp"),
            P(),
            P(),
            P(),
            P("dp", "tensor"),
            P("tensor"),
            P("tensor", "dp"),
            P(),
            P(),
            P(),
        ),
        check_vma=False,
    )
```

```python
import functools

import jax
import jax.numpy as jnp
from jax import lax
from jax.experimental import pallas as pl
from jax.experimental.pallas import tpu as pltpu
from jax.sharding import PartitionSpec as P

HD = 64
LEN = 1024
MEM = 256
PAIR = 128
BLOCK = 256
BACK_BLOCK = 512

EPSILON = 1e-05
MASKED = -1e30
SCALE = float(HD) ** (-0.5)

F32 = jnp.float32
BF16 = jnp.bfloat16
NN = (((1,), (0,)), ((), ()))
NT = (((1,), (1,)), ((), ()))
TN = (((0,), (0,)), ((), ()))
SMEM = pl.BlockSpec(memory_space=pltpu.SMEM)
ANY = pl.BlockSpec(memory_space=pl.ANY)
VMEM = pl.BlockSpec(memory_space=pltpu.VMEM)


def mm(left_side, right_side, dims):
    return lax.dot_general(left_side, right_side, dims, preferred_element_type=F32)


def shaped(shape, dtype):
    return jax.ShapeDtypeStruct(shape, dtype)


def shaped_far(shape, dtype):
    return pltpu.HBM(shape, dtype)


def cost(macs, moved):
    return pl.CostEstimate(flops=macs // 64, bytes_accessed=moved // 64, transcendentals=0)


def limit(mebibytes):
    return pltpu.CompilerParams(vmem_limit_bytes=mebibytes << 20)


def far(*arrays):
    return [pltpu.with_memory_space_constraint(array, pltpu.HBM) for array in arrays]


def swap(array, dp_mask, tensor_mask):
    nd, nt = lax.axis_size("dp"), lax.axis_size("tensor")
    pairs = [
        (d * nt + t, (d ^ dp_mask) * nt + (t ^ tensor_mask)) for d in range(nd) for t in range(nt)
    ]
    return lax.ppermute(array, ("dp", "tensor"), pairs)


def hand_over(array, parity, step):
    nd, nt = lax.axis_size("dp"), lax.axis_size("tensor")
    pairs = [(d * nt + t, d * nt + t + step) for d in range(nd) for t in range(parity, nt, 2)]
    return lax.ppermute(array, ("dp", "tensor"), pairs)


def tree_sum(terms):
    while len(terms) > 1:
        terms = [terms[i] + terms[i + 1] for i in range(0, len(terms), 2)]
    return terms[0]


def doubled(line, bits):
    for bit in bits:
        line = jnp.concatenate([line, swap(line, 0, bit)])
    return line


def plane_bits(group):
    bits = [1 << i for i in range((lax.axis_size("dp") // 2).bit_length() - 1)]
    return bits if group % 2 == 0 else bits[::-1]


def grown(slots, pieces, bit):
    return [j | bit for j in slots], swap(pieces, 2 * bit, 0)


def merged(held):
    (slots, pieces), (more_slots, more) = held
    return slots + more_slots, jnp.concatenate([pieces, more])


class Halves:
    def __init__(self, groups, r, rider):
        self.planes, self.nt = lax.axis_size("dp") // 2, lax.axis_size("tensor")
        self.groups, self.r, self.rider = groups, r, rider
        self.rounds = self.planes.bit_length() - 1
        self.sizes = [self.nt * count * r for count in groups]
        self.bases = [self.planes * sum(self.sizes[:g]) for g in range(len(groups))]
        self.main = self.planes * sum(self.sizes)
        self.total = self.main + rider

    def bit(self, group, index):
        return 1 << (index if group % 2 == 0 else self.rounds - 1 - index)

    def place(self, i, j):
        group = 0
        while i >= self.groups[group]:
            i -= self.groups[group]
            group += 1
        bits = [self.bit(group, index) for index in range(self.rounds)]
        position = sum((j & b > 0) << (self.rounds - 1 - n) for n, b in enumerate(bits))
        count = self.groups[group]
        return self.bases[group] + position * self.sizes[group] + i * self.r, count * self.r

    def split(self, arrays, held, rider, index):
        stay, sent = [], []
        for group, terms in enumerate(held):
            rows = (self.planes >> (index + 1)) * self.sizes[group]
            stay.append([(rows, terms)])
            sent.append([(rows, [(array, lo + rows) for array, lo in terms])])
        if self.rider:
            sent[-1].append((self.rider, rider))
        return stay + sent


def add_rows_kernel(*refs, plans, count):
    for out, plan in zip(refs[count:], plans):
        at = 0
        for rows, terms in plan:
            total = tree_sum([refs[i][lo : lo + rows, :].astype(F32) for i, lo in terms])
            out[at : at + rows, :] = total.astype(out.dtype)
            at += rows


def add_rows(arrays, plans, dtype=BF16):
    width = arrays[0].shape[1]
    moved = sum(array.size * array.dtype.itemsize for array in arrays)
    return pl.pallas_call(
        functools.partial(add_rows_kernel, plans=plans, count=len(arrays)),
        out_shape=tuple(shaped((sum(n for n, _ in plan), width), dtype) for plan in plans),
        in_specs=[VMEM] * len(arrays),
        out_specs=(VMEM,) * len(plans),
        compiler_params=limit(20),
        cost_estimate=cost(0, 2 * moved),
    )(*arrays)


def finish_kernel(info, *refs, plans, count, nt):
    outs = refs[count:-2]
    early, late = refs[-2:]
    w = early.shape[1]
    add_rows_kernel(*refs[:count], *outs[:-3], early, late, plans=plans, count=count)
    rows, mine, hidden = outs[-3:]
    for q in range(nt):
        lanes = slice(q * w, q * w + w)
        rows[:, lanes] = early[16 * q : 16 * q + 16, :]
    for k in range(4):
        block = 4 * info[3] + k
        at = 16 * lax.rem(block, nt) + 11 + lax.div(block, nt)
        hidden[:, k * w : k * w + w] = early[pl.ds(at, 1), :]
    for i, (source, at) in enumerate(
        ((early, 16 * info[3] + 9), (early, 16 * info[3] + 10), (late, info[3]), (late, nt + info[3]))
    ):
        mine[i : i + 1, :] = source[pl.ds(at, 1), :]


def finish(info, arrays, plans, nt, width):
    w = arrays[0].shape[1]
    sizes = [sum(n for n, _ in plan) for plan in plans]
    shapes = [(n, w) for n in sizes[:-2]] + [(16, width), (4, w), (1, 4 * w)]
    return pl.pallas_call(
        functools.partial(finish_kernel, plans=plans, count=len(arrays), nt=nt),
        out_shape=tuple(shaped(shape, F32) for shape in shapes),
        in_specs=[SMEM] + [VMEM] * len(arrays),
        out_specs=(VMEM,) * len(shapes),
        scratch_shapes=[pltpu.VMEM((n, w), F32) for n in sizes[-2:]],
        compiler_params=limit(20),
        cost_estimate=cost(0, 16 * w * sum(sizes)),
    )(info, *arrays)


def halve(halves, arrays, held, rider, index):
    groups = len(halves.groups)
    outs = list(add_rows(arrays, halves.split(arrays, held, rider, index)))
    stay, sent = outs[:groups], outs[groups:]
    got = [swap(part, 2 * halves.bit(group, index), 0) for group, part in enumerate(sent)]
    held = [[(group, 0), (groups + group, 0)] for group in range(groups)]
    end = sent[-1].shape[0] - halves.rider
    rider = [(2 * groups, end), (2 * groups - 1, end)]
    return stay + got + sent[-1:], held, rider


def line_round(arrays, segments, rider, bit, extra=None):
    stay, sent, after_round, lo = [], [], [], 0
    for rows, terms in segments:
        half = rows // 2
        stay.append((half, terms))
        sent.append((half, [(array, first + half) for array, first in terms]))
        after_round.append((half, [(0, lo), (1, lo)]))
        lo += half
    if rider:
        sent.append(rider)
        rider = (rider[0], [(1, lo), (2, lo)])
    if extra is not None:
        sent.append((extra.shape[0], [(len(arrays), 0)]))
        arrays = arrays + [extra]
    stay, sent = add_rows(arrays, [stay, sent])
    return [stay, swap(sent, 0, bit), sent], after_round, rider


def line_swaps(parts):
    return [parts[0]] + [swap(part, 0, k) for k, part in enumerate(parts) if k]


def after(array, *others):
    return lax.optimization_barrier((array,) + others)[0]


def aligned(r, w):
    return w % PAIR == 0 and r % 16 == 0


def assemble_kernel(info, *refs, entries):
    whole = refs[-1]
    for piece, (core, slots, first) in zip(refs, entries):
        _, nt, n, r, w = piece.shape
        for k, j in enumerate(slots):
            d = jnp.bitwise_xor(info[2], 2 * j + core)
            rows = pl.ds(pl.multiple_of(d * r, r), r)
            for s in range(nt):
                t = jnp.bitwise_xor(info[3], s)
                columns = pl.ds(pl.multiple_of(t * w, w), w)
                for i in range(n):
                    whole[first + i, rows, columns] = piece[k, s, i]


def assemble(info, arrays, entries):
    _, nt, _, r, w = arrays[0].shape
    nd = lax.axis_size("dp")
    count = max(entry[2] + array.shape[2] for array, entry in zip(arrays, entries))
    if aligned(r, w):
        return pl.pallas_call(
            functools.partial(assemble_kernel, entries=entries),
            out_shape=shaped((count, nd * r, nt * w), BF16),
            in_specs=[SMEM] + [VMEM] * len(arrays),
            out_specs=VMEM,
            compiler_params=limit(18),
            cost_estimate=cost(0, 4 * count * nd * r * nt * w),
        )(info, *arrays)
    wholes = []
    for first in sorted({entry[2] for entry in entries}):
        found = {}
        for array, (core, slots, at) in zip(arrays, entries):
            if at == first:
                found.update({2 * j + core: array[k] for k, j in enumerate(slots)})
        full = jnp.stack([found[d] for d in range(nd)])
        full = jnp.take(full, jnp.bitwise_xor(jnp.arange(nd), info[2]), axis=0)
        full = jnp.take(full, jnp.bitwise_xor(jnp.arange(nt), info[3]), axis=1)
        wholes.append(full.transpose(2, 0, 3, 1, 4).reshape(-1, nd * r, nt * w))
    return jnp.concatenate(wholes)


def disperse(info, halves, scratch, i, t, s, keep, send):
    for j in range(halves.planes):
        base, stride = halves.place(i, j)
        lo = base + s * stride
        if not isinstance(s, int):
            lo = pl.multiple_of(lo, 16)
        for c in range(2):
            d = jnp.bitwise_xor(info[2], 2 * j + c)
            rows = pl.ds(pl.multiple_of(d * halves.r, halves.r), halves.r)
            (keep, send)[c][pl.ds(lo, halves.r), :] = scratch[rows, t]


def disperse_whole(info, halves, scratch, i, keep, send):
    w = keep.shape[1]
    for s in range(halves.nt):
        t = jnp.bitwise_xor(info[3], s)
        disperse(info, halves, scratch, i, pl.ds(pl.multiple_of(t * w, w), w), s, keep, send)


def disperse_plain(info, halves, whole, rider):
    nd, nt = 2 * halves.planes, halves.nt
    n, r, w = whole.shape[0], halves.r, whole.shape[2] // nt
    full = whole.reshape(n, nd, r, nt, w).transpose(1, 3, 0, 2, 4)
    full = jnp.take(full, jnp.bitwise_xor(jnp.arange(nd), info[2]), axis=0)
    full = jnp.take(full, jnp.bitwise_xor(jnp.arange(nt), info[3]), axis=1)
    full = full.reshape(nd // 2, 2, nt, n, r, w)
    flats = []
    for c in range(2):
        rows, first = [], 0
        for count in halves.groups:
            order = sorted(range(halves.planes), key=lambda j: halves.place(first, j)[0])
            group = jnp.stack([full[j, c, :, first : first + count] for j in order])
            rows.append(group.reshape(-1, w))
            first += count
        flats.append(jnp.concatenate(rows + [rider]))
    return flats


def pack_kernel(*refs, blocks):
    out = refs[-1]
    r, w = refs[0].shape
    for i, block in enumerate(refs[:blocks]):
        out[i * r : (i + 1) * r, :] = block[...]
    row = lax.broadcasted_iota(jnp.int32, (16, w), 0)
    filled = jnp.zeros((16, w), F32)
    count = 0
    for vector in refs[blocks:-1]:
        for i in range(vector.shape[0]):
            filled = jnp.where(row == count, vector[i : i + 1, :].astype(F32), filled)
            count += 1
    out[blocks * r :, :] = filled.astype(BF16)


def pack(blocks, vectors):
    r, w = blocks[0].shape
    if aligned(r, w):
        return pl.pallas_call(
            functools.partial(pack_kernel, blocks=len(blocks)),
            out_shape=shaped((len(blocks) * r + 16, w), BF16),
            in_specs=[VMEM] * (len(blocks) + len(vectors)),
            out_specs=VMEM,
            cost_estimate=cost(0, 32 * r * w),
        )(*blocks, *[vector.reshape(-1, w) for vector in vectors])
    rows = jnp.concatenate(vectors).reshape(-1, w)
    return jnp.concatenate(list(blocks) + [jnp.pad(rows, ((0, 16 - rows.shape[0]), (0, 0)))])


def spread_kernel(info, riders, small, hidden):
    nt, _, w = riders.shape
    for s in range(nt):
        t = jnp.bitwise_xor(info[3], s)
        block = riders[s].astype(F32)
        small[:, pl.ds(pl.multiple_of(t * w, w), w)] = block
        for i in range(4):
            hidden[:, pl.ds(pl.multiple_of((4 * t + i) * w, w), w)] = block[4 + i : 5 + i]


def spread(info, riders):
    nt, _, w = riders.shape
    if aligned(16, w):
        return pl.pallas_call(
            spread_kernel,
            out_shape=(shaped((16, nt * w), F32), shaped((1, 4 * nt * w), F32)),
            in_specs=[SMEM, VMEM],
            out_specs=(VMEM, VMEM),
            cost_estimate=cost(0, 64 * nt * w),
        )(info, riders)
    full = jnp.take(riders, jnp.bitwise_xor(jnp.arange(nt), info[3]), axis=0).astype(F32)
    return full.transpose(1, 0, 2).reshape(16, nt * w), full[:, 4:8].reshape(1, -1)


def norm_forward(summed):
    row_mean = jnp.mean(summed, axis=-1, keepdims=True)
    centred = summed - row_mean
    variance = jnp.mean(centred * centred, axis=-1, keepdims=True)
    inverse = lax.rsqrt(variance + EPSILON)
    return centred * inverse, inverse


def norm_backward(grad_out, normed, inverse, norm_gain):
    grad_normed = grad_out * norm_gain
    return inverse * (
        grad_normed
        - jnp.mean(grad_normed, axis=-1, keepdims=True)
        - normed * jnp.mean(grad_normed * normed, axis=-1, keepdims=True)
    )


def column_sum(values):
    return jnp.sum(values.astype(F32), axis=0, keepdims=True)


def head_lanes(e):
    lane = lax.broadcasted_iota(jnp.int32, (1, PAIR), 1)
    chosen = (lane < HD) if e == 0 else (lane >= HD)
    return jnp.where(chosen, 1.0, 0.0)


def join_heads(first, second):
    lane = lax.broadcasted_iota(jnp.int32, first.shape, 1)
    return jnp.where(lane < HD, first, second)


def attend_forward(q, segments, contexts, logs, lo):
    rows = slice(lo, lo + BLOCK)
    results = []
    for e in range(2):
        query = q[rows, :] * head_lanes(e).astype(BF16)
        scores = [edit(mm(query, k, NT)) for k, _, edit in segments]
        peak = functools.reduce(
            jnp.maximum, [jnp.max(piece, axis=-1, keepdims=True) for piece in scores]
        )
        total = None
        for piece, (_, v, _) in zip(scores, segments):
            weights = jnp.exp(piece - peak).astype(BF16)
            wide = jnp.concatenate([v, jnp.ones(v.shape, BF16)], axis=1)
            part = mm(weights, wide, NN)
            total = part if total is None else total + part
        row_total = total[:, PAIR:]
        results.append((total[:, :PAIR] / row_total, peak + jnp.log(row_total)))
    contexts[rows, :] = join_heads(results[0][0], results[1][0]).astype(BF16)
    logs[rows, :] = join_heads(results[0][1], results[1][1])


def attend_backward(q, grad, ctx, logs, segments, grad_query, lo):
    rows = slice(lo, lo + BACK_BLOCK)
    grad_rows = grad[rows, :]
    product = grad_rows.astype(F32) * ctx[rows, :].astype(F32)
    query_rows = q[rows, :]
    query_turned = jnp.transpose(query_rows)
    grad_turned = jnp.transpose(grad_rows)
    total = None
    for e in range(2):
        lanes = head_lanes(e)
        low_lanes = lanes.astype(BF16)
        delta = jnp.sum(product * lanes, axis=-1, keepdims=True)
        row_log = logs[rows, e * HD : e * HD + 1]
        grad_low = grad_rows * low_lanes
        query = query_rows * low_lanes
        for k, v, edit, add in segments:
            weights = jnp.exp(edit(mm(query, k, NT)) - row_log)
            slope = mm(grad_low, v, NT) - delta
            grad_scores = (weights * slope).astype(BF16)
            part = mm(grad_scores, k * low_lanes, NN)
            total = part if total is None else total + part
            head = slice(e * HD, e * HD + HD)
            add(
                head,
                mm(query_turned[head], grad_scores, NN),
                mm(grad_turned[head], weights.astype(BF16), NN),
            )
    grad_query[rows, :] = (total * SCALE).astype(BF16)


def same(scores):
    return scores


def masked(lo, col_lo, prefix_len):
    def edit(scores):
        row = lo + lax.broadcasted_iota(jnp.int32, scores.shape, 0)
        col = col_lo + lax.broadcasted_iota(jnp.int32, scores.shape, 1)
        allowed = col <= row
        if prefix_len is not None:
            allowed = allowed | (col < prefix_len)
        return jnp.where(allowed, scores, MASKED)

    return edit


def adder(keys, values, col_lo, width):
    def add(head, part_keys, part_values):
        keys[head, col_lo : col_lo + width] += part_keys
        values[head, col_lo : col_lo + width] += part_values

    return add


def self_forward_kernel(info, q, k, v, ko, vo, ctx, logs):
    tokens = q.shape[0]

    @pl.when(info[0] == 0)
    def _():
        for lo in range(0, tokens, BLOCK):
            attend_forward(q, [(k[...], v[...], masked(lo, 0, info[1]))], ctx, logs, lo)

    @pl.when(info[0] != 0)
    def _():
        for lo in range(0, tokens, BLOCK):
            near = slice(lo, lo + BLOCK)
            segments = [(ko[...], vo[...], same)]
            if lo:
                segments.append((k[:lo, :], v[:lo, :], same))
            segments.append((k[near, :], v[near, :], masked(lo, lo, None)))
            attend_forward(q, segments, ctx, logs, lo)


def self_backward_kernel(
    info, q, k, v, ko, vo, ctx, logs, low, w, dq, dk, dv, dko, dvo, ak, av, ako, avo, grad
):
    tokens = q.shape[0]
    ak[...] = jnp.zeros_like(ak)
    av[...] = jnp.zeros_like(av)
    grad[...] = mm(low[...], w[0], NN).astype(BF16)

    @pl.when(info[0] == 0)
    def _():
        for lo in range(0, tokens, BACK_BLOCK):
            segments = [(k[...], v[...], masked(lo, 0, info[1]), adder(ak, av, 0, tokens))]
            attend_backward(q, grad, ctx, logs, segments, dq, lo)

    @pl.when(info[0] != 0)
    def _():
        ako[...] = jnp.zeros_like(ako)
        avo[...] = jnp.zeros_like(avo)
        for lo in range(0, tokens, BACK_BLOCK):
            near = slice(lo, lo + BACK_BLOCK)
            segments = [(ko[...], vo[...], same, adder(ako, avo, 0, tokens))]
            if lo:
                segments.append((k[:lo, :], v[:lo, :], same, adder(ak, av, 0, lo)))
            segments.append(
                (k[near, :], v[near, :], masked(lo, lo, None), adder(ak, av, lo, BACK_BLOCK))
            )
            attend_backward(q, grad, ctx, logs, segments, dq, lo)
        dko[...] = jnp.transpose(ako[...]).astype(BF16)
        dvo[...] = jnp.transpose(avo[...]).astype(BF16)

    dk[...] = jnp.transpose(ak[...]).astype(BF16)
    dv[...] = jnp.transpose(av[...]).astype(BF16)


def cross_forward_kernel(q, k, v, ctx, logs):
    for lo in range(0, q.shape[0], BLOCK):
        attend_forward(q, [(k[...], v[...], same)], ctx, logs, lo)


def cross_backward_kernel(q, k, v, ctx, logs, low, w, dq, dk, dv, ak, av, grad):
    ak[...] = jnp.zeros_like(ak)
    av[...] = jnp.zeros_like(av)
    grad[...] = mm(low[...], w[0], NN).astype(BF16)
    for lo in range(0, q.shape[0], BACK_BLOCK):
        segments = [(k[...], v[...], same, adder(ak, av, 0, k.shape[0]))]
        attend_backward(q, grad, ctx, logs, segments, dq, lo)
    dk[...] = jnp.transpose(ak[...]).astype(BF16)
    dv[...] = jnp.transpose(av[...]).astype(BF16)


def lanes_of(rows, first=0):
    return pl.BlockSpec((rows, PAIR), lambda h: (0, first + h))


def output_columns(slot, width, first=0):
    return pl.BlockSpec((1, width, PAIR), lambda h: (slot, 0, first + h))


def self_forward(info, q, k, v, ko, vo):
    tokens, width = q.shape
    row = lanes_of(tokens)
    return pl.pallas_call(
        self_forward_kernel,
        grid=(width // PAIR,),
        out_shape=(shaped((tokens, width), BF16), shaped_far((tokens, width), F32)),
        in_specs=[SMEM] + [row] * 5,
        out_specs=(row, row),
        compiler_params=limit(16),
        cost_estimate=cost(width // HD * tokens * tokens * 2 * 256 * 2, 5 << 20),
    )(info, q, k, v, ko, vo)


def self_backward(info, q, k, v, ko, vo, ctx, logs, low, w, first, pairs):
    tokens, width = q.shape
    row = lanes_of(tokens, first)
    out = shaped((tokens, pairs * PAIR), BF16)
    return pl.pallas_call(
        self_backward_kernel,
        grid=(pairs,),
        out_shape=(out,) * 5,
        in_specs=[SMEM] + [row] * 7 + [VMEM, output_columns(3, width, first)],
        out_specs=(lanes_of(tokens),) * 5,
        scratch_shapes=[pltpu.VMEM((PAIR, tokens), F32)] * 4 + [pltpu.VMEM((tokens, PAIR), BF16)],
        compiler_params=limit(16),
        cost_estimate=cost(width // HD * tokens * tokens * 256 * 5, 8 << 20),
    )(info, *far(q, k, v, ko, vo, ctx, logs), low, *far(w))


def cross_forward(q, k, v):
    tokens, width = q.shape
    rows = k.shape[0]
    return pl.pallas_call(
        cross_forward_kernel,
        grid=(width // PAIR,),
        out_shape=(shaped((tokens, width), BF16), shaped_far((tokens, width), F32)),
        in_specs=[lanes_of(tokens), lanes_of(rows), lanes_of(rows)],
        out_specs=(lanes_of(tokens), lanes_of(tokens)),
        compiler_params=limit(16),
        cost_estimate=cost(width // HD * tokens * rows * 256 * 2, 3 << 20),
    )(q, k, v)


def cross_backward(q, k, v, ctx, logs, low, w):
    tokens, width = q.shape
    rows = k.shape[0]
    small = shaped((rows, width), BF16)
    return pl.pallas_call(
        cross_backward_kernel,
        grid=(width // PAIR,),
        out_shape=(shaped((tokens, width), BF16), small, small),
        in_specs=[lanes_of(tokens), lanes_of(rows), lanes_of(rows)]
        + [lanes_of(tokens)] * 2
        + [VMEM, output_columns(7, width)],
        out_specs=(lanes_of(tokens), lanes_of(rows), lanes_of(rows)),
        scratch_shapes=[pltpu.VMEM((PAIR, rows), F32)] * 2 + [pltpu.VMEM((tokens, PAIR), BF16)],
        compiler_params=limit(16),
        cost_estimate=cost(width // HD * tokens * rows * 256 * 5, 4 << 20),
    )(*far(q, k, v, ctx, logs), low, *far(w))


def project_self_kernel(info, x, xo, wq, wk, wv, b, q, k, v, ko, vo):
    rows = x[...]
    q[...] = (mm(rows, wq[0], NN) + b[0:1, :]).astype(BF16) * jnp.asarray(SCALE, BF16)
    k[...] = mm(rows, wk[0], NN).astype(BF16)
    v[...] = (mm(rows, wv[0], NN) + b[1:2, :]).astype(BF16)

    @pl.when(info[0] != 0)
    def _():
        other = xo[...]
        ko[...] = mm(other, wk[0], NN).astype(BF16)
        vo[...] = (mm(other, wv[0], NN) + b[1:2, :]).astype(BF16)


def project_self(info, x, xo, w, b):
    low = shaped(x.shape, BF16)
    return pl.pallas_call(
        project_self_kernel,
        grid=(1,),
        out_shape=(low,) * 5,
        in_specs=[SMEM] + [VMEM] * 2 + [matrix(i, x.shape[1]) for i in range(3)] + [VMEM],
        compiler_params=limit(16),
        cost_estimate=cost(5 * x.size * x.shape[1], 5 << 20),
    )(info, x, xo, w, w, w, b)


def first_norm_kernel(
    ctx, x, mem, memo, wo, wq, wk, wv, ob, gain, bias, b, first, normed, inverse, q, k, v
):
    summed = x[...].astype(F32) + mm(ctx[...], wo[0], NT) + ob[...].astype(F32)
    n, r = norm_forward(summed)
    out = n * gain[...].astype(F32) + bias[...].astype(F32)
    normed[...] = n
    inverse[...] = r
    first[...] = out
    q[...] = (mm(out.astype(BF16), wq[0], NN) + b[2:3, :]).astype(BF16) * jnp.asarray(SCALE, BF16)
    rows = mem.shape[0]
    for source, lo in ((mem, 0), (memo, rows)):
        k[lo : lo + rows, :] = mm(source[...], wk[0], NN).astype(BF16)
        v[lo : lo + rows, :] = (mm(source[...], wv[0], NN) + b[3:4, :]).astype(BF16)


def first_norm(ctx, x, mem, memo, w, ob, gain, bias, b):
    rows = 2 * mem.shape[0]
    tokens, width = x.shape
    full = shaped(x.shape, F32)
    return pl.pallas_call(
        first_norm_kernel,
        grid=(1,),
        out_shape=(
            full,
            shaped_far(x.shape, F32),
            shaped_far((tokens, 1), F32),
            shaped(x.shape, BF16),
            shaped((rows, width), BF16),
            shaped((rows, width), BF16),
        ),
        in_specs=[VMEM] * 4 + [matrix(i, width) for i in range(3, 7)] + [VMEM] * 4,
        compiler_params=limit(16),
        cost_estimate=cost(3 * x.size * width, 8 << 20),
    )(ctx, x, mem, memo, w, w, w, w, ob, gain, bias, b)


def feed_kernel(
    info,
    ctx,
    first,
    cot,
    wo,
    wf,
    ob,
    gain2,
    bias2,
    fib,
    fob,
    gain3,
    bias3,
    out,
    keep,
    send,
    du3,
    dhid,
    normed,
    inverse,
    sums,
    hsum,
    act,
    slope,
    acc,
    second,
    db3,
    turn,
    *,
    halves,
):
    tokens, width = first.shape
    w = keep.shape[1]
    summed = first[...] + mm(ctx[...], wo[0], NT) + ob[...].astype(F32)
    n2, r2 = norm_forward(summed)
    normed[...] = n2
    inverse[...] = r2
    out2 = n2 * gain2[...].astype(F32) + bias2[...].astype(F32)
    second[...] = out2.astype(BF16)
    acc[...] = out2 + fob[...].astype(F32)

    @pl.loop(0, halves.nt, unroll=2)
    def _(t):
        cols = pl.ds(pl.multiple_of(t * w, w), w)
        hidden = mm(second[...], wf[0, :, cols], NN) + fib[:, cols]
        gate = 1.0 / (1.0 + jnp.exp(-hidden))
        active = (hidden * gate).astype(BF16)
        act[:, cols] = active
        slope[:, cols] = (gate * (1.0 + hidden * (1.0 - gate))).astype(BF16)
        acc[...] += mm(active, wf[1, :, cols], NT)

    n3, r3 = norm_forward(acc[...])
    out[...] = (n3 * gain3[...].astype(F32) + bias3[...].astype(F32)).astype(BF16)
    dy = cot[...].astype(F32)
    grad3 = norm_backward(dy, n3, r3, gain3[...].astype(F32))
    low3 = grad3.astype(BF16)
    sums[0:1, :] = column_sum(low3)
    sums[1:2, :] = column_sum(dy * n3)
    sums[2:3, :] = column_sum(dy)
    sums[3:8, :] = jnp.zeros((5, width), F32)
    du3[...] = grad3
    db3[...] = low3

    @pl.loop(0, halves.nt, unroll=2)
    def _(t):
        cols = pl.ds(pl.multiple_of(t * w, w), w)
        s = jnp.bitwise_xor(info[3], t)
        everything = slice(None)
        back = db3[...]
        dact = mm(back, wf[1, :, cols], NN)
        part = (dact * slope[:, cols].astype(F32)).astype(BF16)
        dhid[:, cols] = part
        hsum[:, cols] = column_sum(part)
        turn[0] = mm(second[...], part, TN).astype(BF16)
        disperse(info, halves, turn.at[0], 0, everything, s, keep, send)
        turn[1] = mm(back, act[:, cols], TN).astype(BF16)
        disperse(info, halves, turn.at[1], 1, everything, s, keep, send)


def feed_back_kernel(du3, dhid, normed, inverse, wf, gain, du2, db2, sums):
    dsecond = du3[...] + mm(dhid[...], wf[0], NT)
    n = normed[...]
    grad = norm_backward(dsecond, n, inverse[...], gain[...].astype(F32))
    low = grad.astype(BF16)
    du2[...] = grad
    db2[...] = low
    sums[0:1, :] = column_sum(low)
    sums[1:2, :] = column_sum(dsecond * n)
    sums[2:3, :] = column_sum(dsecond)
    sums[3:8, :] = jnp.zeros((5, du2.shape[1]), F32)


def feed_back(du3, dhid, normed, inverse, wf, gain):
    tokens, width = du3.shape
    wide = wf.shape[2]
    return pl.pallas_call(
        feed_back_kernel,
        grid=(1,),
        out_shape=(shaped(du3.shape, F32), shaped(du3.shape, BF16), shaped((8, width), F32)),
        in_specs=[VMEM] * 4 + [pl.BlockSpec((1, width, wide), lambda h: (0, 0, 0)), VMEM],
        compiler_params=limit(16),
        cost_estimate=cost(tokens * width * wide, 8 << 20),
    )(du3, dhid, normed, inverse, wf, gain)


def matrix(slot, width):
    return pl.BlockSpec((1, width, width), lambda h: (slot, 0, 0))


def feed(info, halves, ctx, first, cot, wo, wf, ob, gain2, bias2, fib, fob, gain3, bias3):
    tokens, width = first.shape
    wide = wf.shape[2]
    w = wide // halves.nt
    flat = shaped((halves.total, w), BF16)
    return pl.pallas_call(
        functools.partial(feed_kernel, halves=halves),
        grid=(1,),
        out_shape=(
            shaped(first.shape, BF16),
            flat,
            flat,
            shaped(first.shape, F32),
            shaped((tokens, wide), BF16),
            shaped(first.shape, F32),
            shaped((tokens, 1), F32),
            shaped((8, width), F32),
            shaped((1, wide), F32),
        ),
        in_specs=[SMEM] + [VMEM] * 3 + [matrix(7, width)] + [VMEM] * 8,
        scratch_shapes=[
            pltpu.VMEM((tokens, wide), BF16),
            pltpu.VMEM((tokens, wide), BF16),
            pltpu.VMEM((tokens, width), F32),
            pltpu.VMEM((tokens, width), BF16),
            pltpu.VMEM((tokens, width), BF16),
            pltpu.VMEM((2, width, w), BF16),
        ],
        compiler_params=limit(28),
        cost_estimate=cost(6 * tokens * width * wide, 14 << 20),
    )(info, ctx, first, cot, wo, wf, ob, gain2, bias2, fib, fob, gain3, bias3)


def middle_kernel(
    info,
    du2,
    dq2,
    dk2,
    dv2,
    db2,
    sums2,
    sums3,
    hsum,
    normed,
    inverse,
    first,
    mem,
    memo,
    ctx2,
    ctx1,
    wq,
    wk,
    wv,
    gain,
    *outs,
    halves,
):
    du1, db1, own, other = outs[:4]
    turn, riders = outs[-2:]
    rows, width = mem.shape
    dfirst = du2[...] + mm(dq2[...], wq[0], NT)
    n = normed[...]
    grad = norm_backward(dfirst, n, inverse[...], gain[...].astype(F32))
    low = grad.astype(BF16)
    du1[...] = grad
    db1[...] = low
    riders[0:1, :] = column_sum(low)
    riders[1:2, :] = column_sum(dfirst * n)
    riders[2:3, :] = column_sum(dfirst)
    riders[3:6, :] = sums2[0:3, :]
    riders[6:9, :] = sums3[0:3, :]
    riders[9:10, :] = column_sum(dq2[...])
    riders[10:11, :] = column_sum(dv2[...])
    for i in range(4):
        riders[11 + i : 12 + i, :] = hsum[:, i * width : (i + 1) * width]
    riders[15:16, :] = jnp.zeros((1, width), F32)
    turn[0] = mm(low, ctx1[...], TN).astype(BF16)
    turn[1] = mm(first[...].astype(BF16), dq2[...], TN).astype(BF16)
    for slot, part in ((2, dk2), (3, dv2)):
        turn[slot] = (
            mm(mem[...], part[:rows, :], TN) + mm(memo[...], part[rows:, :], TN)
        ).astype(BF16)
    turn[4] = mm(db2[...], ctx2[...], TN).astype(BF16)
    back = mm(dk2[...], wk[0], NT) + mm(dv2[...], wv[0], NT)
    own[...] = back[:rows, :]
    other[...] = back[rows:, :].astype(BF16)
    if halves is None:
        outs[4][...] = turn[...]
        outs[5][...] = riders[...]
        return
    for i in range(5):
        disperse_whole(info, halves, turn.at[i], i, outs[4], outs[5])
    w = outs[4].shape[1]
    for target in outs[4:6]:
        for q in range(width // w):
            lo = halves.main + 16 * q
            target[lo : lo + 16, :] = riders[:, q * w : q * w + w].astype(BF16)


def middle(info, near, normed, inverse, first, mem, memo, ctx2, ctx1, w, gain):
    tokens, width = first.shape
    rows = mem.shape[0]
    nd, nt = lax.axis_size("dp"), lax.axis_size("tensor")
    r, columns = width // nd, width // nt
    halves = Halves((3, 2), r, 16 * nt)
    direct = aligned(r, columns)
    if direct:
        last = (shaped((halves.total, columns), BF16),) * 2
    else:
        last = (shaped((5, width, width), BF16), shaped((16, width), F32))
    outs = pl.pallas_call(
        functools.partial(middle_kernel, halves=halves if direct else None),
        grid=(1,),
        out_shape=(
            shaped_far(first.shape, F32),
            shaped(first.shape, BF16),
            shaped((rows, width), F32),
            shaped((rows, width), BF16),
        )
        + last,
        in_specs=[SMEM] + [VMEM] * 15 + [matrix(i, width) for i in (4, 5, 6)] + [VMEM],
        scratch_shapes=[pltpu.VMEM((5, width, width), BF16), pltpu.VMEM((16, width), F32)],
        compiler_params=limit(20),
        cost_estimate=cost(6 * first.size * width, 12 << 20),
    )(
        info,
        *near,
        *far(normed, inverse, first, mem, memo, ctx2, ctx1, w, w, w),
        gain,
    )
    if not direct:
        rider = outs[5].astype(BF16).reshape(16, nt, columns).transpose(1, 0, 2)
        outs = outs[:4] + tuple(disperse_plain(info, halves, outs[4], rider.reshape(-1, columns)))
    return halves, outs


def self_grads_kernel(
    info, x, xo, dqa, dka, dva, dkoa, dvoa, dqb, dkb, dvb, dkob, dvob, wk, wv, *outs, halves
):
    other = outs[0]
    turn, sums = outs[-2:]
    width = x.shape[1]
    both = lambda left, right: jnp.concatenate([left[...], right[...]], axis=1)
    dq, dk, dv = both(dqa, dqb), both(dka, dkb), both(dva, dvb)
    turn[0] = mm(x[...], dq, TN).astype(BF16)
    sums[0:1, :] = column_sum(dq)

    @pl.when(info[0] == 0)
    def _():
        turn[1] = mm(x[...], dk, TN).astype(BF16)
        turn[2] = mm(x[...], dv, TN).astype(BF16)
        sums[1:2, :] = column_sum(dv)
        other[...] = jnp.zeros_like(other)

    @pl.when(info[0] != 0)
    def _():
        dko, dvo = both(dkoa, dkob), both(dvoa, dvob)
        turn[1] = (mm(x[...], dk, TN) + mm(xo[...], dko, TN)).astype(BF16)
        turn[2] = (mm(x[...], dv, TN) + mm(xo[...], dvo, TN)).astype(BF16)
        sums[1:2, :] = column_sum(dv) + column_sum(dvo)
        other[...] = (mm(dko, wk[0], NT) + mm(dvo, wv[0], NT)).astype(BF16)

    if halves is None:
        outs[1][...] = turn[...]
        outs[2][...] = sums[...]
        return
    for i in range(3):
        disperse_whole(info, halves, turn.at[i], i, outs[1], outs[2])
    w = outs[1].shape[1]
    row = lax.broadcasted_iota(jnp.int32, (16, w), 0)
    filled = jnp.zeros((16, w), F32)
    for i in range(2):
        for t in range(width // w):
            piece = sums[i : i + 1, t * w : t * w + w]
            filled = jnp.where(row == i * (width // w) + t, piece, filled)
    for target in outs[1:3]:
        target[halves.main :, :] = filled.astype(BF16)


def self_grads(info, x, xo, early, late, w):
    width = x.shape[1]
    nd, nt = lax.axis_size("dp"), lax.axis_size("tensor")
    r, columns = width // nd, width // nt
    halves = Halves((3,), r, 16)
    direct = aligned(r, columns)
    if direct:
        last = (shaped((halves.total, columns), BF16),) * 2
    else:
        last = (shaped((3, width, width), BF16), shaped((8, width), F32))
    outs = pl.pallas_call(
        functools.partial(self_grads_kernel, halves=halves if direct else None),
        grid=(1,),
        out_shape=(shaped(x.shape, BF16),) + last,
        in_specs=[SMEM] + [VMEM] * 12 + [matrix(i, width) for i in (1, 2)],
        scratch_shapes=[pltpu.VMEM((3, width, width), BF16), pltpu.VMEM((8, width), F32)],
        compiler_params=limit(16),
        cost_estimate=cost(7 * x.size * width, 8 << 20),
    )(info, *far(x, xo), *early, *late, *far(w, w))
    if not direct:
        rider = outs[2][:2].astype(BF16).reshape(-1, columns)
        rider = jnp.pad(rider, ((0, 16 - rider.shape[0]), (0, 0)))
        outs = outs[:1] + tuple(disperse_plain(info, halves, outs[1], rider))
    return halves, outs


def input_grads_kernel(du1, dqa, dka, dva, dqb, dkb, dvb, wq, wk, wv, back, out):
    both = lambda left, right: jnp.concatenate([left[...], right[...]], axis=1)
    out[...] = (
        du1[...]
        + mm(both(dqa, dqb), wq[0], NT)
        + mm(both(dka, dkb), wk[0], NT)
        + mm(both(dva, dvb), wv[0], NT)
        + back[...].astype(F32)
    )


def input_grads(du1, early, late, w, back):
    return pl.pallas_call(
        input_grads_kernel,
        grid=(1,),
        out_shape=shaped(du1.shape, F32),
        in_specs=[VMEM] * 7 + [matrix(i, du1.shape[1]) for i in range(3)] + [VMEM],
        compiler_params=limit(16),
        cost_estimate=cost(3 * du1.size * du1.shape[1], 6 << 20),
    )(*far(du1), *early, *late, *far(w, w, w), back)


def on_device(
    inputs,
    memory,
    prefix,
    self_query,
    self_query_bias,
    self_key,
    self_value,
    self_value_bias,
    self_out,
    self_out_bias,
    self_norm_gain,
    self_norm_bias,
    cross_query,
    cross_query_bias,
    cross_key,
    cross_value,
    cross_value_bias,
    cross_out,
    cross_out_bias,
    cross_norm_gain,
    cross_norm_bias,
    feed_in,
    feed_in_bias,
    feed_out,
    feed_out_bias,
    feed_norm_gain,
    feed_norm_bias,
    cotangent,
):
    nd, nt = lax.axis_size("dp"), lax.axis_size("tensor")
    me_d, me_t = lax.axis_index("dp"), lax.axis_index("tensor")
    late = me_t % 2
    width = inputs.shape[1]
    assert LEN == 2 * inputs.shape[0] and MEM == 2 * memory.shape[0]
    assert nd & (nd - 1) == 0 and nt & (nt - 1) == 0
    prefix_here = jnp.where(late == 0, lax.dynamic_index_in_dim(prefix, me_t // 2, keepdims=False), 0)
    info = jnp.stack([late, prefix_here, me_d, me_t]).astype(jnp.int32)

    columns = self_query_bias.shape[0]
    row = lambda vector: vector.reshape(1, -1)
    packed = pack(
        (
            self_query,
            self_key,
            self_value,
            self_out.T,
            cross_query,
            cross_key,
            cross_value,
            cross_out.T,
        ),
        (self_query_bias, self_value_bias, cross_query_bias, cross_value_bias, feed_in_bias),
    )
    feed_shard = jnp.stack([feed_in, feed_out.T])

    bits = [1 << i for i in range(nt.bit_length() - 1)]
    swapped = [swap(packed, 0, k) for k in range(1, nt)]
    parts = [packed] + swapped
    size = 4 * self_query.shape[0]
    shape = (1, nt, 4) + self_query.shape
    lines = [
        jnp.stack([part[g * size : g * size + size] for part in parts]).reshape(shape)
        for g in range(2)
    ]
    riders = jnp.stack([part[2 * size :] for part in parts])
    rounds = len(plane_bits(0))
    line_feed = doubled(after(feed_shard, lines[0])[None], bits[:1])
    held = [([0], line) for line in lines]
    for index in range(rounds):
        more = [grown(*held[g], plane_bits(g)[index]) for g in range(2)]
        if index < rounds - 1:
            held = [merged([held[g], more[g]]) for g in range(2)]
    inputs_other = hand_over(after(inputs, line_feed), 0, 1)
    line_feed = doubled(line_feed, bits[1:])
    head_biases, hidden_bias = spread(info, riders)
    more[0] = more[0][0], after(more[0][1], inputs_other, line_feed, head_biases)
    arrays, entries = [], []
    for g in range(2):
        for slots, pieces in (held[g], more[g]):
            arrays += [pieces, swap(pieces, 1, 0)]
            entries += [(0, tuple(slots), 4 * g), (1, tuple(slots), 4 * g)]
    weights = assemble(info, arrays, entries)

    line_feed = after(line_feed, more[0][1], more[1][1])
    memory_other = swap(after(memory, line_feed), 0, 1)
    held = [([0], line_feed[None, :, g : g + 1]) for g in range(2)]
    q1, k1, v1, k1o, v1o = project_self(info, inputs, inputs_other, weights, head_biases)
    for index in range(rounds):
        more = [grown(*held[g], plane_bits(g)[index]) for g in range(2)]
        if index < rounds - 1:
            held = [(slots, after(pieces, q1)) for slots, pieces in held]
            held = [merged([held[g], more[g]]) for g in range(2)]
    q1 = after(q1, held[0][1], held[1][1])
    ctx1, log1 = self_forward(info, q1, k1, v1, k1o, v1o)
    first, normed1, inverse1, q2, k2, v2 = first_norm(
        ctx1,
        inputs,
        memory,
        memory_other,
        weights,
        row(self_out_bias),
        row(self_norm_gain),
        row(self_norm_bias),
        head_biases,
    )
    ctx2, log2 = cross_forward(q2, k2, v2)
    more[0] = more[0][0], after(more[0][1], ctx2)
    more[1] = more[1][0], after(more[1][1], ctx2)
    arrays, entries = [], []
    for g in range(2):
        for slots, pieces in (held[g], more[g]):
            arrays += [pieces, swap(pieces, 1, 0)]
            entries += [(0, tuple(slots), g), (1, tuple(slots), g)]
    w_feed = assemble(info, arrays, entries)
    feed_halves = Halves((1, 1), width // nd, 0)
    outputs, keep, send, du3, dhidden, normed2, inverse2, sums_feed, sums_hidden = feed(
        info,
        feed_halves,
        ctx2,
        first,
        cotangent,
        weights,
        w_feed,
        row(cross_out_bias),
        row(cross_norm_gain),
        row(cross_norm_bias),
        hidden_bias,
        row(feed_out_bias),
        row(feed_norm_gain),
        row(feed_norm_bias),
    )
    rounds = feed_halves.rounds
    got = swap(send, 1, 0)
    du2, db2, sums_second = feed_back(
        du3, dhidden, normed2, inverse2, w_feed, row(cross_norm_gain)
    )
    whole = [[(0, base), (1, base)] for base in feed_halves.bases]
    arrays, held, _ = halve(feed_halves, [after(keep, db2), got], whole, None, 0)
    db2 = after(db2, arrays[0])
    dq2, dk2, dv2 = cross_backward(q2, k2, v2, ctx2, log2, db2, weights)
    middle_halves, (du1, db1, memory_own, memory_back, keep, send) = middle(
        info,
        (du2, dq2, dk2, dv2, db2, sums_second, sums_feed, sums_hidden),
        normed1,
        inverse1,
        first,
        memory,
        memory_other,
        ctx2,
        ctx1,
        weights,
        row(self_norm_gain),
    )
    arrays[0] = after(arrays[0], db1)
    for index in range(1, rounds):
        arrays, held, _ = halve(feed_halves, arrays, held, None, index)
    got = swap(after(send, arrays[0]), 1, 0)
    db1 = after(db1, arrays[0])
    pairs = width // PAIR // 2
    operands = (info, q1, k1, v1, k1o, v1o, ctx1, log1)
    grads_early = self_backward(*operands, db1, weights, 0, pairs)
    arrays[0] = after(arrays[0], grads_early[0])
    block = feed_in.shape[0]
    feed_segments = list(zip(feed_halves.sizes, held))
    feed_arrays = arrays
    for bit in reversed(bits[1:]):
        feed_arrays, feed_segments, _ = line_round(feed_arrays, feed_segments, None, bit)
    whole = [[(0, base), (1, base)] for base in middle_halves.bases]
    rider = [(0, middle_halves.main), (1, middle_halves.main)]
    keep = after(keep, feed_arrays[0])
    arrays, held, rider = halve(middle_halves, [keep, got], whole, rider, 0)
    db1 = after(db1, arrays[0])
    grads_late = list(self_backward(*operands, db1, weights, pairs, pairs))
    arrays[0] = after(arrays[0], grads_late[0])
    for index in range(1, rounds):
        arrays, held, rider = halve(middle_halves, arrays, held, rider, index)
    grads_late[0] = after(grads_late[0], arrays[0])
    self_halves, (inputs_back, keep, send) = self_grads(
        info, inputs, inputs_other, grads_early, grads_late, weights
    )
    send = after(send, *arrays, *feed_arrays)
    got = swap(send, 1, 0)
    inputs_got = hand_over(after(inputs_back, send), 1, -1)
    arrays[0] = after(arrays[0], send)
    segments = list(zip(middle_halves.sizes, held))
    rider = (middle_halves.rider, rider)
    for bit in reversed(bits[1:]):
        arrays, segments, rider = line_round(arrays, segments, rider, bit)
    keep = after(keep, arrays[0])

    size = self_halves.sizes[0]
    end = (self_halves.rider, [(0, self_halves.main), (1, self_halves.main)])
    places = [self_halves.place(0, j)[0] for j in range(nd // 2)]
    parts = add_rows([keep, got], [[(size, [(0, lo), (1, lo)]), end] for lo in places])
    planes = [parts[0]] + [swap(part, 2 * j, 0) for j, part in enumerate(parts) if j]
    planes[0] = after(planes[0], *arrays, inputs_got)
    at = range(len(planes))
    rows = 3 * block
    end = (self_halves.rider, [(p, size) for p in at])
    lines = add_rows(planes, [[(rows, [(p, k * rows) for p in at]), end] for k in range(nt)])
    lines = line_swaps(lines)
    arrays[0] = after(arrays[0], lines[0])
    arrays, segments, rider = line_round(arrays, segments, rider, 1)
    riding = memory_back.shape[1] == feed_arrays[0].shape[1]
    feed_arrays[0] = after(feed_arrays[0], lines[0])
    feed_arrays, feed_segments, _ = line_round(
        feed_arrays, feed_segments, None, 1, memory_back if riding else None
    )

    grad_feed_in, grad_feed_out = add_rows(
        feed_arrays[:2], [[(block, terms)] for _, terms in feed_segments], F32
    )
    if riding:
        memory_got = feed_arrays[1][2 * block :]
    else:
        memory_got = swap(after(memory_back, lines[0]), 0, 1)
    grad_memory = memory_own + memory_got.astype(F32)
    du1 = after(du1, arrays[0], lines[0], feed_arrays[0])
    grad_inputs = input_grads(du1, grads_early[:3], grads_late[:3], weights, inputs_got)
    lines[0] = after(lines[0], grad_inputs, grad_feed_in, grad_memory)
    plans = [
        [(block, [(array, lo + i * block) for array, lo in terms])]
        for count, (_, terms) in zip(middle_halves.groups, segments)
        for i in range(count)
    ]
    cuts = [(i * block, block) for i in range(3)] + [(rows, self_halves.rider)]
    cuts = [[(n, [(3 + k, lo) for k in range(nt)])] for lo, n in cuts]
    plans = plans + cuts[:3] + [[rider], cuts[3]]
    sums = finish(info, arrays + lines, plans, nt, width)
    grad_middle, grad_self = sums[:5], sums[5:8]
    early, mine, hidden_mine = sums[8:]

    return (
        outputs,
        grad_inputs,
        grad_memory,
        grad_self[0],
        mine[2],
        grad_self[1],
        grad_self[2],
        mine[3],
        grad_middle[0].T,
        early[0],
        early[1],
        early[2],
        grad_middle[1],
        mine[0],
        grad_middle[2],
        grad_middle[3],
        mine[1],
        grad_middle[4].T,
        early[3],
        early[4],
        early[5],
        grad_feed_in,
        hidden_mine[0],
        grad_feed_out.T,
        early[6],
        early[7],
        early[8],
    )


def solution(mesh):
    placed = (
        P(("dp", "tensor"), None),
        P(("dp", "tensor"), None),
        P("dp"),
        P("dp", "tensor"),
        P("tensor"),
        P("dp", "tensor"),
        P("dp", "tensor"),
        P("tensor"),
        P("tensor", "dp"),
        P(),
        P(),
        P(),
        P("dp", "tensor"),
        P("tensor"),
        P("dp", "tensor"),
        P("dp", "tensor"),
        P("tensor"),
        P("tensor", "dp"),
        P(),
        P(),
        P(),
        P("dp", "tensor"),
        P("tensor"),
        P("tensor", "dp"),
        P(),
        P(),
        P(),
        P(("dp", "tensor"), None),
    )
    return jax.shard_map(
        on_device,
        mesh=mesh,
        in_specs=placed,
        out_specs=(
            P(("dp", "tensor"), None),
            P(("dp", "tensor"), None),
            P(("dp", "tensor"), None),
            P("dp", "tensor"),
            P("tensor"),
            P("dp", "tensor"),
            P("dp", "tensor"),
            P("tensor"),
            P("tensor", "dp"),
            P(),
            P(),
            P(),
            P("dp", "tensor"),
            P("tensor"),
            P("dp", "tensor"),
            P("dp", "tensor"),
            P("tensor"),
            P("tensor", "dp"),
            P(),
            P(),
            P(),
            P("dp", "tensor"),
            P("tensor"),
            P("tensor", "dp"),
            P(),
            P(),
            P(),
        ),
        check_vma=False,
    )
```

```python
import functools

import jax
import jax.numpy as jnp
from jax import lax
from jax.experimental import pallas as pl
from jax.experimental.pallas import tpu as pltpu
from jax.sharding import PartitionSpec as P

HD = 64
LEN = 1024
MEM = 256
PAIR = 128
BLOCK = 256
BACK_BLOCK = 512

EPSILON = 1e-05
MASKED = -1e30
SCALE = float(HD) ** (-0.5)

F32 = jnp.float32
BF16 = jnp.bfloat16
NN = (((1,), (0,)), ((), ()))
NT = (((1,), (1,)), ((), ()))
TN = (((0,), (0,)), ((), ()))
SMEM = pl.BlockSpec(memory_space=pltpu.SMEM)
ANY = pl.BlockSpec(memory_space=pl.ANY)
VMEM = pl.BlockSpec(memory_space=pltpu.VMEM)


def mm(left_side, right_side, dims):
    return lax.dot_general(left_side, right_side, dims, preferred_element_type=F32)


def shaped(shape, dtype):
    return jax.ShapeDtypeStruct(shape, dtype)


def shaped_far(shape, dtype):
    return pltpu.HBM(shape, dtype)


def cost(macs, moved):
    return pl.CostEstimate(flops=macs // 64, bytes_accessed=moved // 64, transcendentals=0)


def limit(mebibytes):
    return pltpu.CompilerParams(vmem_limit_bytes=mebibytes << 20)


def far(*arrays):
    return [pltpu.with_memory_space_constraint(array, pltpu.HBM) for array in arrays]


def swap(array, dp_mask, tensor_mask):
    nd, nt = lax.axis_size("dp"), lax.axis_size("tensor")
    pairs = [
        (d * nt + t, (d ^ dp_mask) * nt + (t ^ tensor_mask)) for d in range(nd) for t in range(nt)
    ]
    return lax.ppermute(array, ("dp", "tensor"), pairs)


def hand_over(array, parity, step):
    nd, nt = lax.axis_size("dp"), lax.axis_size("tensor")
    pairs = [(d * nt + t, d * nt + t + step) for d in range(nd) for t in range(parity, nt, 2)]
    return lax.ppermute(array, ("dp", "tensor"), pairs)


def tree_sum(terms):
    while len(terms) > 1:
        terms = [terms[i] + terms[i + 1] for i in range(0, len(terms), 2)]
    return terms[0]


def doubled(line, bits):
    for bit in bits:
        line = jnp.concatenate([line, swap(line, 0, bit)])
    return line


def plane_bits(group):
    bits = [1 << i for i in range((lax.axis_size("dp") // 2).bit_length() - 1)]
    return bits if group % 2 == 0 else bits[::-1]


def grown(slots, pieces, bit):
    return [j | bit for j in slots], swap(pieces, 2 * bit, 0)


def merged(held):
    (slots, pieces), (more_slots, more) = held
    return slots + more_slots, jnp.concatenate([pieces, more])


class Halves:
    def __init__(self, groups, r, rider):
        self.planes, self.nt = lax.axis_size("dp") // 2, lax.axis_size("tensor")
        self.groups, self.r, self.rider = groups, r, rider
        self.rounds = self.planes.bit_length() - 1
        self.sizes = [self.nt * count * r for count in groups]
        self.bases = [self.planes * sum(self.sizes[:g]) for g in range(len(groups))]
        self.main = self.planes * sum(self.sizes)
        self.total = self.main + rider

    def bit(self, group, index):
        return 1 << (index if group % 2 == 0 else self.rounds - 1 - index)

    def place(self, i, j):
        group = 0
        while i >= self.groups[group]:
            i -= self.groups[group]
            group += 1
        bits = [self.bit(group, index) for index in range(self.rounds)]
        position = sum((j & b > 0) << (self.rounds - 1 - n) for n, b in enumerate(bits))
        count = self.groups[group]
        return self.bases[group] + position * self.sizes[group] + i * self.r, count * self.r

    def split(self, arrays, held, rider, index):
        stay, sent = [], []
        for group, terms in enumerate(held):
            rows = (self.planes >> (index + 1)) * self.sizes[group]
            stay.append([(rows, terms)])
            sent.append([(rows, [(array, lo + rows) for array, lo in terms])])
        if self.rider:
            sent[-1].append((self.rider, rider))
        return stay + sent


def add_rows_kernel(*refs, plans, count):
    for out, plan in zip(refs[count:], plans):
        at = 0
        for rows, terms in plan:
            total = tree_sum([refs[i][lo : lo + rows, :].astype(F32) for i, lo in terms])
            out[at : at + rows, :] = total.astype(out.dtype)
            at += rows


def add_rows(arrays, plans, dtype=BF16):
    width = arrays[0].shape[1]
    moved = sum(array.size * array.dtype.itemsize for array in arrays)
    return pl.pallas_call(
        functools.partial(add_rows_kernel, plans=plans, count=len(arrays)),
        out_shape=tuple(shaped((sum(n for n, _ in plan), width), dtype) for plan in plans),
        in_specs=[VMEM] * len(arrays),
        out_specs=(VMEM,) * len(plans),
        compiler_params=limit(20),
        cost_estimate=cost(0, 2 * moved),
    )(*arrays)


def finish_kernel(info, *refs, plans, count, nt):
    outs = refs[count:-2]
    early, late = refs[-2:]
    w = early.shape[1]
    add_rows_kernel(*refs[:count], *outs[:-3], early, late, plans=plans, count=count)
    rows, mine, hidden = outs[-3:]
    for q in range(nt):
        lanes = slice(q * w, q * w + w)
        rows[:, lanes] = early[16 * q : 16 * q + 16, :]
    for k in range(4):
        block = 4 * info[3] + k
        at = 16 * lax.rem(block, nt) + 11 + lax.div(block, nt)
        hidden[:, k * w : k * w + w] = early[pl.ds(at, 1), :]
    for i, (source, at) in enumerate(
        ((early, 16 * info[3] + 9), (early, 16 * info[3] + 10), (late, info[3]), (late, nt + info[3]))
    ):
        mine[i : i + 1, :] = source[pl.ds(at, 1), :]


def finish(info, arrays, plans, nt, width):
    w = arrays[0].shape[1]
    sizes = [sum(n for n, _ in plan) for plan in plans]
    shapes = [(n, w) for n in sizes[:-2]] + [(16, width), (4, w), (1, 4 * w)]
    return pl.pallas_call(
        functools.partial(finish_kernel, plans=plans, count=len(arrays), nt=nt),
        out_shape=tuple(shaped(shape, F32) for shape in shapes),
        in_specs=[SMEM] + [VMEM] * len(arrays),
        out_specs=(VMEM,) * len(shapes),
        scratch_shapes=[pltpu.VMEM((n, w), F32) for n in sizes[-2:]],
        compiler_params=limit(20),
        cost_estimate=cost(0, 16 * w * sum(sizes)),
    )(info, *arrays)


def halve(halves, arrays, held, rider, index):
    groups = len(halves.groups)
    outs = list(add_rows(arrays, halves.split(arrays, held, rider, index)))
    stay, sent = outs[:groups], outs[groups:]
    got = [swap(part, 2 * halves.bit(group, index), 0) for group, part in enumerate(sent)]
    held = [[(group, 0), (groups + group, 0)] for group in range(groups)]
    end = sent[-1].shape[0] - halves.rider
    rider = [(2 * groups, end), (2 * groups - 1, end)]
    return stay + got + sent[-1:], held, rider


def line_round(arrays, segments, rider, bit, extra=None):
    stay, sent, after_round, lo = [], [], [], 0
    for rows, terms in segments:
        half = rows // 2
        stay.append((half, terms))
        sent.append((half, [(array, first + half) for array, first in terms]))
        after_round.append((half, [(0, lo), (1, lo)]))
        lo += half
    if rider:
        sent.append(rider)
        rider = (rider[0], [(1, lo), (2, lo)])
    if extra is not None:
        sent.append((extra.shape[0], [(len(arrays), 0)]))
        arrays = arrays + [extra]
    stay, sent = add_rows(arrays, [stay, sent])
    return [stay, swap(sent, 0, bit), sent], after_round, rider


def line_swaps(parts):
    return [parts[0]] + [swap(part, 0, k) for k, part in enumerate(parts) if k]


def after(array, *others):
    return lax.optimization_barrier((array,) + others)[0]


def aligned(r, w):
    return w % PAIR == 0 and r % 16 == 0


def assemble_kernel(info, *refs, entries):
    whole = refs[-1]
    for piece, (core, slots, first) in zip(refs, entries):
        _, nt, n, r, w = piece.shape
        for k, j in enumerate(slots):
            d = jnp.bitwise_xor(info[2], 2 * j + core)
            rows = pl.ds(pl.multiple_of(d * r, r), r)
            for s in range(nt):
                t = jnp.bitwise_xor(info[3], s)
                columns = pl.ds(pl.multiple_of(t * w, w), w)
                for i in range(n):
                    whole[first + i, rows, columns] = piece[k, s, i]


def assemble(info, arrays, entries):
    _, nt, _, r, w = arrays[0].shape
    nd = lax.axis_size("dp")
    count = max(entry[2] + array.shape[2] for array, entry in zip(arrays, entries))
    if aligned(r, w):
        return pl.pallas_call(
            functools.partial(assemble_kernel, entries=entries),
            out_shape=shaped((count, nd * r, nt * w), BF16),
            in_specs=[SMEM] + [VMEM] * len(arrays),
            out_specs=VMEM,
            compiler_params=limit(18),
            cost_estimate=cost(0, 4 * count * nd * r * nt * w),
        )(info, *arrays)
    wholes = []
    for first in sorted({entry[2] for entry in entries}):
        found = {}
        for array, (core, slots, at) in zip(arrays, entries):
            if at == first:
                found.update({2 * j + core: array[k] for k, j in enumerate(slots)})
        full = jnp.stack([found[d] for d in range(nd)])
        full = jnp.take(full, jnp.bitwise_xor(jnp.arange(nd), info[2]), axis=0)
        full = jnp.take(full, jnp.bitwise_xor(jnp.arange(nt), info[3]), axis=1)
        wholes.append(full.transpose(2, 0, 3, 1, 4).reshape(-1, nd * r, nt * w))
    return jnp.concatenate(wholes)


def disperse(info, halves, scratch, i, t, s, keep, send):
    for j in range(halves.planes):
        base, stride = halves.place(i, j)
        lo = base + s * stride
        if not isinstance(s, int):
            lo = pl.multiple_of(lo, 16)
        for c in range(2):
            d = jnp.bitwise_xor(info[2], 2 * j + c)
            rows = pl.ds(pl.multiple_of(d * halves.r, halves.r), halves.r)
            (keep, send)[c][pl.ds(lo, halves.r), :] = scratch[rows, t]


def disperse_whole(info, halves, scratch, i, keep, send):
    w = keep.shape[1]
    for s in range(halves.nt):
        t = jnp.bitwise_xor(info[3], s)
        disperse(info, halves, scratch, i, pl.ds(pl.multiple_of(t * w, w), w), s, keep, send)


def disperse_plain(info, halves, whole, rider):
    nd, nt = 2 * halves.planes, halves.nt
    n, r, w = whole.shape[0], halves.r, whole.shape[2] // nt
    full = whole.reshape(n, nd, r, nt, w).transpose(1, 3, 0, 2, 4)
    full = jnp.take(full, jnp.bitwise_xor(jnp.arange(nd), info[2]), axis=0)
    full = jnp.take(full, jnp.bitwise_xor(jnp.arange(nt), info[3]), axis=1)
    full = full.reshape(nd // 2, 2, nt, n, r, w)
    flats = []
    for c in range(2):
        rows, first = [], 0
        for count in halves.groups:
            order = sorted(range(halves.planes), key=lambda j: halves.place(first, j)[0])
            group = jnp.stack([full[j, c, :, first : first + count] for j in order])
            rows.append(group.reshape(-1, w))
            first += count
        flats.append(jnp.concatenate(rows + [rider]))
    return flats


def pack_kernel(*refs, blocks):
    out = refs[-1]
    r, w = refs[0].shape
    for i, block in enumerate(refs[:blocks]):
        out[i * r : (i + 1) * r, :] = block[...]
    row = lax.broadcasted_iota(jnp.int32, (16, w), 0)
    filled = jnp.zeros((16, w), F32)
    count = 0
    for vector in refs[blocks:-1]:
        for i in range(vector.shape[0]):
            filled = jnp.where(row == count, vector[i : i + 1, :].astype(F32), filled)
            count += 1
    out[blocks * r :, :] = filled.astype(BF16)


def pack(blocks, vectors):
    r, w = blocks[0].shape
    if aligned(r, w):
        return pl.pallas_call(
            functools.partial(pack_kernel, blocks=len(blocks)),
            out_shape=shaped((len(blocks) * r + 16, w), BF16),
            in_specs=[VMEM] * (len(blocks) + len(vectors)),
            out_specs=VMEM,
            cost_estimate=cost(0, 32 * r * w),
        )(*blocks, *[vector.reshape(-1, w) for vector in vectors])
    rows = jnp.concatenate(vectors).reshape(-1, w)
    return jnp.concatenate(list(blocks) + [jnp.pad(rows, ((0, 16 - rows.shape[0]), (0, 0)))])


def spread_kernel(info, riders, small, hidden):
    nt, _, w = riders.shape
    for s in range(nt):
        t = jnp.bitwise_xor(info[3], s)
        block = riders[s].astype(F32)
        small[:, pl.ds(pl.multiple_of(t * w, w), w)] = block
        for i in range(4):
            hidden[:, pl.ds(pl.multiple_of((4 * t + i) * w, w), w)] = block[4 + i : 5 + i]


def spread(info, riders):
    nt, _, w = riders.shape
    if aligned(16, w):
        return pl.pallas_call(
            spread_kernel,
            out_shape=(shaped((16, nt * w), F32), shaped((1, 4 * nt * w), F32)),
            in_specs=[SMEM, VMEM],
            out_specs=(VMEM, VMEM),
            cost_estimate=cost(0, 64 * nt * w),
        )(info, riders)
    full = jnp.take(riders, jnp.bitwise_xor(jnp.arange(nt), info[3]), axis=0).astype(F32)
    return full.transpose(1, 0, 2).reshape(16, nt * w), full[:, 4:8].reshape(1, -1)


def norm_forward(summed):
    row_mean = jnp.mean(summed, axis=-1, keepdims=True)
    centred = summed - row_mean
    variance = jnp.mean(centred * centred, axis=-1, keepdims=True)
    inverse = lax.rsqrt(variance + EPSILON)
    return centred * inverse, inverse


def norm_backward(grad_out, normed, inverse, norm_gain):
    grad_normed = grad_out * norm_gain
    return inverse * (
        grad_normed
        - jnp.mean(grad_normed, axis=-1, keepdims=True)
        - normed * jnp.mean(grad_normed * normed, axis=-1, keepdims=True)
    )


def column_sum(values):
    return jnp.sum(values.astype(F32), axis=0, keepdims=True)


def head_lanes(e):
    lane = lax.broadcasted_iota(jnp.int32, (1, PAIR), 1)
    chosen = (lane < HD) if e == 0 else (lane >= HD)
    return jnp.where(chosen, 1.0, 0.0)


def join_heads(first, second):
    lane = lax.broadcasted_iota(jnp.int32, first.shape, 1)
    return jnp.where(lane < HD, first, second)


def attend_forward(q, segments, contexts, logs, lo):
    rows = slice(lo, lo + BLOCK)
    results = []
    for e in range(2):
        query = q[rows, :] * head_lanes(e).astype(BF16)
        scores = [edit(mm(query, k, NT)) for k, _, edit in segments]
        peak = functools.reduce(
            jnp.maximum, [jnp.max(piece, axis=-1, keepdims=True) for piece in scores]
        )
        total = None
        for piece, (_, v, _) in zip(scores, segments):
            weights = jnp.exp(piece - peak).astype(BF16)
            wide = jnp.concatenate([v, jnp.ones(v.shape, BF16)], axis=1)
            part = mm(weights, wide, NN)
            total = part if total is None else total + part
        row_total = total[:, PAIR:]
        results.append((total[:, :PAIR] / row_total, peak + jnp.log(row_total)))
    contexts[rows, :] = join_heads(results[0][0], results[1][0]).astype(BF16)
    logs[rows, :] = join_heads(results[0][1], results[1][1])


def attend_backward(q, grad, ctx, logs, segments, grad_query, lo):
    rows = slice(lo, lo + BACK_BLOCK)
    grad_rows = grad[rows, :]
    product = grad_rows.astype(F32) * ctx[rows, :].astype(F32)
    query_rows = q[rows, :]
    query_turned = jnp.transpose(query_rows)
    grad_turned = jnp.transpose(grad_rows)
    total = None
    for e in range(2):
        lanes = head_lanes(e)
        low_lanes = lanes.astype(BF16)
        delta = jnp.sum(product * lanes, axis=-1, keepdims=True)
        row_log = logs[rows, e * HD : e * HD + 1]
        grad_low = grad_rows * low_lanes
        query = query_rows * low_lanes
        for k, v, edit, add in segments:
            weights = jnp.exp(edit(mm(query, k, NT)) - row_log)
            slope = mm(grad_low, v, NT) - delta
            grad_scores = (weights * slope).astype(BF16)
            part = mm(grad_scores, k * low_lanes, NN)
            total = part if total is None else total + part
            head = slice(e * HD, e * HD + HD)
            add(
                head,
                mm(query_turned[head], grad_scores, NN),
                mm(grad_turned[head], weights.astype(BF16), NN),
            )
    grad_query[rows, :] = (total * SCALE).astype(BF16)


def same(scores):
    return scores


def masked(lo, col_lo, prefix_len):
    def edit(scores):
        row = lo + lax.broadcasted_iota(jnp.int32, scores.shape, 0)
        col = col_lo + lax.broadcasted_iota(jnp.int32, scores.shape, 1)
        allowed = col <= row
        if prefix_len is not None:
            allowed = allowed | (col < prefix_len)
        return jnp.where(allowed, scores, MASKED)

    return edit


def adder(keys, values, col_lo, width):
    def add(head, part_keys, part_values):
        keys[head, col_lo : col_lo + width] += part_keys
        values[head, col_lo : col_lo + width] += part_values

    return add


def self_forward_kernel(info, q, k, v, ko, vo, ctx, logs):
    tokens = q.shape[0]

    @pl.when(info[0] == 0)
    def _():
        for lo in range(0, tokens, BLOCK):
            attend_forward(q, [(k[...], v[...], masked(lo, 0, info[1]))], ctx, logs, lo)

    @pl.when(info[0] != 0)
    def _():
        for lo in range(0, tokens, BLOCK):
            near = slice(lo, lo + BLOCK)
            segments = [(ko[...], vo[...], same)]
            if lo:
                segments.append((k[:lo, :], v[:lo, :], same))
            segments.append((k[near, :], v[near, :], masked(lo, lo, None)))
            attend_forward(q, segments, ctx, logs, lo)


def self_backward_kernel(
    info, q, k, v, ko, vo, ctx, logs, low, w, dq, dk, dv, dko, dvo, ak, av, ako, avo, grad
):
    tokens = q.shape[0]
    ak[...] = jnp.zeros_like(ak)
    av[...] = jnp.zeros_like(av)
    grad[...] = mm(low[...], w[0], NN).astype(BF16)

    @pl.when(info[0] == 0)
    def _():
        for lo in range(0, tokens, BACK_BLOCK):
            segments = [(k[...], v[...], masked(lo, 0, info[1]), adder(ak, av, 0, tokens))]
            attend_backward(q, grad, ctx, logs, segments, dq, lo)

    @pl.when(info[0] != 0)
    def _():
        ako[...] = jnp.zeros_like(ako)
        avo[...] = jnp.zeros_like(avo)
        for lo in range(0, tokens, BACK_BLOCK):
            near = slice(lo, lo + BACK_BLOCK)
            segments = [(ko[...], vo[...], same, adder(ako, avo, 0, tokens))]
            if lo:
                segments.append((k[:lo, :], v[:lo, :], same, adder(ak, av, 0, lo)))
            segments.append(
                (k[near, :], v[near, :], masked(lo, lo, None), adder(ak, av, lo, BACK_BLOCK))
            )
            attend_backward(q, grad, ctx, logs, segments, dq, lo)
        dko[...] = jnp.transpose(ako[...]).astype(BF16)
        dvo[...] = jnp.transpose(avo[...]).astype(BF16)

    dk[...] = jnp.transpose(ak[...]).astype(BF16)
    dv[...] = jnp.transpose(av[...]).astype(BF16)


def cross_forward_kernel(q, k, v, ctx, logs):
    for lo in range(0, q.shape[0], BLOCK):
        attend_forward(q, [(k[...], v[...], same)], ctx, logs, lo)


def cross_backward_kernel(q, k, v, ctx, logs, low, w, dq, dk, dv, ak, av, grad):
    ak[...] = jnp.zeros_like(ak)
    av[...] = jnp.zeros_like(av)
    grad[...] = mm(low[...], w[0], NN).astype(BF16)
    for lo in range(0, q.shape[0], BACK_BLOCK):
        segments = [(k[...], v[...], same, adder(ak, av, 0, k.shape[0]))]
        attend_backward(q, grad, ctx, logs, segments, dq, lo)
    dk[...] = jnp.transpose(ak[...]).astype(BF16)
    dv[...] = jnp.transpose(av[...]).astype(BF16)


def lanes_of(rows, first=0):
    return pl.BlockSpec((rows, PAIR), lambda h: (0, first + h))


def output_columns(slot, width, first=0):
    return pl.BlockSpec((1, width, PAIR), lambda h: (slot, 0, first + h))


def self_forward(info, q, k, v, ko, vo):
    tokens, width = q.shape
    row = lanes_of(tokens)
    return pl.pallas_call(
        self_forward_kernel,
        grid=(width // PAIR,),
        out_shape=(shaped((tokens, width), BF16), shaped((tokens, width), F32)),
        in_specs=[SMEM] + [row] * 5,
        out_specs=(row, row),
        compiler_params=limit(16),
        cost_estimate=cost(width // HD * tokens * tokens * 2 * 256 * 2, 5 << 20),
    )(info, q, k, v, ko, vo)


def self_backward(info, q, k, v, ko, vo, ctx, logs, low, w, first, pairs):
    tokens, width = q.shape
    row = lanes_of(tokens, first)
    out = shaped((tokens, pairs * PAIR), BF16)
    return pl.pallas_call(
        self_backward_kernel,
        grid=(pairs,),
        out_shape=(out,) * 5,
        in_specs=[SMEM] + [row] * 7 + [VMEM, output_columns(3, width, first)],
        out_specs=(lanes_of(tokens),) * 5,
        scratch_shapes=[pltpu.VMEM((PAIR, tokens), F32)] * 4 + [pltpu.VMEM((tokens, PAIR), BF16)],
        compiler_params=limit(16),
        cost_estimate=cost(width // HD * tokens * tokens * 256 * 5, 8 << 20),
    )(info, *far(q, k, v, ko, vo, ctx, logs), low, *far(w))


def cross_forward(q, k, v):
    tokens, width = q.shape
    rows = k.shape[0]
    return pl.pallas_call(
        cross_forward_kernel,
        grid=(width // PAIR,),
        out_shape=(shaped((tokens, width), BF16), shaped_far((tokens, width), F32)),
        in_specs=[lanes_of(tokens), lanes_of(rows), lanes_of(rows)],
        out_specs=(lanes_of(tokens), lanes_of(tokens)),
        compiler_params=limit(16),
        cost_estimate=cost(width // HD * tokens * rows * 256 * 2, 3 << 20),
    )(q, k, v)


def cross_backward(q, k, v, ctx, logs, low, w):
    tokens, width = q.shape
    rows = k.shape[0]
    small = shaped((rows, width), BF16)
    return pl.pallas_call(
        cross_backward_kernel,
        grid=(width // PAIR,),
        out_shape=(shaped((tokens, width), BF16), small, small),
        in_specs=[lanes_of(tokens), lanes_of(rows), lanes_of(rows)]
        + [lanes_of(tokens)] * 2
        + [VMEM, output_columns(7, width)],
        out_specs=(lanes_of(tokens), lanes_of(rows), lanes_of(rows)),
        scratch_shapes=[pltpu.VMEM((PAIR, rows), F32)] * 2 + [pltpu.VMEM((tokens, PAIR), BF16)],
        compiler_params=limit(16),
        cost_estimate=cost(width // HD * tokens * rows * 256 * 5, 4 << 20),
    )(*far(q, k, v, ctx, logs), low, *far(w))


def project_self_kernel(info, x, xo, wq, wk, wv, b, q, k, v, ko, vo):
    rows = x[...]
    q[...] = (mm(rows, wq[0], NN) + b[0:1, :]).astype(BF16) * jnp.asarray(SCALE, BF16)
    k[...] = mm(rows, wk[0], NN).astype(BF16)
    v[...] = (mm(rows, wv[0], NN) + b[1:2, :]).astype(BF16)

    @pl.when(info[0] != 0)
    def _():
        other = xo[...]
        ko[...] = mm(other, wk[0], NN).astype(BF16)
        vo[...] = (mm(other, wv[0], NN) + b[1:2, :]).astype(BF16)


def project_self(info, x, xo, w, b):
    low = shaped(x.shape, BF16)
    return pl.pallas_call(
        project_self_kernel,
        grid=(1,),
        out_shape=(low,) * 5,
        in_specs=[SMEM] + [VMEM] * 2 + [matrix(i, x.shape[1]) for i in range(3)] + [VMEM],
        compiler_params=limit(16),
        cost_estimate=cost(5 * x.size * x.shape[1], 5 << 20),
    )(info, x, xo, w, w, w, b)


def first_norm_kernel(
    ctx, x, mem, memo, wo, wq, wk, wv, ob, gain, bias, b, first, normed, inverse, q, k, v
):
    summed = x[...].astype(F32) + mm(ctx[...], wo[0], NT) + ob[...].astype(F32)
    n, r = norm_forward(summed)
    out = n * gain[...].astype(F32) + bias[...].astype(F32)
    normed[...] = n
    inverse[...] = r
    first[...] = out
    q[...] = (mm(out.astype(BF16), wq[0], NN) + b[2:3, :]).astype(BF16) * jnp.asarray(SCALE, BF16)
    rows = mem.shape[0]
    for source, lo in ((mem, 0), (memo, rows)):
        k[lo : lo + rows, :] = mm(source[...], wk[0], NN).astype(BF16)
        v[lo : lo + rows, :] = (mm(source[...], wv[0], NN) + b[3:4, :]).astype(BF16)


def first_norm(ctx, x, mem, memo, w, ob, gain, bias, b):
    rows = 2 * mem.shape[0]
    tokens, width = x.shape
    full = shaped(x.shape, F32)
    return pl.pallas_call(
        first_norm_kernel,
        grid=(1,),
        out_shape=(
            full,
            shaped_far(x.shape, F32),
            shaped_far((tokens, 1), F32),
            shaped(x.shape, BF16),
            shaped((rows, width), BF16),
            shaped((rows, width), BF16),
        ),
        in_specs=[VMEM] * 4 + [matrix(i, width) for i in range(3, 7)] + [VMEM] * 4,
        compiler_params=limit(16),
        cost_estimate=cost(3 * x.size * width, 8 << 20),
    )(ctx, x, mem, memo, w, w, w, w, ob, gain, bias, b)


def feed_kernel(
    info,
    ctx,
    first,
    cot,
    wo,
    wf,
    ob,
    gain2,
    bias2,
    fib,
    fob,
    gain3,
    bias3,
    out,
    keep,
    send,
    du3,
    dhid,
    normed,
    inverse,
    sums,
    hsum,
    act,
    slope,
    acc,
    second,
    db3,
    turn,
    *,
    halves,
):
    tokens, width = first.shape
    w = keep.shape[1]
    summed = first[...] + mm(ctx[...], wo[0], NT) + ob[...].astype(F32)
    n2, r2 = norm_forward(summed)
    normed[...] = n2
    inverse[...] = r2
    out2 = n2 * gain2[...].astype(F32) + bias2[...].astype(F32)
    second[...] = out2.astype(BF16)
    acc[...] = out2 + fob[...].astype(F32)

    @pl.loop(0, halves.nt, unroll=2)
    def _(t):
        cols = pl.ds(pl.multiple_of(t * w, w), w)
        hidden = mm(second[...], wf[0, :, cols], NN) + fib[:, cols]
        gate = 1.0 / (1.0 + jnp.exp(-hidden))
        active = (hidden * gate).astype(BF16)
        act[:, cols] = active
        slope[:, cols] = (gate * (1.0 + hidden * (1.0 - gate))).astype(BF16)
        acc[...] += mm(active, wf[1, :, cols], NT)

    n3, r3 = norm_forward(acc[...])
    out[...] = (n3 * gain3[...].astype(F32) + bias3[...].astype(F32)).astype(BF16)
    dy = cot[...].astype(F32)
    grad3 = norm_backward(dy, n3, r3, gain3[...].astype(F32))
    low3 = grad3.astype(BF16)
    sums[0:1, :] = column_sum(low3)
    sums[1:2, :] = column_sum(dy * n3)
    sums[2:3, :] = column_sum(dy)
    sums[3:8, :] = jnp.zeros((5, width), F32)
    du3[...] = grad3
    db3[...] = low3

    @pl.loop(0, halves.nt, unroll=2)
    def _(t):
        cols = pl.ds(pl.multiple_of(t * w, w), w)
        s = jnp.bitwise_xor(info[3], t)
        everything = slice(None)
        back = db3[...]
        dact = mm(back, wf[1, :, cols], NN)
        part = (dact * slope[:, cols].astype(F32)).astype(BF16)
        dhid[:, cols] = part
        hsum[:, cols] = column_sum(part)
        turn[0] = mm(second[...], part, TN).astype(BF16)
        disperse(info, halves, turn.at[0], 0, everything, s, keep, send)
        turn[1] = mm(back, act[:, cols], TN).astype(BF16)
        disperse(info, halves, turn.at[1], 1, everything, s, keep, send)


def feed_back_kernel(du3, dhid, normed, inverse, wf, gain, du2, db2, sums):
    dsecond = du3[...] + mm(dhid[...], wf[0], NT)
    n = normed[...]
    grad = norm_backward(dsecond, n, inverse[...], gain[...].astype(F32))
    low = grad.astype(BF16)
    du2[...] = grad
    db2[...] = low
    sums[0:1, :] = column_sum(low)
    sums[1:2, :] = column_sum(dsecond * n)
    sums[2:3, :] = column_sum(dsecond)
    sums[3:8, :] = jnp.zeros((5, du2.shape[1]), F32)


def feed_back(du3, dhid, normed, inverse, wf, gain):
    tokens, width = du3.shape
    wide = wf.shape[2]
    return pl.pallas_call(
        feed_back_kernel,
        grid=(1,),
        out_shape=(shaped(du3.shape, F32), shaped(du3.shape, BF16), shaped((8, width), F32)),
        in_specs=[VMEM] * 4 + [pl.BlockSpec((1, width, wide), lambda h: (0, 0, 0)), VMEM],
        compiler_params=limit(16),
        cost_estimate=cost(tokens * width * wide, 8 << 20),
    )(du3, dhid, normed, inverse, wf, gain)


def matrix(slot, width):
    return pl.BlockSpec((1, width, width), lambda h: (slot, 0, 0))


def feed(info, halves, ctx, first, cot, wo, wf, ob, gain2, bias2, fib, fob, gain3, bias3):
    tokens, width = first.shape
    wide = wf.shape[2]
    w = wide // halves.nt
    flat = shaped((halves.total, w), BF16)
    return pl.pallas_call(
        functools.partial(feed_kernel, halves=halves),
        grid=(1,),
        out_shape=(
            shaped(first.shape, BF16),
            flat,
            flat,
            shaped(first.shape, F32),
            shaped((tokens, wide), BF16),
            shaped(first.shape, F32),
            shaped((tokens, 1), F32),
            shaped((8, width), F32),
            shaped((1, wide), F32),
        ),
        in_specs=[SMEM] + [VMEM] * 3 + [matrix(7, width)] + [VMEM] * 8,
        scratch_shapes=[
            pltpu.VMEM((tokens, wide), BF16),
            pltpu.VMEM((tokens, wide), BF16),
            pltpu.VMEM((tokens, width), F32),
            pltpu.VMEM((tokens, width), BF16),
            pltpu.VMEM((tokens, width), BF16),
            pltpu.VMEM((2, width, w), BF16),
        ],
        compiler_params=limit(28),
        cost_estimate=cost(6 * tokens * width * wide, 14 << 20),
    )(info, ctx, first, cot, wo, wf, ob, gain2, bias2, fib, fob, gain3, bias3)


def middle_kernel(
    info,
    du2,
    dq2,
    dk2,
    dv2,
    db2,
    sums2,
    sums3,
    hsum,
    normed,
    inverse,
    first,
    mem,
    memo,
    ctx2,
    ctx1,
    wq,
    wk,
    wv,
    gain,
    *outs,
    halves,
):
    du1, db1, own, other = outs[:4]
    turn, riders = outs[-2:]
    rows, width = mem.shape
    dfirst = du2[...] + mm(dq2[...], wq[0], NT)
    n = normed[...]
    grad = norm_backward(dfirst, n, inverse[...], gain[...].astype(F32))
    low = grad.astype(BF16)
    du1[...] = grad
    db1[...] = low
    riders[0:1, :] = column_sum(low)
    riders[1:2, :] = column_sum(dfirst * n)
    riders[2:3, :] = column_sum(dfirst)
    riders[3:6, :] = sums2[0:3, :]
    riders[6:9, :] = sums3[0:3, :]
    riders[9:10, :] = column_sum(dq2[...])
    riders[10:11, :] = column_sum(dv2[...])
    for i in range(4):
        riders[11 + i : 12 + i, :] = hsum[:, i * width : (i + 1) * width]
    riders[15:16, :] = jnp.zeros((1, width), F32)
    turn[0] = mm(low, ctx1[...], TN).astype(BF16)
    turn[1] = mm(first[...].astype(BF16), dq2[...], TN).astype(BF16)
    for slot, part in ((2, dk2), (3, dv2)):
        turn[slot] = (
            mm(mem[...], part[:rows, :], TN) + mm(memo[...], part[rows:, :], TN)
        ).astype(BF16)
    turn[4] = mm(db2[...], ctx2[...], TN).astype(BF16)
    back = mm(dk2[...], wk[0], NT) + mm(dv2[...], wv[0], NT)
    own[...] = back[:rows, :]
    other[...] = back[rows:, :].astype(BF16)
    if halves is None:
        outs[4][...] = turn[...]
        outs[5][...] = riders[...]
        return
    for i in range(5):
        disperse_whole(info, halves, turn.at[i], i, outs[4], outs[5])
    w = outs[4].shape[1]
    for target in outs[4:6]:
        for q in range(width // w):
            lo = halves.main + 16 * q
            target[lo : lo + 16, :] = riders[:, q * w : q * w + w].astype(BF16)


def middle(info, near, normed, inverse, first, mem, memo, ctx2, ctx1, w, gain):
    tokens, width = first.shape
    rows = mem.shape[0]
    nd, nt = lax.axis_size("dp"), lax.axis_size("tensor")
    r, columns = width // nd, width // nt
    halves = Halves((3, 2), r, 16 * nt)
    direct = aligned(r, columns)
    if direct:
        last = (shaped((halves.total, columns), BF16),) * 2
    else:
        last = (shaped((5, width, width), BF16), shaped((16, width), F32))
    outs = pl.pallas_call(
        functools.partial(middle_kernel, halves=halves if direct else None),
        grid=(1,),
        out_shape=(
            shaped_far(first.shape, F32),
            shaped(first.shape, BF16),
            shaped((rows, width), F32),
            shaped((rows, width), BF16),
        )
        + last,
        in_specs=[SMEM] + [VMEM] * 15 + [matrix(i, width) for i in (4, 5, 6)] + [VMEM],
        scratch_shapes=[pltpu.VMEM((5, width, width), BF16), pltpu.VMEM((16, width), F32)],
        compiler_params=limit(20),
        cost_estimate=cost(6 * first.size * width, 12 << 20),
    )(
        info,
        *near,
        *far(normed, inverse, first, mem, memo, ctx2, ctx1, w, w, w),
        gain,
    )
    if not direct:
        rider = outs[5].astype(BF16).reshape(16, nt, columns).transpose(1, 0, 2)
        outs = outs[:4] + tuple(disperse_plain(info, halves, outs[4], rider.reshape(-1, columns)))
    return halves, outs


def self_grads_kernel(
    info, x, xo, dqa, dka, dva, dkoa, dvoa, dqb, dkb, dvb, dkob, dvob, wk, wv, *outs, halves
):
    other = outs[0]
    turn, sums = outs[-2:]
    width = x.shape[1]
    both = lambda left, right: jnp.concatenate([left[...], right[...]], axis=1)
    dq, dk, dv = both(dqa, dqb), both(dka, dkb), both(dva, dvb)
    turn[0] = mm(x[...], dq, TN).astype(BF16)
    sums[0:1, :] = column_sum(dq)

    @pl.when(info[0] == 0)
    def _():
        turn[1] = mm(x[...], dk, TN).astype(BF16)
        turn[2] = mm(x[...], dv, TN).astype(BF16)
        sums[1:2, :] = column_sum(dv)
        other[...] = jnp.zeros_like(other)

    @pl.when(info[0] != 0)
    def _():
        dko, dvo = both(dkoa, dkob), both(dvoa, dvob)
        turn[1] = (mm(x[...], dk, TN) + mm(xo[...], dko, TN)).astype(BF16)
        turn[2] = (mm(x[...], dv, TN) + mm(xo[...], dvo, TN)).astype(BF16)
        sums[1:2, :] = column_sum(dv) + column_sum(dvo)
        other[...] = (mm(dko, wk[0], NT) + mm(dvo, wv[0], NT)).astype(BF16)

    if halves is None:
        outs[1][...] = turn[...]
        outs[2][...] = sums[...]
        return
    for i in range(3):
        disperse_whole(info, halves, turn.at[i], i, outs[1], outs[2])
    w = outs[1].shape[1]
    row = lax.broadcasted_iota(jnp.int32, (16, w), 0)
    filled = jnp.zeros((16, w), F32)
    for i in range(2):
        for t in range(width // w):
            piece = sums[i : i + 1, t * w : t * w + w]
            filled = jnp.where(row == i * (width // w) + t, piece, filled)
    for target in outs[1:3]:
        target[halves.main :, :] = filled.astype(BF16)


def self_grads(info, x, xo, early, late, w):
    width = x.shape[1]
    nd, nt = lax.axis_size("dp"), lax.axis_size("tensor")
    r, columns = width // nd, width // nt
    halves = Halves((3,), r, 16)
    direct = aligned(r, columns)
    if direct:
        last = (shaped((halves.total, columns), BF16),) * 2
    else:
        last = (shaped((3, width, width), BF16), shaped((8, width), F32))
    outs = pl.pallas_call(
        functools.partial(self_grads_kernel, halves=halves if direct else None),
        grid=(1,),
        out_shape=(shaped(x.shape, BF16),) + last,
        in_specs=[SMEM] + [VMEM] * 12 + [matrix(i, width) for i in (1, 2)],
        scratch_shapes=[pltpu.VMEM((3, width, width), BF16), pltpu.VMEM((8, width), F32)],
        compiler_params=limit(16),
        cost_estimate=cost(7 * x.size * width, 8 << 20),
    )(info, *far(x, xo), *early, *late, *far(w, w))
    if not direct:
        rider = outs[2][:2].astype(BF16).reshape(-1, columns)
        rider = jnp.pad(rider, ((0, 16 - rider.shape[0]), (0, 0)))
        outs = outs[:1] + tuple(disperse_plain(info, halves, outs[1], rider))
    return halves, outs


def input_grads_kernel(du1, dqa, dka, dva, dqb, dkb, dvb, wq, wk, wv, back, out):
    both = lambda left, right: jnp.concatenate([left[...], right[...]], axis=1)
    out[...] = (
        du1[...]
        + mm(both(dqa, dqb), wq[0], NT)
        + mm(both(dka, dkb), wk[0], NT)
        + mm(both(dva, dvb), wv[0], NT)
        + back[...].astype(F32)
    )


def input_grads(du1, early, late, w, back):
    return pl.pallas_call(
        input_grads_kernel,
        grid=(1,),
        out_shape=shaped(du1.shape, F32),
        in_specs=[VMEM] * 7 + [matrix(i, du1.shape[1]) for i in range(3)] + [VMEM],
        compiler_params=limit(16),
        cost_estimate=cost(3 * du1.size * du1.shape[1], 6 << 20),
    )(*far(du1), *early, *late, *far(w, w, w), back)


def on_device(
    inputs,
    memory,
    prefix,
    self_query,
    self_query_bias,
    self_key,
    self_value,
    self_value_bias,
    self_out,
    self_out_bias,
    self_norm_gain,
    self_norm_bias,
    cross_query,
    cross_query_bias,
    cross_key,
    cross_value,
    cross_value_bias,
    cross_out,
    cross_out_bias,
    cross_norm_gain,
    cross_norm_bias,
    feed_in,
    feed_in_bias,
    feed_out,
    feed_out_bias,
    feed_norm_gain,
    feed_norm_bias,
    cotangent,
):
    nd, nt = lax.axis_size("dp"), lax.axis_size("tensor")
    me_d, me_t = lax.axis_index("dp"), lax.axis_index("tensor")
    late = me_t % 2
    width = inputs.shape[1]
    assert LEN == 2 * inputs.shape[0] and MEM == 2 * memory.shape[0]
    assert nd & (nd - 1) == 0 and nt & (nt - 1) == 0
    prefix_here = jnp.where(late == 0, lax.dynamic_index_in_dim(prefix, me_t // 2, keepdims=False), 0)
    info = jnp.stack([late, prefix_here, me_d, me_t]).astype(jnp.int32)

    columns = self_query_bias.shape[0]
    row = lambda vector: vector.reshape(1, -1)
    packed = pack(
        (
            self_query,
            self_key,
            self_value,
            self_out.T,
            cross_query,
            cross_key,
            cross_value,
            cross_out.T,
        ),
        (self_query_bias, self_value_bias, cross_query_bias, cross_value_bias, feed_in_bias),
    )
    feed_shard = jnp.stack([feed_in, feed_out.T])

    bits = [1 << i for i in range(nt.bit_length() - 1)]
    swapped = [swap(packed, 0, k) for k in range(1, nt)]
    parts = [packed] + swapped
    size = 4 * self_query.shape[0]
    shape = (1, nt, 4) + self_query.shape
    lines = [
        jnp.stack([part[g * size : g * size + size] for part in parts]).reshape(shape)
        for g in range(2)
    ]
    riders = jnp.stack([part[2 * size :] for part in parts])
    rounds = len(plane_bits(0))
    line_feed = doubled(after(feed_shard, lines[0])[None], bits[:1])
    held = [([0], line) for line in lines]
    for index in range(rounds):
        more = [grown(*held[g], plane_bits(g)[index]) for g in range(2)]
        if index < rounds - 1:
            held = [merged([held[g], more[g]]) for g in range(2)]
    inputs_other = hand_over(after(inputs, lines[0]), 0, 1)
    line_feed = doubled(line_feed, bits[1:])
    head_biases, hidden_bias = spread(info, riders)
    more[0] = more[0][0], after(more[0][1], inputs_other, line_feed, head_biases)
    arrays, entries = [], []
    for g in range(2):
        for slots, pieces in (held[g], more[g]):
            arrays += [pieces, swap(pieces, 1, 0)]
            entries += [(0, tuple(slots), 4 * g), (1, tuple(slots), 4 * g)]
    weights = assemble(info, arrays, entries)

    line_feed = after(line_feed, more[0][1], more[1][1])
    memory_other = swap(after(memory, line_feed), 0, 1)
    held = [([0], line_feed[None, :, g : g + 1]) for g in range(2)]
    q1, k1, v1, k1o, v1o = project_self(info, inputs, inputs_other, weights, head_biases)
    for index in range(rounds):
        more = [grown(*held[g], plane_bits(g)[index]) for g in range(2)]
        if index < rounds - 1:
            held = [(slots, after(pieces, q1)) for slots, pieces in held]
            held = [merged([held[g], more[g]]) for g in range(2)]
    q1 = after(q1, held[0][1], held[1][1])
    ctx1, log1 = self_forward(info, q1, k1, v1, k1o, v1o)
    first, normed1, inverse1, q2, k2, v2 = first_norm(
        ctx1,
        inputs,
        memory,
        memory_other,
        weights,
        row(self_out_bias),
        row(self_norm_gain),
        row(self_norm_bias),
        head_biases,
    )
    ctx2, log2 = cross_forward(q2, k2, v2)
    more[0] = more[0][0], after(more[0][1], ctx2)
    more[1] = more[1][0], after(more[1][1], ctx2)
    arrays, entries = [], []
    for g in range(2):
        for slots, pieces in (held[g], more[g]):
            arrays += [pieces, swap(pieces, 1, 0)]
            entries += [(0, tuple(slots), g), (1, tuple(slots), g)]
    w_feed = assemble(info, arrays, entries)
    feed_halves = Halves((1, 1), width // nd, 0)
    outputs, keep, send, du3, dhidden, normed2, inverse2, sums_feed, sums_hidden = feed(
        info,
        feed_halves,
        ctx2,
        first,
        cotangent,
        weights,
        w_feed,
        row(cross_out_bias),
        row(cross_norm_gain),
        row(cross_norm_bias),
        hidden_bias,
        row(feed_out_bias),
        row(feed_norm_gain),
        row(feed_norm_bias),
    )
    rounds = feed_halves.rounds
    got = swap(send, 1, 0)
    du2, db2, sums_second = feed_back(
        du3, dhidden, normed2, inverse2, w_feed, row(cross_norm_gain)
    )
    whole = [[(0, base), (1, base)] for base in feed_halves.bases]
    arrays, held, _ = halve(feed_halves, [after(keep, db2), got], whole, None, 0)
    db2 = after(db2, arrays[0])
    dq2, dk2, dv2 = cross_backward(q2, k2, v2, ctx2, log2, db2, weights)
    middle_halves, (du1, db1, memory_own, memory_back, keep, send) = middle(
        info,
        (du2, dq2, dk2, dv2, db2, sums_second, sums_feed, sums_hidden),
        normed1,
        inverse1,
        first,
        memory,
        memory_other,
        ctx2,
        ctx1,
        weights,
        row(self_norm_gain),
    )
    arrays[0] = after(arrays[0], db1)
    for index in range(1, rounds):
        arrays, held, _ = halve(feed_halves, arrays, held, None, index)
    got = swap(after(send, arrays[0]), 1, 0)
    db1 = after(db1, arrays[0])
    pairs = width // PAIR // 2
    operands = (info, q1, k1, v1, k1o, v1o, ctx1, log1)
    grads_early = self_backward(*operands, db1, weights, 0, pairs)
    arrays[0] = after(arrays[0], grads_early[0])
    block = feed_in.shape[0]
    feed_segments = list(zip(feed_halves.sizes, held))
    feed_arrays = arrays
    for bit in reversed(bits[1:]):
        feed_arrays, feed_segments, _ = line_round(feed_arrays, feed_segments, None, bit)
    whole = [[(0, base), (1, base)] for base in middle_halves.bases]
    rider = [(0, middle_halves.main), (1, middle_halves.main)]
    keep = after(keep, feed_arrays[0])
    arrays, held, rider = halve(middle_halves, [keep, got], whole, rider, 0)
    db1 = after(db1, arrays[0])
    grads_late = list(self_backward(*operands, db1, weights, pairs, pairs))
    arrays[0] = after(arrays[0], grads_late[0])
    for index in range(1, rounds):
        arrays, held, rider = halve(middle_halves, arrays, held, rider, index)
    grads_late[0] = after(grads_late[0], arrays[0])
    self_halves, (inputs_back, keep, send) = self_grads(
        info, inputs, inputs_other, grads_early, grads_late, weights
    )
    send = after(send, *arrays, *feed_arrays)
    got = swap(send, 1, 0)
    inputs_got = hand_over(after(inputs_back, send), 1, -1)
    arrays[0] = after(arrays[0], send)
    segments = list(zip(middle_halves.sizes, held))
    rider = (middle_halves.rider, rider)
    for bit in reversed(bits[1:]):
        arrays, segments, rider = line_round(arrays, segments, rider, bit)
    keep = after(keep, arrays[0])

    size = self_halves.sizes[0]
    end = (self_halves.rider, [(0, self_halves.main), (1, self_halves.main)])
    places = [self_halves.place(0, j)[0] for j in range(nd // 2)]
    parts = add_rows([keep, got], [[(size, [(0, lo), (1, lo)]), end] for lo in places])
    planes = [parts[0]] + [swap(part, 2 * j, 0) for j, part in enumerate(parts) if j]
    arrays[0] = after(arrays[0], *planes, inputs_got)
    arrays, segments, rider = line_round(arrays, segments, rider, 1)
    planes[0] = after(planes[0], arrays[0])
    at = range(len(planes))
    rows = 3 * block
    end = (self_halves.rider, [(p, size) for p in at])
    lines = add_rows(planes, [[(rows, [(p, k * rows) for p in at]), end] for k in range(nt)])
    lines = line_swaps(lines)
    riding = memory_back.shape[1] == feed_arrays[0].shape[1]
    feed_arrays[0] = after(feed_arrays[0], lines[0])
    feed_arrays, feed_segments, _ = line_round(
        feed_arrays, feed_segments, None, 1, memory_back if riding else None
    )

    grad_feed_in, grad_feed_out = add_rows(
        feed_arrays[:2], [[(block, terms)] for _, terms in feed_segments], F32
    )
    if riding:
        memory_got = feed_arrays[1][2 * block :]
    else:
        memory_got = swap(after(memory_back, lines[0]), 0, 1)
    grad_memory = memory_own + memory_got.astype(F32)
    du1 = after(du1, arrays[0], lines[0], feed_arrays[0])
    grad_inputs = input_grads(du1, grads_early[:3], grads_late[:3], weights, inputs_got)
    lines[0] = after(lines[0], grad_inputs, grad_feed_in, grad_memory)
    plans = [
        [(block, [(array, lo + i * block) for array, lo in terms])]
        for count, (_, terms) in zip(middle_halves.groups, segments)
        for i in range(count)
    ]
    cuts = [(i * block, block) for i in range(3)] + [(rows, self_halves.rider)]
    cuts = [[(n, [(3 + k, lo) for k in range(nt)])] for lo, n in cuts]
    plans = plans + cuts[:3] + [[rider], cuts[3]]
    sums = finish(info, arrays + lines, plans, nt, width)
    grad_middle, grad_self = sums[:5], sums[5:8]
    early, mine, hidden_mine = sums[8:]

    return (
        outputs,
        grad_inputs,
        grad_memory,
        grad_self[0],
        mine[2],
        grad_self[1],
        grad_self[2],
        mine[3],
        grad_middle[0].T,
        early[0],
        early[1],
        early[2],
        grad_middle[1],
        mine[0],
        grad_middle[2],
        grad_middle[3],
        mine[1],
        grad_middle[4].T,
        early[3],
        early[4],
        early[5],
        grad_feed_in,
        hidden_mine[0],
        grad_feed_out.T,
        early[6],
        early[7],
        early[8],
    )


def solution(mesh):
    placed = (
        P(("dp", "tensor"), None),
        P(("dp", "tensor"), None),
        P("dp"),
        P("dp", "tensor"),
        P("tensor"),
        P("dp", "tensor"),
        P("dp", "tensor"),
        P("tensor"),
        P("tensor", "dp"),
        P(),
        P(),
        P(),
        P("dp", "tensor"),
        P("tensor"),
        P("dp", "tensor"),
        P("dp", "tensor"),
        P("tensor"),
        P("tensor", "dp"),
        P(),
        P(),
        P(),
        P("dp", "tensor"),
        P("tensor"),
        P("tensor", "dp"),
        P(),
        P(),
        P(),
        P(("dp", "tensor"), None),
    )
    return jax.shard_map(
        on_device,
        mesh=mesh,
        in_specs=placed,
        out_specs=(
            P(("dp", "tensor"), None),
            P(("dp", "tensor"), None),
            P(("dp", "tensor"), None),
            P("dp", "tensor"),
            P("tensor"),
            P("dp", "tensor"),
            P("dp", "tensor"),
            P("tensor"),
            P("tensor", "dp"),
            P(),
            P(),
            P(),
            P("dp", "tensor"),
            P("tensor"),
            P("dp", "tensor"),
            P("dp", "tensor"),
            P("tensor"),
            P("tensor", "dp"),
            P(),
            P(),
            P(),
            P("dp", "tensor"),
            P("tensor"),
            P("tensor", "dp"),
            P(),
            P(),
            P(),
        ),
        check_vma=False,
    )
```

```python
import functools

import jax
import jax.numpy as jnp
from jax import lax
from jax.experimental import pallas as pl
from jax.experimental.pallas import tpu as pltpu
from jax.sharding import PartitionSpec as P

HD = 64
LEN = 1024
MEM = 256
PAIR = 128
BLOCK = 256
BACK_BLOCK = 512

EPSILON = 1e-05
MASKED = -1e30
SCALE = float(HD) ** (-0.5)

F32 = jnp.float32
BF16 = jnp.bfloat16
NN = (((1,), (0,)), ((), ()))
NT = (((1,), (1,)), ((), ()))
TN = (((0,), (0,)), ((), ()))
SMEM = pl.BlockSpec(memory_space=pltpu.SMEM)
ANY = pl.BlockSpec(memory_space=pl.ANY)
VMEM = pl.BlockSpec(memory_space=pltpu.VMEM)


def mm(left_side, right_side, dims):
    return lax.dot_general(left_side, right_side, dims, preferred_element_type=F32)


def shaped(shape, dtype):
    return jax.ShapeDtypeStruct(shape, dtype)


def shaped_far(shape, dtype):
    return pltpu.HBM(shape, dtype)


def cost(macs, moved):
    return pl.CostEstimate(flops=macs // 64, bytes_accessed=moved // 64, transcendentals=0)


def limit(mebibytes):
    return pltpu.CompilerParams(vmem_limit_bytes=mebibytes << 20)


def far(*arrays):
    return [pltpu.with_memory_space_constraint(array, pltpu.HBM) for array in arrays]


def swap(array, dp_mask, tensor_mask):
    nd, nt = lax.axis_size("dp"), lax.axis_size("tensor")
    pairs = [
        (d * nt + t, (d ^ dp_mask) * nt + (t ^ tensor_mask)) for d in range(nd) for t in range(nt)
    ]
    return lax.ppermute(array, ("dp", "tensor"), pairs)


def hand_over(array, parity, step):
    nd, nt = lax.axis_size("dp"), lax.axis_size("tensor")
    pairs = [(d * nt + t, d * nt + t + step) for d in range(nd) for t in range(parity, nt, 2)]
    return lax.ppermute(array, ("dp", "tensor"), pairs)


def tree_sum(terms):
    while len(terms) > 1:
        terms = [terms[i] + terms[i + 1] for i in range(0, len(terms), 2)]
    return terms[0]


def doubled(line, bits):
    for bit in bits:
        line = jnp.concatenate([line, swap(line, 0, bit)])
    return line


def plane_bits(group):
    bits = [1 << i for i in range((lax.axis_size("dp") // 2).bit_length() - 1)]
    return bits if group % 2 == 0 else bits[::-1]


def grown(slots, pieces, bit):
    return [j | bit for j in slots], swap(pieces, 2 * bit, 0)


def merged(held):
    (slots, pieces), (more_slots, more) = held
    return slots + more_slots, jnp.concatenate([pieces, more])


class Halves:
    def __init__(self, groups, r, rider):
        self.planes, self.nt = lax.axis_size("dp") // 2, lax.axis_size("tensor")
        self.groups, self.r, self.rider = groups, r, rider
        self.rounds = self.planes.bit_length() - 1
        self.sizes = [self.nt * count * r for count in groups]
        self.bases = [self.planes * sum(self.sizes[:g]) for g in range(len(groups))]
        self.main = self.planes * sum(self.sizes)
        self.total = self.main + rider

    def bit(self, group, index):
        return 1 << (index if group % 2 == 0 else self.rounds - 1 - index)

    def place(self, i, j):
        group = 0
        while i >= self.groups[group]:
            i -= self.groups[group]
            group += 1
        bits = [self.bit(group, index) for index in range(self.rounds)]
        position = sum((j & b > 0) << (self.rounds - 1 - n) for n, b in enumerate(bits))
        count = self.groups[group]
        return self.bases[group] + position * self.sizes[group] + i * self.r, count * self.r

    def split(self, arrays, held, rider, index):
        stay, sent = [], []
        for group, terms in enumerate(held):
            rows = (self.planes >> (index + 1)) * self.sizes[group]
            stay.append([(rows, terms)])
            sent.append([(rows, [(array, lo + rows) for array, lo in terms])])
        if self.rider:
            sent[-1].append((self.rider, rider))
        return stay + sent


def add_rows_kernel(*refs, plans, count):
    for out, plan in zip(refs[count:], plans):
        at = 0
        for rows, terms in plan:
            total = tree_sum([refs[i][lo : lo + rows, :].astype(F32) for i, lo in terms])
            out[at : at + rows, :] = total.astype(out.dtype)
            at += rows


def add_rows(arrays, plans, dtype=BF16):
    width = arrays[0].shape[1]
    moved = sum(array.size * array.dtype.itemsize for array in arrays)
    return pl.pallas_call(
        functools.partial(add_rows_kernel, plans=plans, count=len(arrays)),
        out_shape=tuple(shaped((sum(n for n, _ in plan), width), dtype) for plan in plans),
        in_specs=[VMEM] * len(arrays),
        out_specs=(VMEM,) * len(plans),
        compiler_params=limit(20),
        cost_estimate=cost(0, 2 * moved),
    )(*arrays)


def finish_kernel(info, *refs, plans, count, nt):
    outs = refs[count:-2]
    early, late = refs[-2:]
    w = early.shape[1]
    add_rows_kernel(*refs[:count], *outs[:-3], early, late, plans=plans, count=count)
    rows, mine, hidden = outs[-3:]
    for q in range(nt):
        lanes = slice(q * w, q * w + w)
        rows[:, lanes] = early[16 * q : 16 * q + 16, :]
    for k in range(4):
        block = 4 * info[3] + k
        at = 16 * lax.rem(block, nt) + 11 + lax.div(block, nt)
        hidden[:, k * w : k * w + w] = early[pl.ds(at, 1), :]
    for i, (source, at) in enumerate(
        ((early, 16 * info[3] + 9), (early, 16 * info[3] + 10), (late, info[3]), (late, nt + info[3]))
    ):
        mine[i : i + 1, :] = source[pl.ds(at, 1), :]


def finish(info, arrays, plans, nt, width):
    w = arrays[0].shape[1]
    sizes = [sum(n for n, _ in plan) for plan in plans]
    shapes = [(n, w) for n in sizes[:-2]] + [(16, width), (4, w), (1, 4 * w)]
    return pl.pallas_call(
        functools.partial(finish_kernel, plans=plans, count=len(arrays), nt=nt),
        out_shape=tuple(shaped(shape, F32) for shape in shapes),
        in_specs=[SMEM] + [VMEM] * len(arrays),
        out_specs=(VMEM,) * len(shapes),
        scratch_shapes=[pltpu.VMEM((n, w), F32) for n in sizes[-2:]],
        compiler_params=limit(20),
        cost_estimate=cost(0, 16 * w * sum(sizes)),
    )(info, *arrays)


def halve(halves, arrays, held, rider, index):
    groups = len(halves.groups)
    outs = list(add_rows(arrays, halves.split(arrays, held, rider, index)))
    stay, sent = outs[:groups], outs[groups:]
    got = [swap(part, 2 * halves.bit(group, index), 0) for group, part in enumerate(sent)]
    held = [[(group, 0), (groups + group, 0)] for group in range(groups)]
    end = sent[-1].shape[0] - halves.rider
    rider = [(2 * groups, end), (2 * groups - 1, end)]
    return stay + got + sent[-1:], held, rider


def line_round(arrays, segments, rider, bit, extra=None):
    stay, sent, after_round, lo = [], [], [], 0
    for rows, terms in segments:
        half = rows // 2
        stay.append((half, terms))
        sent.append((half, [(array, first + half) for array, first in terms]))
        after_round.append((half, [(0, lo), (1, lo)]))
        lo += half
    if rider:
        sent.append(rider)
        rider = (rider[0], [(1, lo), (2, lo)])
    if extra is not None:
        sent.append((extra.shape[0], [(len(arrays), 0)]))
        arrays = arrays + [extra]
    stay, sent = add_rows(arrays, [stay, sent])
    return [stay, swap(sent, 0, bit), sent], after_round, rider


def line_swaps(parts):
    return [parts[0]] + [swap(part, 0, k) for k, part in enumerate(parts) if k]


def after(array, *others):
    return lax.optimization_barrier((array,) + others)[0]


def aligned(r, w):
    return w % PAIR == 0 and r % 16 == 0


def assemble_kernel(info, *refs, entries):
    whole = refs[-1]
    for piece, (core, slots, first) in zip(refs, entries):
        _, nt, n, r, w = piece.shape
        for k, j in enumerate(slots):
            d = jnp.bitwise_xor(info[2], 2 * j + core)
            rows = pl.ds(pl.multiple_of(d * r, r), r)
            for s in range(nt):
                t = jnp.bitwise_xor(info[3], s)
                columns = pl.ds(pl.multiple_of(t * w, w), w)
                for i in range(n):
                    whole[first + i, rows, columns] = piece[k, s, i]


def assemble(info, arrays, entries):
    _, nt, _, r, w = arrays[0].shape
    nd = lax.axis_size("dp")
    count = max(entry[2] + array.shape[2] for array, entry in zip(arrays, entries))
    if aligned(r, w):
        return pl.pallas_call(
            functools.partial(assemble_kernel, entries=entries),
            out_shape=shaped((count, nd * r, nt * w), BF16),
            in_specs=[SMEM] + [VMEM] * len(arrays),
            out_specs=VMEM,
            compiler_params=limit(18),
            cost_estimate=cost(0, 4 * count * nd * r * nt * w),
        )(info, *arrays)
    wholes = []
    for first in sorted({entry[2] for entry in entries}):
        found = {}
        for array, (core, slots, at) in zip(arrays, entries):
            if at == first:
                found.update({2 * j + core: array[k] for k, j in enumerate(slots)})
        full = jnp.stack([found[d] for d in range(nd)])
        full = jnp.take(full, jnp.bitwise_xor(jnp.arange(nd), info[2]), axis=0)
        full = jnp.take(full, jnp.bitwise_xor(jnp.arange(nt), info[3]), axis=1)
        wholes.append(full.transpose(2, 0, 3, 1, 4).reshape(-1, nd * r, nt * w))
    return jnp.concatenate(wholes)


def disperse(info, halves, scratch, i, t, s, keep, send):
    for j in range(halves.planes):
        base, stride = halves.place(i, j)
        lo = base + s * stride
        if not isinstance(s, int):
            lo = pl.multiple_of(lo, 16)
        for c in range(2):
            d = jnp.bitwise_xor(info[2], 2 * j + c)
            rows = pl.ds(pl.multiple_of(d * halves.r, halves.r), halves.r)
            (keep, send)[c][pl.ds(lo, halves.r), :] = scratch[rows, t]


def disperse_whole(info, halves, scratch, i, keep, send):
    w = keep.shape[1]
    for s in range(halves.nt):
        t = jnp.bitwise_xor(info[3], s)
        disperse(info, halves, scratch, i, pl.ds(pl.multiple_of(t * w, w), w), s, keep, send)


def disperse_plain(info, halves, whole, rider):
    nd, nt = 2 * halves.planes, halves.nt
    n, r, w = whole.shape[0], halves.r, whole.shape[2] // nt
    full = whole.reshape(n, nd, r, nt, w).transpose(1, 3, 0, 2, 4)
    full = jnp.take(full, jnp.bitwise_xor(jnp.arange(nd), info[2]), axis=0)
    full = jnp.take(full, jnp.bitwise_xor(jnp.arange(nt), info[3]), axis=1)
    full = full.reshape(nd // 2, 2, nt, n, r, w)
    flats = []
    for c in range(2):
        rows, first = [], 0
        for count in halves.groups:
            order = sorted(range(halves.planes), key=lambda j: halves.place(first, j)[0])
            group = jnp.stack([full[j, c, :, first : first + count] for j in order])
            rows.append(group.reshape(-1, w))
            first += count
        flats.append(jnp.concatenate(rows + [rider]))
    return flats


def pack_kernel(*refs, blocks):
    out = refs[-1]
    r, w = refs[0].shape
    for i, block in enumerate(refs[:blocks]):
        out[i * r : (i + 1) * r, :] = block[...]
    row = lax.broadcasted_iota(jnp.int32, (16, w), 0)
    filled = jnp.zeros((16, w), F32)
    count = 0
    for vector in refs[blocks:-1]:
        for i in range(vector.shape[0]):
            filled = jnp.where(row == count, vector[i : i + 1, :].astype(F32), filled)
            count += 1
    out[blocks * r :, :] = filled.astype(BF16)


def pack(blocks, vectors):
    r, w = blocks[0].shape
    if aligned(r, w):
        return pl.pallas_call(
            functools.partial(pack_kernel, blocks=len(blocks)),
            out_shape=shaped((len(blocks) * r + 16, w), BF16),
            in_specs=[VMEM] * (len(blocks) + len(vectors)),
            out_specs=VMEM,
            cost_estimate=cost(0, 32 * r * w),
        )(*blocks, *[vector.reshape(-1, w) for vector in vectors])
    rows = jnp.concatenate(vectors).reshape(-1, w)
    return jnp.concatenate(list(blocks) + [jnp.pad(rows, ((0, 16 - rows.shape[0]), (0, 0)))])


def spread_kernel(info, riders, small, hidden):
    nt, _, w = riders.shape
    for s in range(nt):
        t = jnp.bitwise_xor(info[3], s)
        block = riders[s].astype(F32)
        small[:, pl.ds(pl.multiple_of(t * w, w), w)] = block
        for i in range(4):
            hidden[:, pl.ds(pl.multiple_of((4 * t + i) * w, w), w)] = block[4 + i : 5 + i]


def spread(info, riders):
    nt, _, w = riders.shape
    if aligned(16, w):
        return pl.pallas_call(
            spread_kernel,
            out_shape=(shaped((16, nt * w), F32), shaped((1, 4 * nt * w), F32)),
            in_specs=[SMEM, VMEM],
            out_specs=(VMEM, VMEM),
            cost_estimate=cost(0, 64 * nt * w),
        )(info, riders)
    full = jnp.take(riders, jnp.bitwise_xor(jnp.arange(nt), info[3]), axis=0).astype(F32)
    return full.transpose(1, 0, 2).reshape(16, nt * w), full[:, 4:8].reshape(1, -1)


def norm_forward(summed):
    row_mean = jnp.mean(summed, axis=-1, keepdims=True)
    centred = summed - row_mean
    variance = jnp.mean(centred * centred, axis=-1, keepdims=True)
    inverse = lax.rsqrt(variance + EPSILON)
    return centred * inverse, inverse


def norm_backward(grad_out, normed, inverse, norm_gain):
    grad_normed = grad_out * norm_gain
    return inverse * (
        grad_normed
        - jnp.mean(grad_normed, axis=-1, keepdims=True)
        - normed * jnp.mean(grad_normed * normed, axis=-1, keepdims=True)
    )


def column_sum(values):
    return jnp.sum(values.astype(F32), axis=0, keepdims=True)


def head_lanes(e):
    lane = lax.broadcasted_iota(jnp.int32, (1, PAIR), 1)
    chosen = (lane < HD) if e == 0 else (lane >= HD)
    return jnp.where(chosen, 1.0, 0.0)


def join_heads(first, second):
    lane = lax.broadcasted_iota(jnp.int32, first.shape, 1)
    return jnp.where(lane < HD, first, second)


def attend_forward(q, segments, contexts, logs, lo):
    rows = slice(lo, lo + BLOCK)
    results = []
    for e in range(2):
        query = q[rows, :] * head_lanes(e).astype(BF16)
        scores = [edit(mm(query, k, NT)) for k, _, edit in segments]
        peak = functools.reduce(
            jnp.maximum, [jnp.max(piece, axis=-1, keepdims=True) for piece in scores]
        )
        total = None
        for piece, (_, v, _) in zip(scores, segments):
            weights = jnp.exp(piece - peak).astype(BF16)
            wide = jnp.concatenate([v, jnp.ones(v.shape, BF16)], axis=1)
            part = mm(weights, wide, NN)
            total = part if total is None else total + part
        row_total = total[:, PAIR:]
        results.append((total[:, :PAIR] / row_total, peak + jnp.log(row_total)))
    contexts[rows, :] = join_heads(results[0][0], results[1][0]).astype(BF16)
    logs[rows, :] = join_heads(results[0][1], results[1][1])


def attend_backward(q, grad, ctx, logs, segments, grad_query, lo):
    rows = slice(lo, lo + BACK_BLOCK)
    grad_rows = grad[rows, :]
    product = grad_rows.astype(F32) * ctx[rows, :].astype(F32)
    query_rows = q[rows, :]
    query_turned = jnp.transpose(query_rows)
    grad_turned = jnp.transpose(grad_rows)
    total = None
    for e in range(2):
        lanes = head_lanes(e)
        low_lanes = lanes.astype(BF16)
        delta = jnp.sum(product * lanes, axis=-1, keepdims=True)
        row_log = logs[rows, e * HD : e * HD + 1]
        grad_low = grad_rows * low_lanes
        query = query_rows * low_lanes
        for k, v, edit, add in segments:
            weights = jnp.exp(edit(mm(query, k, NT)) - row_log)
            slope = mm(grad_low, v, NT) - delta
            grad_scores = (weights * slope).astype(BF16)
            part = mm(grad_scores, k * low_lanes, NN)
            total = part if total is None else total + part
            head = slice(e * HD, e * HD + HD)
            add(
                head,
                mm(query_turned[head], grad_scores, NN),
                mm(grad_turned[head], weights.astype(BF16), NN),
            )
    grad_query[rows, :] = (total * SCALE).astype(BF16)


def same(scores):
    return scores


def masked(lo, col_lo, prefix_len):
    def edit(scores):
        row = lo + lax.broadcasted_iota(jnp.int32, scores.shape, 0)
        col = col_lo + lax.broadcasted_iota(jnp.int32, scores.shape, 1)
        allowed = col <= row
        if prefix_len is not None:
            allowed = allowed | (col < prefix_len)
        return jnp.where(allowed, scores, MASKED)

    return edit


def adder(keys, values, col_lo, width):
    def add(head, part_keys, part_values):
        keys[head, col_lo : col_lo + width] += part_keys
        values[head, col_lo : col_lo + width] += part_values

    return add


def self_forward_kernel(info, q, k, v, ko, vo, ctx, logs):
    tokens = q.shape[0]

    @pl.when(info[0] == 0)
    def _():
        for lo in range(0, tokens, BLOCK):
            attend_forward(q, [(k[...], v[...], masked(lo, 0, info[1]))], ctx, logs, lo)

    @pl.when(info[0] != 0)
    def _():
        for lo in range(0, tokens, BLOCK):
            near = slice(lo, lo + BLOCK)
            segments = [(ko[...], vo[...], same)]
            if lo:
                segments.append((k[:lo, :], v[:lo, :], same))
            segments.append((k[near, :], v[near, :], masked(lo, lo, None)))
            attend_forward(q, segments, ctx, logs, lo)


def self_backward_kernel(
    info, q, k, v, ko, vo, ctx, logs, low, w, dq, dk, dv, dko, dvo, ak, av, ako, avo, grad
):
    tokens = q.shape[0]
    ak[...] = jnp.zeros_like(ak)
    av[...] = jnp.zeros_like(av)
    grad[...] = mm(low[...], w[0], NN).astype(BF16)

    @pl.when(info[0] == 0)
    def _():
        for lo in range(0, tokens, BACK_BLOCK):
            segments = [(k[...], v[...], masked(lo, 0, info[1]), adder(ak, av, 0, tokens))]
            attend_backward(q, grad, ctx, logs, segments, dq, lo)

    @pl.when(info[0] != 0)
    def _():
        ako[...] = jnp.zeros_like(ako)
        avo[...] = jnp.zeros_like(avo)
        for lo in range(0, tokens, BACK_BLOCK):
            near = slice(lo, lo + BACK_BLOCK)
            segments = [(ko[...], vo[...], same, adder(ako, avo, 0, tokens))]
            if lo:
                segments.append((k[:lo, :], v[:lo, :], same, adder(ak, av, 0, lo)))
            segments.append(
                (k[near, :], v[near, :], masked(lo, lo, None), adder(ak, av, lo, BACK_BLOCK))
            )
            attend_backward(q, grad, ctx, logs, segments, dq, lo)
        dko[...] = jnp.transpose(ako[...]).astype(BF16)
        dvo[...] = jnp.transpose(avo[...]).astype(BF16)

    dk[...] = jnp.transpose(ak[...]).astype(BF16)
    dv[...] = jnp.transpose(av[...]).astype(BF16)


def cross_forward_kernel(q, k, v, ctx, logs):
    for lo in range(0, q.shape[0], BLOCK):
        attend_forward(q, [(k[...], v[...], same)], ctx, logs, lo)


def cross_backward_kernel(q, k, v, ctx, logs, low, w, dq, dk, dv, ak, av, grad):
    ak[...] = jnp.zeros_like(ak)
    av[...] = jnp.zeros_like(av)
    grad[...] = mm(low[...], w[0], NN).astype(BF16)
    for lo in range(0, q.shape[0], BACK_BLOCK):
        segments = [(k[...], v[...], same, adder(ak, av, 0, k.shape[0]))]
        attend_backward(q, grad, ctx, logs, segments, dq, lo)
    dk[...] = jnp.transpose(ak[...]).astype(BF16)
    dv[...] = jnp.transpose(av[...]).astype(BF16)


def lanes_of(rows, first=0):
    return pl.BlockSpec((rows, PAIR), lambda h: (0, first + h))


def output_columns(slot, width, first=0):
    return pl.BlockSpec((1, width, PAIR), lambda h: (slot, 0, first + h))


def self_forward(info, q, k, v, ko, vo):
    tokens, width = q.shape
    row = lanes_of(tokens)
    return pl.pallas_call(
        self_forward_kernel,
        grid=(width // PAIR,),
        out_shape=(shaped((tokens, width), BF16), shaped((tokens, width), F32)),
        in_specs=[SMEM] + [row] * 5,
        out_specs=(row, row),
        compiler_params=limit(16),
        cost_estimate=cost(width // HD * tokens * tokens * 2 * 256 * 2, 5 << 20),
    )(info, q, k, v, ko, vo)


def self_backward(info, q, k, v, ko, vo, ctx, logs, low, w, first, pairs):
    tokens, width = q.shape
    row = lanes_of(tokens, first)
    out = shaped((tokens, pairs * PAIR), BF16)
    return pl.pallas_call(
        self_backward_kernel,
        grid=(pairs,),
        out_shape=(out,) * 5,
        in_specs=[SMEM] + [row] * 7 + [VMEM, output_columns(3, width, first)],
        out_specs=(lanes_of(tokens),) * 5,
        scratch_shapes=[pltpu.VMEM((PAIR, tokens), F32)] * 4 + [pltpu.VMEM((tokens, PAIR), BF16)],
        compiler_params=limit(16),
        cost_estimate=cost(width // HD * tokens * tokens * 256 * 5, 8 << 20),
    )(info, *far(q, k, v, ko, vo, ctx, logs), low, *far(w))


def cross_forward(q, k, v):
    tokens, width = q.shape
    rows = k.shape[0]
    return pl.pallas_call(
        cross_forward_kernel,
        grid=(width // PAIR,),
        out_shape=(shaped((tokens, width), BF16), shaped_far((tokens, width), F32)),
        in_specs=[lanes_of(tokens), lanes_of(rows), lanes_of(rows)],
        out_specs=(lanes_of(tokens), lanes_of(tokens)),
        compiler_params=limit(16),
        cost_estimate=cost(width // HD * tokens * rows * 256 * 2, 3 << 20),
    )(q, k, v)


def cross_backward(q, k, v, ctx, logs, low, w):
    tokens, width = q.shape
    rows = k.shape[0]
    small = shaped((rows, width), BF16)
    return pl.pallas_call(
        cross_backward_kernel,
        grid=(width // PAIR,),
        out_shape=(shaped((tokens, width), BF16), small, small),
        in_specs=[lanes_of(tokens), lanes_of(rows), lanes_of(rows)]
        + [lanes_of(tokens)] * 2
        + [VMEM, output_columns(7, width)],
        out_specs=(lanes_of(tokens), lanes_of(rows), lanes_of(rows)),
        scratch_shapes=[pltpu.VMEM((PAIR, rows), F32)] * 2 + [pltpu.VMEM((tokens, PAIR), BF16)],
        compiler_params=limit(16),
        cost_estimate=cost(width // HD * tokens * rows * 256 * 5, 4 << 20),
    )(*far(q, k, v, ctx, logs), low, *far(w))


def project_self_kernel(info, x, xo, wq, wk, wv, b, q, k, v, ko, vo):
    rows = x[...]
    q[...] = (mm(rows, wq[0], NN) + b[0:1, :]).astype(BF16) * jnp.asarray(SCALE, BF16)
    k[...] = mm(rows, wk[0], NN).astype(BF16)
    v[...] = (mm(rows, wv[0], NN) + b[1:2, :]).astype(BF16)

    @pl.when(info[0] != 0)
    def _():
        other = xo[...]
        ko[...] = mm(other, wk[0], NN).astype(BF16)
        vo[...] = (mm(other, wv[0], NN) + b[1:2, :]).astype(BF16)


def project_self(info, x, xo, w, b):
    low = shaped(x.shape, BF16)
    return pl.pallas_call(
        project_self_kernel,
        grid=(1,),
        out_shape=(low,) * 5,
        in_specs=[SMEM] + [VMEM] * 2 + [matrix(i, x.shape[1]) for i in range(3)] + [VMEM],
        compiler_params=limit(16),
        cost_estimate=cost(5 * x.size * x.shape[1], 5 << 20),
    )(info, x, xo, w, w, w, b)


def first_norm_kernel(
    ctx, x, mem, memo, wo, wq, wk, wv, ob, gain, bias, b, first, normed, inverse, q, k, v
):
    summed = x[...].astype(F32) + mm(ctx[...], wo[0], NT) + ob[...].astype(F32)
    n, r = norm_forward(summed)
    out = n * gain[...].astype(F32) + bias[...].astype(F32)
    normed[...] = n
    inverse[...] = r
    first[...] = out
    q[...] = (mm(out.astype(BF16), wq[0], NN) + b[2:3, :]).astype(BF16) * jnp.asarray(SCALE, BF16)
    rows = mem.shape[0]
    for source, lo in ((mem, 0), (memo, rows)):
        k[lo : lo + rows, :] = mm(source[...], wk[0], NN).astype(BF16)
        v[lo : lo + rows, :] = (mm(source[...], wv[0], NN) + b[3:4, :]).astype(BF16)


def first_norm(ctx, x, mem, memo, w, ob, gain, bias, b):
    rows = 2 * mem.shape[0]
    tokens, width = x.shape
    full = shaped(x.shape, F32)
    return pl.pallas_call(
        first_norm_kernel,
        grid=(1,),
        out_shape=(
            full,
            shaped_far(x.shape, F32),
            shaped_far((tokens, 1), F32),
            shaped(x.shape, BF16),
            shaped((rows, width), BF16),
            shaped((rows, width), BF16),
        ),
        in_specs=[VMEM] * 4 + [matrix(i, width) for i in range(3, 7)] + [VMEM] * 4,
        compiler_params=limit(16),
        cost_estimate=cost(3 * x.size * width, 8 << 20),
    )(ctx, x, mem, memo, w, w, w, w, ob, gain, bias, b)


def feed_kernel(
    info,
    ctx,
    first,
    cot,
    wo,
    wf,
    ob,
    gain2,
    bias2,
    fib,
    fob,
    gain3,
    bias3,
    out,
    keep,
    send,
    du3,
    dhid,
    normed,
    inverse,
    sums,
    hsum,
    act,
    slope,
    acc,
    second,
    db3,
    turn,
    *,
    halves,
):
    tokens, width = first.shape
    w = keep.shape[1]
    summed = first[...] + mm(ctx[...], wo[0], NT) + ob[...].astype(F32)
    n2, r2 = norm_forward(summed)
    normed[...] = n2
    inverse[...] = r2
    out2 = n2 * gain2[...].astype(F32) + bias2[...].astype(F32)
    second[...] = out2.astype(BF16)
    acc[...] = out2 + fob[...].astype(F32)

    @pl.loop(0, halves.nt, unroll=4)
    def _(t):
        cols = pl.ds(pl.multiple_of(t * w, w), w)
        hidden = mm(second[...], wf[0, :, cols], NN) + fib[:, cols]
        gate = 1.0 / (1.0 + jnp.exp(-hidden))
        active = (hidden * gate).astype(BF16)
        act[:, cols] = active
        slope[:, cols] = (gate * (1.0 + hidden * (1.0 - gate))).astype(BF16)
        acc[...] += mm(active, wf[1, :, cols], NT)

    n3, r3 = norm_forward(acc[...])
    out[...] = (n3 * gain3[...].astype(F32) + bias3[...].astype(F32)).astype(BF16)
    dy = cot[...].astype(F32)
    grad3 = norm_backward(dy, n3, r3, gain3[...].astype(F32))
    low3 = grad3.astype(BF16)
    sums[0:1, :] = column_sum(low3)
    sums[1:2, :] = column_sum(dy * n3)
    sums[2:3, :] = column_sum(dy)
    sums[3:8, :] = jnp.zeros((5, width), F32)
    du3[...] = grad3
    db3[...] = low3

    @pl.loop(0, halves.nt, unroll=4)
    def _(t):
        cols = pl.ds(pl.multiple_of(t * w, w), w)
        s = jnp.bitwise_xor(info[3], t)
        everything = slice(None)
        back = db3[...]
        dact = mm(back, wf[1, :, cols], NN)
        part = (dact * slope[:, cols].astype(F32)).astype(BF16)
        dhid[:, cols] = part
        hsum[:, cols] = column_sum(part)
        turn[0] = mm(second[...], part, TN).astype(BF16)
        disperse(info, halves, turn.at[0], 0, everything, s, keep, send)
        turn[1] = mm(back, act[:, cols], TN).astype(BF16)
        disperse(info, halves, turn.at[1], 1, everything, s, keep, send)


def feed_back_kernel(du3, dhid, normed, inverse, wf, gain, du2, db2, sums):
    dsecond = du3[...] + mm(dhid[...], wf[0], NT)
    n = normed[...]
    grad = norm_backward(dsecond, n, inverse[...], gain[...].astype(F32))
    low = grad.astype(BF16)
    du2[...] = grad
    db2[...] = low
    sums[0:1, :] = column_sum(low)
    sums[1:2, :] = column_sum(dsecond * n)
    sums[2:3, :] = column_sum(dsecond)
    sums[3:8, :] = jnp.zeros((5, du2.shape[1]), F32)


def feed_back(du3, dhid, normed, inverse, wf, gain):
    tokens, width = du3.shape
    wide = wf.shape[2]
    return pl.pallas_call(
        feed_back_kernel,
        grid=(1,),
        out_shape=(shaped(du3.shape, F32), shaped(du3.shape, BF16), shaped((8, width), F32)),
        in_specs=[VMEM] * 4 + [pl.BlockSpec((1, width, wide), lambda h: (0, 0, 0)), VMEM],
        compiler_params=limit(16),
        cost_estimate=cost(tokens * width * wide, 8 << 20),
    )(du3, dhid, normed, inverse, wf, gain)


def matrix(slot, width):
    return pl.BlockSpec((1, width, width), lambda h: (slot, 0, 0))


def feed(info, halves, ctx, first, cot, wo, wf, ob, gain2, bias2, fib, fob, gain3, bias3):
    tokens, width = first.shape
    wide = wf.shape[2]
    w = wide // halves.nt
    flat = shaped((halves.total, w), BF16)
    return pl.pallas_call(
        functools.partial(feed_kernel, halves=halves),
        grid=(1,),
        out_shape=(
            shaped(first.shape, BF16),
            flat,
            flat,
            shaped(first.shape, F32),
            shaped((tokens, wide), BF16),
            shaped(first.shape, F32),
            shaped((tokens, 1), F32),
            shaped((8, width), F32),
            shaped((1, wide), F32),
        ),
        in_specs=[SMEM] + [VMEM] * 3 + [matrix(7, width)] + [VMEM] * 8,
        scratch_shapes=[
            pltpu.VMEM((tokens, wide), BF16),
            pltpu.VMEM((tokens, wide), BF16),
            pltpu.VMEM((tokens, width), F32),
            pltpu.VMEM((tokens, width), BF16),
            pltpu.VMEM((tokens, width), BF16),
            pltpu.VMEM((2, width, w), BF16),
        ],
        compiler_params=limit(28),
        cost_estimate=cost(6 * tokens * width * wide, 14 << 20),
    )(info, ctx, first, cot, wo, wf, ob, gain2, bias2, fib, fob, gain3, bias3)


def middle_kernel(
    info,
    du2,
    dq2,
    dk2,
    dv2,
    db2,
    sums2,
    sums3,
    hsum,
    normed,
    inverse,
    first,
    mem,
    memo,
    ctx2,
    ctx1,
    wq,
    wk,
    wv,
    gain,
    *outs,
    halves,
):
    du1, db1, own, other = outs[:4]
    turn, riders = outs[-2:]
    rows, width = mem.shape
    dfirst = du2[...] + mm(dq2[...], wq[0], NT)
    n = normed[...]
    grad = norm_backward(dfirst, n, inverse[...], gain[...].astype(F32))
    low = grad.astype(BF16)
    du1[...] = grad
    db1[...] = low
    riders[0:1, :] = column_sum(low)
    riders[1:2, :] = column_sum(dfirst * n)
    riders[2:3, :] = column_sum(dfirst)
    riders[3:6, :] = sums2[0:3, :]
    riders[6:9, :] = sums3[0:3, :]
    riders[9:10, :] = column_sum(dq2[...])
    riders[10:11, :] = column_sum(dv2[...])
    for i in range(4):
        riders[11 + i : 12 + i, :] = hsum[:, i * width : (i + 1) * width]
    riders[15:16, :] = jnp.zeros((1, width), F32)
    turn[0] = mm(low, ctx1[...], TN).astype(BF16)
    turn[1] = mm(first[...].astype(BF16), dq2[...], TN).astype(BF16)
    for slot, part in ((2, dk2), (3, dv2)):
        turn[slot] = (
            mm(mem[...], part[:rows, :], TN) + mm(memo[...], part[rows:, :], TN)
        ).astype(BF16)
    turn[4] = mm(db2[...], ctx2[...], TN).astype(BF16)
    back = mm(dk2[...], wk[0], NT) + mm(dv2[...], wv[0], NT)
    own[...] = back[:rows, :]
    other[...] = back[rows:, :].astype(BF16)
    if halves is None:
        outs[4][...] = turn[...]
        outs[5][...] = riders[...]
        return
    for i in range(5):
        disperse_whole(info, halves, turn.at[i], i, outs[4], outs[5])
    w = outs[4].shape[1]
    for target in outs[4:6]:
        for q in range(width // w):
            lo = halves.main + 16 * q
            target[lo : lo + 16, :] = riders[:, q * w : q * w + w].astype(BF16)


def middle(info, near, normed, inverse, first, mem, memo, ctx2, ctx1, w, gain):
    tokens, width = first.shape
    rows = mem.shape[0]
    nd, nt = lax.axis_size("dp"), lax.axis_size("tensor")
    r, columns = width // nd, width // nt
    halves = Halves((3, 2), r, 16 * nt)
    direct = aligned(r, columns)
    if direct:
        last = (shaped((halves.total, columns), BF16),) * 2
    else:
        last = (shaped((5, width, width), BF16), shaped((16, width), F32))
    outs = pl.pallas_call(
        functools.partial(middle_kernel, halves=halves if direct else None),
        grid=(1,),
        out_shape=(
            shaped_far(first.shape, F32),
            shaped(first.shape, BF16),
            shaped((rows, width), F32),
            shaped((rows, width), BF16),
        )
        + last,
        in_specs=[SMEM] + [VMEM] * 15 + [matrix(i, width) for i in (4, 5, 6)] + [VMEM],
        scratch_shapes=[pltpu.VMEM((5, width, width), BF16), pltpu.VMEM((16, width), F32)],
        compiler_params=limit(20),
        cost_estimate=cost(6 * first.size * width, 12 << 20),
    )(
        info,
        *near,
        *far(normed, inverse, first, mem, memo, ctx2, ctx1, w, w, w),
        gain,
    )
    if not direct:
        rider = outs[5].astype(BF16).reshape(16, nt, columns).transpose(1, 0, 2)
        outs = outs[:4] + tuple(disperse_plain(info, halves, outs[4], rider.reshape(-1, columns)))
    return halves, outs


def self_grads_kernel(
    info, x, xo, dqa, dka, dva, dkoa, dvoa, dqb, dkb, dvb, dkob, dvob, wk, wv, *outs, halves
):
    other = outs[0]
    turn, sums = outs[-2:]
    width = x.shape[1]
    both = lambda left, right: jnp.concatenate([left[...], right[...]], axis=1)
    dq, dk, dv = both(dqa, dqb), both(dka, dkb), both(dva, dvb)
    turn[0] = mm(x[...], dq, TN).astype(BF16)
    sums[0:1, :] = column_sum(dq)

    @pl.when(info[0] == 0)
    def _():
        turn[1] = mm(x[...], dk, TN).astype(BF16)
        turn[2] = mm(x[...], dv, TN).astype(BF16)
        sums[1:2, :] = column_sum(dv)
        other[...] = jnp.zeros_like(other)

    @pl.when(info[0] != 0)
    def _():
        dko, dvo = both(dkoa, dkob), both(dvoa, dvob)
        turn[1] = (mm(x[...], dk, TN) + mm(xo[...], dko, TN)).astype(BF16)
        turn[2] = (mm(x[...], dv, TN) + mm(xo[...], dvo, TN)).astype(BF16)
        sums[1:2, :] = column_sum(dv) + column_sum(dvo)
        other[...] = (mm(dko, wk[0], NT) + mm(dvo, wv[0], NT)).astype(BF16)

    if halves is None:
        outs[1][...] = turn[...]
        outs[2][...] = sums[...]
        return
    for i in range(3):
        disperse_whole(info, halves, turn.at[i], i, outs[1], outs[2])
    w = outs[1].shape[1]
    row = lax.broadcasted_iota(jnp.int32, (16, w), 0)
    filled = jnp.zeros((16, w), F32)
    for i in range(2):
        for t in range(width // w):
            piece = sums[i : i + 1, t * w : t * w + w]
            filled = jnp.where(row == i * (width // w) + t, piece, filled)
    for target in outs[1:3]:
        target[halves.main :, :] = filled.astype(BF16)


def self_grads(info, x, xo, early, late, w):
    width = x.shape[1]
    nd, nt = lax.axis_size("dp"), lax.axis_size("tensor")
    r, columns = width // nd, width // nt
    halves = Halves((3,), r, 16)
    direct = aligned(r, columns)
    if direct:
        last = (shaped((halves.total, columns), BF16),) * 2
    else:
        last = (shaped((3, width, width), BF16), shaped((8, width), F32))
    outs = pl.pallas_call(
        functools.partial(self_grads_kernel, halves=halves if direct else None),
        grid=(1,),
        out_shape=(shaped(x.shape, BF16),) + last,
        in_specs=[SMEM] + [VMEM] * 12 + [matrix(i, width) for i in (1, 2)],
        scratch_shapes=[pltpu.VMEM((3, width, width), BF16), pltpu.VMEM((8, width), F32)],
        compiler_params=limit(16),
        cost_estimate=cost(7 * x.size * width, 8 << 20),
    )(info, *far(x, xo), *early, *late, *far(w, w))
    if not direct:
        rider = outs[2][:2].astype(BF16).reshape(-1, columns)
        rider = jnp.pad(rider, ((0, 16 - rider.shape[0]), (0, 0)))
        outs = outs[:1] + tuple(disperse_plain(info, halves, outs[1], rider))
    return halves, outs


def input_grads_kernel(du1, dqa, dka, dva, dqb, dkb, dvb, wq, wk, wv, back, out):
    both = lambda left, right: jnp.concatenate([left[...], right[...]], axis=1)
    out[...] = (
        du1[...]
        + mm(both(dqa, dqb), wq[0], NT)
        + mm(both(dka, dkb), wk[0], NT)
        + mm(both(dva, dvb), wv[0], NT)
        + back[...].astype(F32)
    )


def input_grads(du1, early, late, w, back):
    return pl.pallas_call(
        input_grads_kernel,
        grid=(1,),
        out_shape=shaped(du1.shape, F32),
        in_specs=[VMEM] * 7 + [matrix(i, du1.shape[1]) for i in range(3)] + [VMEM],
        compiler_params=limit(16),
        cost_estimate=cost(3 * du1.size * du1.shape[1], 6 << 20),
    )(*far(du1), *early, *late, *far(w, w, w), back)


def on_device(
    inputs,
    memory,
    prefix,
    self_query,
    self_query_bias,
    self_key,
    self_value,
    self_value_bias,
    self_out,
    self_out_bias,
    self_norm_gain,
    self_norm_bias,
    cross_query,
    cross_query_bias,
    cross_key,
    cross_value,
    cross_value_bias,
    cross_out,
    cross_out_bias,
    cross_norm_gain,
    cross_norm_bias,
    feed_in,
    feed_in_bias,
    feed_out,
    feed_out_bias,
    feed_norm_gain,
    feed_norm_bias,
    cotangent,
):
    nd, nt = lax.axis_size("dp"), lax.axis_size("tensor")
    me_d, me_t = lax.axis_index("dp"), lax.axis_index("tensor")
    late = me_t % 2
    width = inputs.shape[1]
    assert LEN == 2 * inputs.shape[0] and MEM == 2 * memory.shape[0]
    assert nd & (nd - 1) == 0 and nt & (nt - 1) == 0
    prefix_here = jnp.where(late == 0, lax.dynamic_index_in_dim(prefix, me_t // 2, keepdims=False), 0)
    info = jnp.stack([late, prefix_here, me_d, me_t]).astype(jnp.int32)

    columns = self_query_bias.shape[0]
    row = lambda vector: vector.reshape(1, -1)
    packed = pack(
        (
            self_query,
            self_key,
            self_value,
            self_out.T,
            cross_query,
            cross_key,
            cross_value,
            cross_out.T,
        ),
        (self_query_bias, self_value_bias, cross_query_bias, cross_value_bias, feed_in_bias),
    )
    feed_shard = jnp.stack([feed_in, feed_out.T])

    bits = [1 << i for i in range(nt.bit_length() - 1)]
    swapped = [swap(packed, 0, k) for k in range(1, nt)]
    parts = [packed] + swapped
    size = 4 * self_query.shape[0]
    shape = (1, nt, 4) + self_query.shape
    lines = [
        jnp.stack([part[g * size : g * size + size] for part in parts]).reshape(shape)
        for g in range(2)
    ]
    riders = jnp.stack([part[2 * size :] for part in parts])
    rounds = len(plane_bits(0))
    line_feed = doubled(after(feed_shard, lines[0])[None], bits[:1])
    held = [([0], line) for line in lines]
    for index in range(rounds):
        more = [grown(*held[g], plane_bits(g)[index]) for g in range(2)]
        if index < rounds - 1:
            held = [merged([held[g], more[g]]) for g in range(2)]
    inputs_other = hand_over(after(inputs, lines[0]), 0, 1)
    line_feed = doubled(line_feed, bits[1:])
    head_biases, hidden_bias = spread(info, riders)
    more[0] = more[0][0], after(more[0][1], inputs_other, line_feed, head_biases)
    arrays, entries = [], []
    for g in range(2):
        for slots, pieces in (held[g], more[g]):
            arrays += [pieces, swap(pieces, 1, 0)]
            entries += [(0, tuple(slots), 4 * g), (1, tuple(slots), 4 * g)]
    weights = assemble(info, arrays, entries)

    line_feed = after(line_feed, more[0][1], more[1][1])
    memory_other = swap(after(memory, line_feed), 0, 1)
    held = [([0], line_feed[None, :, g : g + 1]) for g in range(2)]
    q1, k1, v1, k1o, v1o = project_self(info, inputs, inputs_other, weights, head_biases)
    for index in range(rounds):
        more = [grown(*held[g], plane_bits(g)[index]) for g in range(2)]
        if index < rounds - 1:
            held = [(slots, after(pieces, q1)) for slots, pieces in held]
            held = [merged([held[g], more[g]]) for g in range(2)]
    q1 = after(q1, held[0][1], held[1][1])
    ctx1, log1 = self_forward(info, q1, k1, v1, k1o, v1o)
    first, normed1, inverse1, q2, k2, v2 = first_norm(
        ctx1,
        inputs,
        memory,
        memory_other,
        weights,
        row(self_out_bias),
        row(self_norm_gain),
        row(self_norm_bias),
        head_biases,
    )
    ctx2, log2 = cross_forward(q2, k2, v2)
    more[0] = more[0][0], after(more[0][1], ctx2)
    more[1] = more[1][0], after(more[1][1], ctx2)
    arrays, entries = [], []
    for g in range(2):
        for slots, pieces in (held[g], more[g]):
            arrays += [pieces, swap(pieces, 1, 0)]
            entries += [(0, tuple(slots), g), (1, tuple(slots), g)]
    w_feed = assemble(info, arrays, entries)
    feed_halves = Halves((1, 1), width // nd, 0)
    outputs, keep, send, du3, dhidden, normed2, inverse2, sums_feed, sums_hidden = feed(
        info,
        feed_halves,
        ctx2,
        first,
        cotangent,
        weights,
        w_feed,
        row(cross_out_bias),
        row(cross_norm_gain),
        row(cross_norm_bias),
        hidden_bias,
        row(feed_out_bias),
        row(feed_norm_gain),
        row(feed_norm_bias),
    )
    rounds = feed_halves.rounds
    got = swap(send, 1, 0)
    du2, db2, sums_second = feed_back(
        du3, dhidden, normed2, inverse2, w_feed, row(cross_norm_gain)
    )
    whole = [[(0, base), (1, base)] for base in feed_halves.bases]
    arrays, held, _ = halve(feed_halves, [after(keep, db2), got], whole, None, 0)
    db2 = after(db2, arrays[0])
    dq2, dk2, dv2 = cross_backward(q2, k2, v2, ctx2, log2, db2, weights)
    middle_halves, (du1, db1, memory_own, memory_back, keep, send) = middle(
        info,
        (du2, dq2, dk2, dv2, db2, sums_second, sums_feed, sums_hidden),
        normed1,
        inverse1,
        first,
        memory,
        memory_other,
        ctx2,
        ctx1,
        weights,
        row(self_norm_gain),
    )
    arrays[0] = after(arrays[0], db1)
    for index in range(1, rounds):
        arrays, held, _ = halve(feed_halves, arrays, held, None, index)
    got = swap(after(send, arrays[0]), 1, 0)
    db1 = after(db1, arrays[0])
    pairs = width // PAIR // 2
    operands = (info, q1, k1, v1, k1o, v1o, ctx1, log1)
    grads_early = self_backward(*operands, db1, weights, 0, pairs)
    arrays[0] = after(arrays[0], grads_early[0])
    block = feed_in.shape[0]
    feed_segments = list(zip(feed_halves.sizes, held))
    feed_arrays = arrays
    for bit in reversed(bits[1:]):
        feed_arrays, feed_segments, _ = line_round(feed_arrays, feed_segments, None, bit)
    whole = [[(0, base), (1, base)] for base in middle_halves.bases]
    rider = [(0, middle_halves.main), (1, middle_halves.main)]
    keep = after(keep, feed_arrays[0])
    arrays, held, rider = halve(middle_halves, [keep, got], whole, rider, 0)
    db1 = after(db1, arrays[0])
    grads_late = list(self_backward(*operands, db1, weights, pairs, pairs))
    arrays[0] = after(arrays[0], grads_late[0])
    for index in range(1, rounds):
        arrays, held, rider = halve(middle_halves, arrays, held, rider, index)
    grads_late[0] = after(grads_late[0], arrays[0])
    self_halves, (inputs_back, keep, send) = self_grads(
        info, inputs, inputs_other, grads_early, grads_late, weights
    )
    send = after(send, *arrays, *feed_arrays)
    got = swap(send, 1, 0)
    inputs_got = hand_over(after(inputs_back, send), 1, -1)
    arrays[0] = after(arrays[0], send)
    segments = list(zip(middle_halves.sizes, held))
    rider = (middle_halves.rider, rider)
    for bit in reversed(bits[1:]):
        arrays, segments, rider = line_round(arrays, segments, rider, bit)
    keep = after(keep, arrays[0])

    size = self_halves.sizes[0]
    end = (self_halves.rider, [(0, self_halves.main), (1, self_halves.main)])
    places = [self_halves.place(0, j)[0] for j in range(nd // 2)]
    parts = add_rows([keep, got], [[(size, [(0, lo), (1, lo)]), end] for lo in places])
    planes = [parts[0]] + [swap(part, 2 * j, 0) for j, part in enumerate(parts) if j]
    arrays[0] = after(arrays[0], *planes, inputs_got)
    arrays, segments, rider = line_round(arrays, segments, rider, 1)
    planes[0] = after(planes[0], arrays[0])
    at = range(len(planes))
    rows = 3 * block
    end = (self_halves.rider, [(p, size) for p in at])
    lines = add_rows(planes, [[(rows, [(p, k * rows) for p in at]), end] for k in range(nt)])
    lines = line_swaps(lines)
    riding = memory_back.shape[1] == feed_arrays[0].shape[1]
    feed_arrays[0] = after(feed_arrays[0], lines[0])
    feed_arrays, feed_segments, _ = line_round(
        feed_arrays, feed_segments, None, 1, memory_back if riding else None
    )

    grad_feed_in, grad_feed_out = add_rows(
        feed_arrays[:2], [[(block, terms)] for _, terms in feed_segments], F32
    )
    if riding:
        memory_got = feed_arrays[1][2 * block :]
    else:
        memory_got = swap(after(memory_back, lines[0]), 0, 1)
    grad_memory = memory_own + memory_got.astype(F32)
    du1 = after(du1, arrays[0], lines[0], feed_arrays[0])
    grad_inputs = input_grads(du1, grads_early[:3], grads_late[:3], weights, inputs_got)
    lines[0] = after(lines[0], grad_inputs, grad_feed_in, grad_memory)
    plans = [
        [(block, [(array, lo + i * block) for array, lo in terms])]
        for count, (_, terms) in zip(middle_halves.groups, segments)
        for i in range(count)
    ]
    cuts = [(i * block, block) for i in range(3)] + [(rows, self_halves.rider)]
    cuts = [[(n, [(3 + k, lo) for k in range(nt)])] for lo, n in cuts]
    plans = plans + cuts[:3] + [[rider], cuts[3]]
    sums = finish(info, arrays + lines, plans, nt, width)
    grad_middle, grad_self = sums[:5], sums[5:8]
    early, mine, hidden_mine = sums[8:]

    return (
        outputs,
        grad_inputs,
        grad_memory,
        grad_self[0],
        mine[2],
        grad_self[1],
        grad_self[2],
        mine[3],
        grad_middle[0].T,
        early[0],
        early[1],
        early[2],
        grad_middle[1],
        mine[0],
        grad_middle[2],
        grad_middle[3],
        mine[1],
        grad_middle[4].T,
        early[3],
        early[4],
        early[5],
        grad_feed_in,
        hidden_mine[0],
        grad_feed_out.T,
        early[6],
        early[7],
        early[8],
    )


def solution(mesh):
    placed = (
        P(("dp", "tensor"), None),
        P(("dp", "tensor"), None),
        P("dp"),
        P("dp", "tensor"),
        P("tensor"),
        P("dp", "tensor"),
        P("dp", "tensor"),
        P("tensor"),
        P("tensor", "dp"),
        P(),
        P(),
        P(),
        P("dp", "tensor"),
        P("tensor"),
        P("dp", "tensor"),
        P("dp", "tensor"),
        P("tensor"),
        P("tensor", "dp"),
        P(),
        P(),
        P(),
        P("dp", "tensor"),
        P("tensor"),
        P("tensor", "dp"),
        P(),
        P(),
        P(),
        P(("dp", "tensor"), None),
    )
    return jax.shard_map(
        on_device,
        mesh=mesh,
        in_specs=placed,
        out_specs=(
            P(("dp", "tensor"), None),
            P(("dp", "tensor"), None),
            P(("dp", "tensor"), None),
            P("dp", "tensor"),
            P("tensor"),
            P("dp", "tensor"),
            P("dp", "tensor"),
            P("tensor"),
            P("tensor", "dp"),
            P(),
            P(),
            P(),
            P("dp", "tensor"),
            P("tensor"),
            P("dp", "tensor"),
            P("dp", "tensor"),
            P("tensor"),
            P("tensor", "dp"),
            P(),
            P(),
            P(),
            P("dp", "tensor"),
            P("tensor"),
            P("tensor", "dp"),
            P(),
            P(),
            P(),
        ),
        check_vma=False,
    )
```
